32 devices in a mesh: dp: 4 (over x, core), expert: 8 (over z, y).
Axes of the slice: x: 2, y: 2, z: 4, core: 2. Of those that a mesh axis runs over, the one named last changes fastest.
Arguments:
- tokens: bfloat16 [1536, 2048], P(('dp', 'expert')), may hold values from -6 to 6
- expert_ids: int32 [1536, 8], P(('dp', 'expert')), may hold values from 0 to 7, all different within a row; in each aligned block of 48 rows (0 to 47, 48 to 95, ...) at most 48 rows name the same one
- gate_probs: float32 [1536, 8], P(('dp', 'expert')), may hold values from 0.05 to 0.5
- out_cot: bfloat16 [1536, 2048], P(('dp', 'expert')), may hold values from -1.5 to 1.5
- w_gate: bfloat16 [8, 2048, 768], P('expert'), may hold values from -0.125 to 0.125
- w_up: bfloat16 [8, 2048, 768], P('expert'), may hold values from -0.125 to 0.125
- w_down: bfloat16 [8, 768, 2048], P('expert'), may hold values from -0.21875 to 0.21875
Outputs:
- layer_out: bfloat16 [1536, 2048], P(('dp', 'expert'))
- input_grad: bfloat16 [1536, 2048], P(('dp', 'expert'))
- gate_wgrad: float32 [8, 2048, 768], P('expert', 'dp')
- up_wgrad: float32 [8, 2048, 768], P('expert', 'dp')
- down_wgrad: float32 [8, 768, 2048], P('expert', 'dp')
The draws below stay inside these ranges and needn't reach their ends.
Inputs may be any that keep to these rules, and one draw needn't show every extreme that they name: `expert_ids`: each token names 8 different experts. Among the 48 tokens of one device, at most 48 name the same expert, and in every draw some expert is named by exactly 48 tokens of some device.
All inputs are finite; a program needn't handle non-finite values.
Results may differ from the reference program's by a relative error of at most 0.012.
Values may be sent and summed in bfloat16 or wider, within the bound.
No kernel may reach another device: no remote copies, remote signals or barrier semaphores. Data moves between devices by JAX's collectives and lax.ppermute only.
A program may use at most 128 MiB of HBM per device.

```python
import math
import jax
import jax.numpy as jnp
import numpy as np
from jax import lax

D = 2048
FF = 768
TOP = 8
TOK_DEV = 48
EXPERTS = 8
CAP = 48
TOKENS = 1536
N_DP = 4
N_EXPERT = 8


def block_scale(own_key, extent, cuts, smallest, high):
    def one(axis_at, parts):
        steps = jax.random.uniform(jax.random.fold_in(jax.random.fold_in(own_key, 6), axis_at), (parts,), jnp.float32, smallest / len(cuts), high / len(cuts))
        return jnp.repeat(jnp.exp(steps), extent[axis_at] // parts).reshape((-1,) + (1,) * (len(extent) - axis_at - 1))

    level = one(*cuts[0])
    for cut in cuts[1:]:
        level = level * one(*cut)
    return level


def assign_block(stream_key, own, number, rows, amount, top, bound, lean):
    ranking = jax.random.permutation(stream_key, amount)
    packed, ordinary = load_shares(amount, rows * top, bound, lean, True), load_shares(amount, rows * top, bound, lean, False)
    places = jnp.arange(amount)

    def named(lengths, rotation):
        used = int((lengths > 0).sum())
        fixed = max(1, used // 4)
        moved = fixed + (places - fixed + rotation * (used - fixed)) % max(1, amount - fixed)
        return jnp.zeros((amount,), jnp.int32).at[ranking[jnp.where(places < fixed, places, moved)]].set(jnp.asarray(lengths, jnp.int32))

    lengths = jnp.where(number % 4 == 0, named(packed, number // 4), named(ordinary, number - number // 4 - 1))
    mixed = jax.random.permutation(jax.random.fold_in(own, 3), amount)
    source_of, taker = mixed[0:amount // 2 * 2:2], mixed[1:amount // 2 * 2:2]
    slack = jnp.minimum(lengths[source_of] - 1, bound - lengths[taker]) // 2
    slack = jnp.where((source_of == ranking[0]) | (taker == ranking[0]) | (lengths[taker] == 0), 0, jnp.maximum(slack, 0))
    moved = jax.random.randint(jax.random.fold_in(own, 4), (amount // 2,), 0, 1 << 20) % (slack + 1)
    lengths = lengths.at[source_of].add(-moved).at[taker].add(moved)
    labels = jnp.searchsorted(jnp.cumsum(lengths), jnp.arange(rows * top), side="right").astype(jnp.int32)
    grid = labels.reshape(top, rows).T
    grid = grid[jax.random.permutation(jax.random.fold_in(own, 1), rows)]
    rotation = jax.random.randint(jax.random.fold_in(own, 2), (rows, 1), 0, top)
    return jnp.take_along_axis(grid, (jnp.arange(top)[None, :] + rotation) % top, axis=1)


def load_shares(amount, total, bound, lean, full):
    weights = [(1 << 20) // math.isqrt(rank ** lean) + 1 for rank in range(1, amount + 1)]
    largest = bound if full else min(bound, max(-(-total // amount), total * weights[0] // sum(weights)))
    least = 1 if total - largest >= amount - 1 else 0
    given, rest = [largest] + [least] * (amount - 1), total - largest - least * (amount - 1)
    while rest > 0:
        free = [i for i in range(1, amount) if given[i] < largest] or [i for i in range(1, amount) if given[i] < bound]
        pool, remaining = sum([weights[i] for i in free]), rest
        for i in free:
            extra = min(bound - given[i], max(1, remaining * weights[i] // pool), rest)
            given[i] = given[i] + extra
            rest = rest - extra
    return np.array(given)


def noise(key, dims, deviation, bound, pieces=(), kind=jnp.bfloat16):
    loudness = block_scale(key, dims, pieces, -0.22, 0.18) if pieces else 1.0
    drawn = jax.random.normal(key, dims, jnp.float32) * deviation * loudness
    return jnp.minimum(jnp.maximum(drawn, -bound), bound).astype(kind)


def setup_inputs(seed: int = 0) -> dict:
    keys = jax.random.split(jax.random.key(seed), 8)
    tokens = noise(keys[0], (TOKENS, D), 1.0, 6.0, ((0, 32),))
    expert_ids_keys = jax.random.split(jax.random.fold_in(keys[1], 1), TOKENS // TOK_DEV)
    expert_ids_turns = jax.random.permutation(jax.random.fold_in(keys[1], 3), TOKENS // TOK_DEV)
    expert_ids = jax.vmap(lambda own, number: assign_block(jax.random.fold_in(keys[1], 2), own, number, TOK_DEV, EXPERTS, TOP, CAP, 2))(expert_ids_keys, expert_ids_turns).reshape((TOKENS, TOP))
    gate_probs = jnp.clip(jnp.exp(math.log(0.5) - 2.3025851 * jax.random.uniform(keys[2], (TOKENS, TOP), jnp.float32) ** block_scale(keys[2], (TOKENS, TOP), ((0, 32),), -0.2, 0.2)), 0.05, 0.5)
    out_cot = noise(keys[3], (TOKENS, D), 0.25, 1.5, ((0, 32),))
    w_gate = noise(keys[4], (EXPERTS, D, FF), D ** -0.5, 0.125, ((0, 8),))
    w_up = noise(keys[5], (EXPERTS, D, FF), D ** -0.5, 0.125, ((0, 8),))
    w_down = noise(keys[6], (EXPERTS, FF, D), FF ** -0.5, 0.21875, ((0, 8),))
    return {"tokens": tokens, "expert_ids": expert_ids, "gate_probs": gate_probs, "out_cot": out_cot, "w_gate": w_gate, "w_up": w_up, "w_down": w_down}


def reference(tokens, expert_ids, gate_probs, out_cot, w_gate, w_up, w_down):
    group_tokens = TOK_DEV * N_EXPERT
    window = N_EXPERT * CAP

    def one_group(wgrads, group):
        begin = (group * group_tokens).astype(jnp.int32)
        own_tokens = lax.dynamic_slice_in_dim(tokens, begin, group_tokens, 0)
        own_cot = lax.dynamic_slice_in_dim(out_cot, begin, group_tokens, 0)
        flat_ids = lax.dynamic_slice_in_dim(expert_ids, begin, group_tokens, 0).reshape(-1).astype(jnp.int32)
        flat_probs = lax.dynamic_slice_in_dim(gate_probs, begin, group_tokens, 0).reshape(-1)
        order = jnp.argsort(flat_ids, stable=True).astype(jnp.int32)
        totals = jnp.sum((flat_ids[:, None] == jnp.arange(EXPERTS, dtype=jnp.int32)[None, :]).astype(jnp.int32), axis=0)
        starts = (jnp.cumsum(totals) - totals).astype(jnp.int32)
        padded = jnp.concatenate([order, jnp.zeros((window,), jnp.int32)])

        def one_expert(carry, expert):
            out_total, grad_total = carry
            index = lax.dynamic_slice(padded, (starts[expert],), (window,))
            live = jnp.arange(window, dtype=jnp.int32) < totals[expert]
            owner = (index // TOP).astype(jnp.int32)
            probs = jnp.where(live, flat_probs[index], 0.0)
            rows = jnp.where(live[:, None], own_tokens[owner], 0).astype(tokens.dtype)
            gate_mat = w_gate[expert]
            up_mat = w_up[expert]
            down_mat = w_down[expert]
            gate_pre = jnp.dot(rows, gate_mat, preferred_element_type=jnp.float32)
            up_pre = jnp.dot(rows, up_mat, preferred_element_type=jnp.float32)
            sigma = jax.nn.sigmoid(gate_pre)
            hidden = (gate_pre * sigma * up_pre).astype(jnp.bfloat16)
            expert_out = jnp.dot(hidden, down_mat, preferred_element_type=jnp.float32).astype(jnp.bfloat16)
            out_total = out_total.at[owner].add(probs[:, None] * expert_out.astype(jnp.float32))
            out_grad = (probs[:, None] * own_cot[owner].astype(jnp.float32)).astype(jnp.bfloat16)
            hidden_grad = jnp.dot(out_grad, down_mat.T, preferred_element_type=jnp.float32)
            gate_grad = (hidden_grad * up_pre * sigma * (1.0 + gate_pre * (1.0 - sigma))).astype(jnp.bfloat16)
            up_grad = (hidden_grad * gate_pre * sigma).astype(jnp.bfloat16)
            row_grad = (jnp.dot(gate_grad, gate_mat.T, preferred_element_type=jnp.float32)
                        + jnp.dot(up_grad, up_mat.T, preferred_element_type=jnp.float32)).astype(jnp.bfloat16)
            grad_total = grad_total.at[owner].add(row_grad.astype(jnp.float32))
            gate_w = jnp.dot(rows.T, gate_grad, preferred_element_type=jnp.float32).astype(jnp.bfloat16)
            up_w = jnp.dot(rows.T, up_grad, preferred_element_type=jnp.float32).astype(jnp.bfloat16)
            down_w = jnp.dot(hidden.T, out_grad, preferred_element_type=jnp.float32).astype(jnp.bfloat16)
            return (out_total, grad_total), (gate_w, up_w, down_w)

        start = (jnp.zeros((group_tokens, D), jnp.float32), jnp.zeros((group_tokens, D), jnp.float32))
        (out_total, grad_total), (gate_w, up_w, down_w) = lax.scan(
            one_expert, start, jnp.arange(EXPERTS, dtype=jnp.int32))
        gate_sum, up_sum, down_sum = wgrads
        wgrads = (gate_sum + gate_w.astype(jnp.float32), up_sum + up_w.astype(jnp.float32),
                  down_sum + down_w.astype(jnp.float32))
        return wgrads, (out_total.astype(jnp.bfloat16), grad_total.astype(jnp.bfloat16))

    zeros = (jnp.zeros((EXPERTS, D, FF), jnp.float32), jnp.zeros((EXPERTS, D, FF), jnp.float32),
             jnp.zeros((EXPERTS, FF, D), jnp.float32))
    (gate_wgrad, up_wgrad, down_wgrad), (outs, grads) = lax.scan(
        one_group, zeros, jnp.arange(N_DP, dtype=jnp.int32))
    return (outs.reshape(TOKENS, D), grads.reshape(TOKENS, D), gate_wgrad, up_wgrad, down_wgrad)
```

```python
import jax
import jax.numpy as jnp
from jax import lax
from jax.sharding import PartitionSpec as P


def contract_rows(left, right):
    return lax.dot_general(
        left, right, (((0,), (0,)), ((), ())), preferred_element_type=jnp.float32
    )


def contract_cols(left, right):
    return lax.dot_general(
        left, right, (((1,), (1,)), ((), ())), preferred_element_type=jnp.float32
    )


def routed(tokens, expert_ids, gate_probs, out_cot, w_gate, w_up, w_down):
    tok_count, width = tokens.shape
    top = expert_ids.shape[1]
    experts = lax.axis_size("expert")
    slots = min(tok_count, 4 * tok_count * top // (3 * experts))
    flat_ids = expert_ids.reshape(-1)
    onehot = (flat_ids[:, None] == jnp.arange(experts, dtype=jnp.int32)[None, :]).astype(jnp.int32)
    ranks = jnp.sum(jnp.cumsum(onehot, axis=0) * onehot, axis=1) - 1
    target = flat_ids * slots + ranks
    token_rows = jnp.repeat(tokens, top, axis=0)
    outbound = jnp.zeros((experts * slots, width), tokens.dtype).at[target].set(token_rows)
    outbound = outbound.reshape(experts, slots, width)
    gate_mat = w_gate[0]
    up_mat = w_up[0]
    down_mat = w_down[0]
    hidden_width = gate_mat.shape[1]
    arrived = lax.all_to_all(outbound, "expert", split_axis=0, concat_axis=0, tiled=True)
    sources = arrived.shape[0]
    count = arrived.shape[1]
    rows = arrived.reshape(-1, width)
    gate_pre = jnp.dot(rows, gate_mat, preferred_element_type=jnp.float32)
    up_pre = jnp.dot(rows, up_mat, preferred_element_type=jnp.float32)
    hidden = (gate_pre * jax.nn.sigmoid(gate_pre) * up_pre).astype(jnp.bfloat16)
    result = jnp.dot(hidden, down_mat, preferred_element_type=jnp.float32).astype(jnp.bfloat16)
    expert_out, hidden, gate_pre, up_pre, arrived = (
        result.reshape(sources, count, width),
        hidden.reshape(sources, count, hidden_width),
        gate_pre.reshape(sources, count, hidden_width),
        up_pre.reshape(sources, count, hidden_width),
        arrived,
    )
    returned = lax.all_to_all(expert_out, "expert", split_axis=0, concat_axis=0, tiled=True)
    picked = returned.reshape(-1, width)[target].reshape(tok_count, top, width)
    layer_out = jnp.sum(gate_probs[:, :, None] * picked.astype(jnp.float32), axis=1).astype(
        jnp.bfloat16
    )
    out_grad = (gate_probs[:, :, None] * out_cot[:, None, :].astype(jnp.float32)).astype(
        jnp.bfloat16
    )
    outbound_grad = (
        jnp.zeros((experts * slots, width), tokens.dtype)
        .at[target]
        .set(out_grad.reshape(-1, width))
    )
    arrived_grad = lax.all_to_all(
        outbound_grad.reshape(experts, slots, width),
        "expert",
        split_axis=0,
        concat_axis=0,
        tiled=True,
    ).reshape(-1, width)
    x_rows = arrived.reshape(-1, width)
    hidden_rows = hidden.reshape(-1, hidden_width)
    gate_rows = gate_pre.reshape(-1, hidden_width)
    up_rows = up_pre.reshape(-1, hidden_width)
    hidden_grad = contract_cols(arrived_grad, down_mat)
    sigma = jax.nn.sigmoid(gate_rows)
    gate_grad = (hidden_grad * up_rows * sigma * (1.0 + gate_rows * (1.0 - sigma))).astype(
        jnp.bfloat16
    )
    up_grad = (hidden_grad * gate_rows * sigma).astype(jnp.bfloat16)
    row_grad = (contract_cols(gate_grad, gate_mat) + contract_cols(up_grad, up_mat)).astype(
        jnp.bfloat16
    )
    back_grad = lax.all_to_all(
        row_grad.reshape(experts, slots, width), "expert", split_axis=0, concat_axis=0, tiled=True
    )
    gathered = back_grad.reshape(-1, width)[target].reshape(tok_count, top, width)
    input_grad = jnp.sum(gathered.astype(jnp.float32), axis=1).astype(jnp.bfloat16)
    down_grad = lax.psum_scatter(
        contract_rows(hidden_rows, arrived_grad).astype(jnp.bfloat16),
        "dp",
        scatter_dimension=0,
        tiled=True,
    ).astype(jnp.float32)
    gate_part = lax.psum_scatter(
        contract_rows(x_rows, gate_grad).astype(jnp.bfloat16), "dp", scatter_dimension=0, tiled=True
    ).astype(jnp.float32)
    up_part = lax.psum_scatter(
        contract_rows(x_rows, up_grad).astype(jnp.bfloat16), "dp", scatter_dimension=0, tiled=True
    ).astype(jnp.float32)
    return (layer_out, input_grad, gate_part[None], up_part[None], down_grad[None])


def swap(value, axis, mask):
    size = lax.axis_size(axis)
    return lax.ppermute(value, axis, [(i, i ^ mask) for i in range(size)])


def dense(tokens, expert_ids, gate_probs, out_cot, w_gate, w_up, w_down):
    count, width = tokens.shape
    experts = lax.axis_size("expert")
    owners = lax.axis_size("dp")
    me = lax.axis_index("expert")
    mine = lax.axis_index("dp")
    evens = range(2, experts, 2)

    named = expert_ids[:, :, None] == jnp.arange(experts, dtype=jnp.int32)[None, None, :]
    probs = jnp.sum(jnp.where(named, gate_probs[:, :, None], 0.0), axis=1)
    high = lax.reduce_precision(probs, 8, 7)
    low = probs - high
    lanes = 128 * (-(-2 * experts // 128))
    extra = jnp.concatenate(
        [high, low, jnp.zeros((count, lanes - 2 * experts), jnp.float32)], axis=1
    ).astype(jnp.bfloat16)
    payload = jnp.concatenate([tokens, extra], axis=1)

    def gather(own):
        even = [own] + [swap(own, "expert", m) for m in evens]
        odd = [swap(block, "expert", 1) for block in even]
        return jnp.concatenate(even + odd, axis=0)

    rows_ext = gather(payload)
    cot_rows = gather(out_cot)
    rows = rows_ext[:, :width]
    column = lax.broadcasted_iota(jnp.int32, (1, lanes), 1)
    chosen = (column == me) | (column == me + experts)
    row_probs = jnp.sum(
        jnp.where(chosen, rows_ext[:, width:].astype(jnp.float32), 0.0), axis=1, keepdims=True
    )

    gate_mat, up_mat, down_mat = w_gate[0], w_up[0], w_down[0]
    gate_pre = jnp.dot(rows, gate_mat, preferred_element_type=jnp.float32)
    up_pre = jnp.dot(rows, up_mat, preferred_element_type=jnp.float32)
    sigma = jax.nn.sigmoid(gate_pre)
    hidden = (gate_pre * sigma * up_pre).astype(jnp.bfloat16)
    expert_out = row_probs * jnp.dot(hidden, down_mat, preferred_element_type=jnp.float32)
    expert_out = expert_out.astype(jnp.bfloat16)
    out_grad = (row_probs * cot_rows.astype(jnp.float32)).astype(jnp.bfloat16)
    hidden_grad = contract_cols(out_grad, down_mat)
    gate_grad = (hidden_grad * up_pre * sigma * (1.0 + gate_pre * (1.0 - sigma))).astype(
        jnp.bfloat16
    )
    up_grad = (hidden_grad * gate_pre * sigma).astype(jnp.bfloat16)
    row_grad = (contract_cols(gate_grad, gate_mat) + contract_cols(up_grad, up_mat)).astype(
        jnp.bfloat16
    )

    def give_back(values):
        half = values.shape[0] // 2
        held = values[:half].astype(jnp.float32) + swap(values[half:], "expert", 1).astype(
            jnp.float32
        )
        parts = held.astype(jnp.bfloat16).reshape(experts // 2, count, width)
        total = held[:count]
        for m in evens:
            total = total + swap(parts[m // 2], "expert", m).astype(jnp.float32)
        return total.astype(jnp.bfloat16)

    def reduced(left, right):
        size = left.shape[1] // owners

        def part(m):
            columns = lax.dynamic_slice_in_dim(left, (mine ^ m) * size, size, 1)
            return contract_rows(columns, right)

        total = None
        for m in range(owners - 2, -1, -2):
            own = part(m) + swap(part(m + 1).astype(jnp.bfloat16), "dp", 1).astype(jnp.float32)
            if m:
                own = swap(own.astype(jnp.bfloat16), "dp", m).astype(jnp.float32)
            total = own if total is None else total + own
        return total[None]

    down_grad = reduced(hidden, out_grad)
    gate_part = reduced(rows, gate_grad)
    up_part = reduced(rows, up_grad)
    layer_out = give_back(expert_out)
    input_grad = give_back(row_grad)
    return (layer_out, input_grad, gate_part, up_part, down_grad)


def shards(tokens, expert_ids, *rest):
    every = expert_ids.shape[1] == lax.axis_size("expert")
    return (dense if every else routed)(tokens, expert_ids, *rest)


def solution(mesh):
    placed = (
        P(("dp", "expert"), None),
        P(("dp", "expert"), None),
        P(("dp", "expert"), None),
        P(("dp", "expert"), None),
        P("expert", None, None),
        P("expert", None, None),
        P("expert", None, None),
    )
    return jax.shard_map(
        shards,
        mesh=mesh,
        in_specs=placed,
        out_specs=(
            P(("dp", "expert"), None),
            P(("dp", "expert"), None),
            P("expert", "dp", None),
            P("expert", "dp", None),
            P("expert", "dp", None),
        ),
        check_vma=False,
    )
```

```python
import jax
import jax.numpy as jnp
from jax import lax
from jax.experimental import pallas as pl
from jax.experimental.pallas import tpu as pltpu
from jax.sharding import PartitionSpec as P


def contract_rows(left, right):
    return lax.dot_general(
        left, right, (((0,), (0,)), ((), ())), preferred_element_type=jnp.float32
    )


def contract_cols(left, right):
    return lax.dot_general(
        left, right, (((1,), (1,)), ((), ())), preferred_element_type=jnp.float32
    )


def routed(tokens, expert_ids, gate_probs, out_cot, w_gate, w_up, w_down):
    tok_count, width = tokens.shape
    top = expert_ids.shape[1]
    experts = lax.axis_size("expert")
    slots = min(tok_count, 4 * tok_count * top // (3 * experts))
    flat_ids = expert_ids.reshape(-1)
    onehot = (flat_ids[:, None] == jnp.arange(experts, dtype=jnp.int32)[None, :]).astype(jnp.int32)
    ranks = jnp.sum(jnp.cumsum(onehot, axis=0) * onehot, axis=1) - 1
    target = flat_ids * slots + ranks
    token_rows = jnp.repeat(tokens, top, axis=0)
    outbound = jnp.zeros((experts * slots, width), tokens.dtype).at[target].set(token_rows)
    outbound = outbound.reshape(experts, slots, width)
    gate_mat = w_gate[0]
    up_mat = w_up[0]
    down_mat = w_down[0]
    hidden_width = gate_mat.shape[1]
    arrived = lax.all_to_all(outbound, "expert", split_axis=0, concat_axis=0, tiled=True)
    sources = arrived.shape[0]
    count = arrived.shape[1]
    rows = arrived.reshape(-1, width)
    gate_pre = jnp.dot(rows, gate_mat, preferred_element_type=jnp.float32)
    up_pre = jnp.dot(rows, up_mat, preferred_element_type=jnp.float32)
    hidden = (gate_pre * jax.nn.sigmoid(gate_pre) * up_pre).astype(jnp.bfloat16)
    result = jnp.dot(hidden, down_mat, preferred_element_type=jnp.float32).astype(jnp.bfloat16)
    expert_out, hidden, gate_pre, up_pre, arrived = (
        result.reshape(sources, count, width),
        hidden.reshape(sources, count, hidden_width),
        gate_pre.reshape(sources, count, hidden_width),
        up_pre.reshape(sources, count, hidden_width),
        arrived,
    )
    returned = lax.all_to_all(expert_out, "expert", split_axis=0, concat_axis=0, tiled=True)
    picked = returned.reshape(-1, width)[target].reshape(tok_count, top, width)
    layer_out = jnp.sum(gate_probs[:, :, None] * picked.astype(jnp.float32), axis=1).astype(
        jnp.bfloat16
    )
    out_grad = (gate_probs[:, :, None] * out_cot[:, None, :].astype(jnp.float32)).astype(
        jnp.bfloat16
    )
    outbound_grad = (
        jnp.zeros((experts * slots, width), tokens.dtype)
        .at[target]
        .set(out_grad.reshape(-1, width))
    )
    arrived_grad = lax.all_to_all(
        outbound_grad.reshape(experts, slots, width),
        "expert",
        split_axis=0,
        concat_axis=0,
        tiled=True,
    ).reshape(-1, width)
    x_rows = arrived.reshape(-1, width)
    hidden_rows = hidden.reshape(-1, hidden_width)
    gate_rows = gate_pre.reshape(-1, hidden_width)
    up_rows = up_pre.reshape(-1, hidden_width)
    hidden_grad = contract_cols(arrived_grad, down_mat)
    sigma = jax.nn.sigmoid(gate_rows)
    gate_grad = (hidden_grad * up_rows * sigma * (1.0 + gate_rows * (1.0 - sigma))).astype(
        jnp.bfloat16
    )
    up_grad = (hidden_grad * gate_rows * sigma).astype(jnp.bfloat16)
    row_grad = (contract_cols(gate_grad, gate_mat) + contract_cols(up_grad, up_mat)).astype(
        jnp.bfloat16
    )
    back_grad = lax.all_to_all(
        row_grad.reshape(experts, slots, width), "expert", split_axis=0, concat_axis=0, tiled=True
    )
    gathered = back_grad.reshape(-1, width)[target].reshape(tok_count, top, width)
    input_grad = jnp.sum(gathered.astype(jnp.float32), axis=1).astype(jnp.bfloat16)
    down_grad = lax.psum_scatter(
        contract_rows(hidden_rows, arrived_grad).astype(jnp.bfloat16),
        "dp",
        scatter_dimension=0,
        tiled=True,
    ).astype(jnp.float32)
    gate_part = lax.psum_scatter(
        contract_rows(x_rows, gate_grad).astype(jnp.bfloat16), "dp", scatter_dimension=0, tiled=True
    ).astype(jnp.float32)
    up_part = lax.psum_scatter(
        contract_rows(x_rows, up_grad).astype(jnp.bfloat16), "dp", scatter_dimension=0, tiled=True
    ).astype(jnp.float32)
    return (layer_out, input_grad, gate_part[None], up_part[None], down_grad[None])


BF16, F32 = jnp.bfloat16, jnp.float32
VMEM, SMEM, HBM, ANY = pltpu.VMEM, pltpu.SMEM, pltpu.HBM, pl.ANY
ORDER = ((8, 128), jnp.float32, pltpu.VMEM)


def stage(body, ins, outs, after=(), scratch=(), aliases=None):
    skipped = len(after)
    given = skipped + len(ins)

    def kernel(*refs):
        token = refs[given + len(outs)]
        body(*refs[skipped : given + len(outs)], *refs[given + len(outs) + 1 :])
        token[...] = jnp.zeros(token.shape, token.dtype)

    outs_all = list(outs) + [ORDER]
    outputs = pl.pallas_call(
        kernel,
        in_specs=[pl.BlockSpec(memory_space=m) for m in [ANY] * skipped + [m for _, m in ins]],
        out_specs=[pl.BlockSpec(memory_space=m) for _, _, m in outs_all],
        out_shape=[jax.ShapeDtypeStruct(shape, dtype) for shape, dtype, _ in outs_all],
        scratch_shapes=list(scratch),
        input_output_aliases={skipped + i: o for i, o in (aliases or {}).items()},
        cost_estimate=pl.CostEstimate(flops=0, bytes_accessed=0, transcendentals=0),
        compiler_params=pltpu.CompilerParams(vmem_limit_bytes=16 * 2**20),
    )(*after, *[a for a, _ in ins])
    return list(outputs)


def swap(value, axis, mask):
    size = lax.axis_size(axis)
    return lax.ppermute(value, axis, [(i, i ^ mask) for i in range(size)])


def chunks(width, most):
    return [(at, min(most, width - at)) for at in range(0, width, most)]


def packed(tokens, expert_ids, gate_probs, out_cot, experts, lanes):
    count, width = tokens.shape
    top = expert_ids.shape[1]

    def body(tok, ids, given, cot, both, sems):
        copies = [
            pltpu.make_async_copy(tok, both.at[:count, :width], sems.at[0]),
            pltpu.make_async_copy(cot, both.at[count:, :width], sems.at[1]),
        ]
        for copy in copies:
            copy.start()
        names = ids[...].T
        values = given[...].T
        column = lax.broadcasted_iota(jnp.int32, (count, lanes), 1)
        total = jnp.zeros((count, lanes), F32)
        for k in range(top):
            named = (names[:, k : k + 1] == column) | (names[:, k : k + 1] + experts == column)
            total = total + jnp.where(named, values[:, k : k + 1], 0.0)
        high = total.astype(BF16).astype(F32)
        both[:count, width:] = jnp.where(column < experts, high, total - high).astype(BF16)
        both[count:, width:] = jnp.zeros((count, lanes), BF16)
        for copy in copies:
            copy.wait()

    return stage(
        body,
        [(tokens, HBM), (expert_ids.T, VMEM), (gate_probs.T, VMEM), (out_cot, HBM)],
        [((2 * count, width + lanes), BF16, VMEM)],
        scratch=[pltpu.SemaphoreType.DMA((2,))],
    )


def kept_near(arrays, after):
    def body(*refs):
        n = len(arrays)
        copies = [pltpu.make_async_copy(refs[i], refs[n + i], refs[2 * n].at[i]) for i in range(n)]
        for copy in copies:
            copy.start()
        for copy in copies:
            copy.wait()

    return stage(
        body,
        [(a, HBM) for a in arrays],
        [(a.shape, a.dtype, VMEM) for a in arrays],
        after=after,
        scratch=[pltpu.SemaphoreType.DMA((len(arrays),))],
    )


def products(places, left, right, outs, own, tile=512):
    size = left.shape[0] // (1 + max(p | 1 for p in places))
    width = right.shape[1]
    for start, some in chunks(width, tile):
        piece = right[:, start : start + some]
        for m, (out, row) in zip(places, outs):
            part = left[pl.ds(pl.multiple_of((own ^ m) * size, size), size), :]
            out[row : row + size, start : start + some] = jnp.dot(
                part, piece, preferred_element_type=F32
            ).astype(out.dtype)


TURNED = (((1,), (1,)), ((), ()))


def dense(tokens, expert_ids, gate_probs, out_cot, w_gate, w_up, w_down):
    count, width = tokens.shape
    ff = w_gate.shape[2]
    experts = lax.axis_size("expert")
    owners = lax.axis_size("dp")
    me = lax.axis_index("expert").astype(jnp.int32).reshape(1)
    mine = lax.axis_index("dp").astype(jnp.int32).reshape(1)
    total = count * experts
    half = total // 2
    lanes = 128 * (-(-2 * experts // 128))
    odd_places = list(range(owners - 1, 0, -2))
    even_places = [m - 1 for m in odd_places]
    slab, band = ff // owners, width // owners

    near_bit, far_bit = 2, 4
    both, _ = packed(tokens, expert_ids, gate_probs, out_cot, experts, lanes)
    wide = width + lanes
    far = swap(both, "expert", far_bit)
    near = swap(both, "expert", near_bit)
    next_both = swap(both, "expert", 1)
    next_near = swap(near, "expert", 1)
    next_far = swap(far, "expert", 1)
    far_on, _ = stage(
        lambda *_: None,
        [(far, ANY), (next_both, ANY)],
        [(far.shape, BF16, ANY)],
        aliases={0: 0},
    )
    far_near = swap(far_on, "expert", near_bit)
    (done,) = stage(lambda *_: None, [(next_near, ANY)], [])

    def apart(pair, tok, cot):
        tok[...] = pair[:count, :]
        cot[...] = pair[count:, :width]

    last_tok, last_cot, done = stage(
        apart,
        [(far_near, VMEM)],
        [((count, wide), BF16, VMEM), ((count, width), BF16, VMEM)],
        after=[done],
    )
    next_last_tok = swap(last_tok, "expert", 1)
    next_last_cot = swap(last_cot, "expert", 1)
    gate_near, up_near, down_near, done = kept_near([w[0] for w in (w_gate, w_up, w_down)], [done])
    whole = [both, far, near, next_both, next_far, next_near]
    tok_pieces = [(a, 0) for a in whole]
    cot_pieces = [(a, count) for a in whole]
    tok_pieces[3:3] = [(last_tok, 0)]
    cot_pieces[3:3] = [(last_cot, 0)]
    tok_pieces.append((next_last_tok, 0))
    cot_pieces.append((next_last_cot, 0))

    def refs_of(pieces):
        arrays = []
        for a, _ in pieces:
            if not any(a is b for b in arrays):
                arrays.append(a)
        where = [next(i for i, b in enumerate(arrays) if b is a) for a, _ in pieces]
        return arrays, [(i, row) for i, (_, row) in zip(where, pieces)]

    tok_arrays, tok_where = refs_of(tok_pieces)
    cot_arrays, cot_where = refs_of(cot_pieces)

    def forward(me_ref, *refs):
        blocks = refs[: len(tok_arrays)]
        gate, up, down, flipped, hidden_t, gate_by, up_by, even, odd, rows, probs, hidden = refs[
            len(tok_arrays) :
        ]
        own = me_ref[0]
        column = lax.broadcasted_iota(jnp.int32, (count, lanes), 1)
        chosen = (column == own) | (column == own + experts)
        for b, (i, row) in enumerate(tok_where):
            place = pl.ds(b * count, count)
            rows[place, :] = blocks[i][row : row + count, :width]
            side = jnp.where(chosen, blocks[i][row : row + count, width:].astype(F32), 0.0)
            probs[place, :] = jnp.sum(side, axis=1, keepdims=True)
        weight = probs[...]
        for start, size in chunks(ff, 256):
            place = slice(start, start + size)
            gate_pre = jnp.dot(rows[...], gate[:, place], preferred_element_type=F32)
            up_pre = jnp.dot(rows[...], up[:, place], preferred_element_type=F32)
            sigma = jax.nn.sigmoid(gate_pre)
            silu = gate_pre * sigma
            scaled = weight * up_pre
            hidden[:, place] = (silu * scaled).astype(BF16)
            gate_by[:, place] = scaled * sigma * (1.0 + gate_pre * (1.0 - sigma))
            up_by[:, place] = weight * silu
        for start, size in chunks(width, 512):
            place = slice(start, start + size)
            part = jnp.dot(hidden[...], down[:, place], preferred_element_type=F32).astype(BF16)
            even[:, place] = part[:half]
            odd[:, place] = part[half:]
        for start, size in chunks(width, 512):
            flipped[start : start + size, :] = rows[:, start : start + size].T
        for start, size in chunks(ff, 256):
            hidden_t[start : start + size, :] = hidden[:, start : start + size].T

    flipped, hidden_t, gate_by, up_by, out_even, out_odd, _ = stage(
        forward,
        [(me, SMEM)] + [(a, VMEM) for a in tok_arrays + [gate_near, up_near, down_near]],
        [
            ((width, total), BF16, VMEM),
            ((ff, total), BF16, VMEM),
            ((total, ff), F32, VMEM),
            ((total, ff), F32, VMEM),
            ((half, width), BF16, VMEM),
            ((half, width), BF16, VMEM),
        ],
        scratch=[VMEM((total, width), BF16), VMEM((total, 1), F32), VMEM((total, ff), BF16)],
    )

    def down_odd(own_ref, *refs):
        blocks = refs[: len(cot_arrays)]
        left, _, _, rows, away = refs[len(cot_arrays) :]
        for b, (i, row) in enumerate(cot_where):
            rows[b * count : (b + 1) * count, :] = blocks[i][row : row + count, :width]
        outs = [(away, i * slab) for i in range(len(odd_places))]
        products(odd_places, left, rows, outs, own_ref[0])

    out_odd, cot_rows, down_away, done = stage(
        down_odd,
        [(mine, SMEM)] + [(a, VMEM) for a in cot_arrays] + [(hidden_t, VMEM), (out_odd, ANY)],
        [
            ((half, width), BF16, ANY),
            ((total, width), BF16, VMEM),
            ((slab * len(odd_places), width), BF16, VMEM),
        ],
        aliases={len(cot_arrays) + 2: 0},
    )
    down_came = swap(down_away, "dp", 1)
    out_came = swap(out_odd, "expert", 1)

    def backward(own_ref, cot, left, down, gate_ref, up_ref, grads, *kept):
        products(even_places, left, cot, [(k, 0) for k in kept], own_ref[0])
        for start, size in chunks(ff, 256):
            place = slice(start, start + size)
            grad = lax.dot_general(cot[...], down[place, :], TURNED, preferred_element_type=F32)
            grads[:, place] = (grad * gate_ref[:, place]).astype(BF16)
            grads[:, ff + start : ff + start + size] = (grad * up_ref[:, place]).astype(BF16)

    grads, *down_kept, done = stage(
        backward,
        [(mine, SMEM)] + [(a, VMEM) for a in (cot_rows, hidden_t, down_near, gate_by, up_by)],
        [((total, 2 * ff), BF16, VMEM)] + [((slab, width), BF16, VMEM)] * len(even_places),
        after=[done],
    )

    def added(kept, came, after=()):
        n, size = len(kept), kept[0].shape[0]

        def body(*refs):
            for i in range(n):
                other = refs[n][i * size : (i + 1) * size, :].astype(F32)
                refs[n + 1 + i][...] = (refs[i][...].astype(F32) + other).astype(BF16)

        return stage(
            body,
            [(a, VMEM) for a in [*kept, came]],
            [(a.shape, BF16, VMEM) for a in kept],
            after=after,
        )

    *down_send, done = added(down_kept[:-1], down_came, [done])
    down_got = [swap(a, "dp", m) for a, m in zip(down_send, even_places)]

    def both_odd(own_ref, left, right, away):
        outs = [(away, i * band) for i in range(len(odd_places))]
        products(odd_places, left, right, outs, own_ref[0], 256)

    def both_even(own_ref, left, right, *kept):
        products(even_places, left, right, [(k, 0) for k in kept], own_ref[0], 256)

    given = [(mine, SMEM), (flipped, VMEM), (grads, VMEM)]
    both_away, done = stage(
        both_odd, given, [((band * len(odd_places), 2 * ff), BF16, VMEM)], after=[done]
    )
    both_came = swap(both_away, "dp", 1)
    *both_kept, done = stage(
        both_even, given, [((band, 2 * ff), BF16, VMEM)] * len(even_places), after=[done]
    )
    def half_added(first, after):
        n = len(both_kept) - 1
        place = slice(first, first + ff)

        def body(*refs):
            for i in range(n):
                other = refs[n][i * band : (i + 1) * band, place].astype(F32)
                refs[n + 1 + i][...] = (refs[i][:, place].astype(F32) + other).astype(BF16)

        *sends, done = stage(
            body,
            [(a, VMEM) for a in [*both_kept[:-1], both_came]],
            [((band, ff), BF16, VMEM)] * n,
            after=after,
        )
        return [swap(a, "dp", m) for a, m in zip(sends, even_places)], done

    gate_got, done = half_added(0, [done])

    def input_rows(grad, gate, up, even, odd):
        for start, size in chunks(width, 512):
            place = slice(start, start + size)
            rows = lax.dot_general(
                grad[:, :ff], gate[place, :], TURNED, preferred_element_type=F32
            ) + lax.dot_general(grad[:, ff:], up[place, :], TURNED, preferred_element_type=F32)
            rows = rows.astype(BF16)
            even[:, place] = rows[:half]
            odd[:, place] = rows[half:]

    in_even, in_odd, done = stage(
        input_rows,
        [(grads, VMEM), (gate_near, VMEM), (up_near, VMEM)],
        [((half, width), BF16, VMEM)] * 2,
        after=[done],
    )
    in_came = swap(in_odd, "expert", 1)

    def folded(held, came, after):
        rows = held.shape[0]
        parts = 1 if rows == count else 2

        def body(a, b, *outs):
            for i, out in enumerate(outs):
                place = slice(i * rows // parts, (i + 1) * rows // parts)
                out[...] = (a[place, :].astype(F32) + b[place, :].astype(F32)).astype(BF16)

        return stage(
            body,
            [(held, VMEM), (came, VMEM)],
            [((rows // parts, width), BF16, VMEM)] * parts,
            after=after,
        )

    def owned(kept, came, got, after, column=0):
        size, wide = got[0].shape
        step = 64
        first = came.shape[0] // step - size // step
        skipped = len(after)

        def body(*refs):
            value = refs[skipped][...].astype(F32)
            for ref in refs[skipped + 1 : -2]:
                value = value + ref[...].astype(F32)
            refs[-2][...] = value
            refs[-1][...] = jnp.zeros(ORDER[0], F32)

        at = column // wide
        outputs = pl.pallas_call(
            body,
            grid=(size // step,),
            in_specs=[pl.BlockSpec(memory_space=ANY)] * skipped
            + [
                pl.BlockSpec((step, wide), lambda i: (i, at)),
                pl.BlockSpec((step, wide), lambda i: (i + first, at)),
            ]
            + [pl.BlockSpec((step, wide), lambda i: (i, 0))] * len(got),
            out_specs=[
                pl.BlockSpec((step, wide), lambda i: (i, 0)),
                pl.BlockSpec(ORDER[0], lambda i: (0, 0)),
            ],
            out_shape=[jax.ShapeDtypeStruct((size, wide), F32), jax.ShapeDtypeStruct(*ORDER[:2])],
            cost_estimate=pl.CostEstimate(flops=0, bytes_accessed=0, transcendentals=0),
            compiler_params=pltpu.CompilerParams(vmem_limit_bytes=16 * 2**20),
        )(*after, kept, came, *got)
        return list(outputs)

    def fold_on(held, came, bit, after):
        held, send, done = folded(held, came, after)
        return held, swap(send, "expert", bit), done

    out_held, out_came, done = fold_on(out_even, out_came, near_bit, [done])
    down_grad, done = owned(down_kept[-1], down_came, down_got, [done])
    up_got, done = half_added(ff, [done])
    out_held, out_came, done = fold_on(out_held, out_came, far_bit, [done])
    gate_part, done = owned(both_kept[-1], both_came, gate_got, [done])
    in_held, in_came, done = fold_on(in_even, in_came, near_bit, [done])
    layer_out, done = folded(out_held, out_came, [done])
    in_held, in_came, done = fold_on(in_held, in_came, far_bit, [done])
    input_grad, done = folded(in_held, in_came, [done])
    up_part, _ = owned(both_kept[-1], both_came, up_got, [done], ff)
    return (layer_out, input_grad, gate_part[None], up_part[None], down_grad[None])


def shards(tokens, expert_ids, *rest):
    experts = lax.axis_size("expert")
    every = expert_ids.shape[1] == experts and experts == 8
    return (dense if every else routed)(tokens, expert_ids, *rest)


def solution(mesh):
    placed = (
        P(("dp", "expert"), None),
        P(("dp", "expert"), None),
        P(("dp", "expert"), None),
        P(("dp", "expert"), None),
        P("expert", None, None),
        P("expert", None, None),
        P("expert", None, None),
    )
    return jax.shard_map(
        shards,
        mesh=mesh,
        in_specs=placed,
        out_specs=(
            P(("dp", "expert"), None),
            P(("dp", "expert"), None),
            P("expert", "dp", None),
            P("expert", "dp", None),
            P("expert", "dp", None),
        ),
        check_vma=False,
    )
```

```python
import jax
import jax.numpy as jnp
from jax import lax
from jax.experimental import pallas as pl
from jax.experimental.pallas import tpu as pltpu
from jax.sharding import PartitionSpec as P


def contract_rows(left, right):
    return lax.dot_general(
        left, right, (((0,), (0,)), ((), ())), preferred_element_type=jnp.float32
    )


def contract_cols(left, right):
    return lax.dot_general(
        left, right, (((1,), (1,)), ((), ())), preferred_element_type=jnp.float32
    )


def routed(tokens, expert_ids, gate_probs, out_cot, w_gate, w_up, w_down):
    tok_count, width = tokens.shape
    top = expert_ids.shape[1]
    experts = lax.axis_size("expert")
    slots = min(tok_count, 4 * tok_count * top // (3 * experts))
    flat_ids = expert_ids.reshape(-1)
    onehot = (flat_ids[:, None] == jnp.arange(experts, dtype=jnp.int32)[None, :]).astype(jnp.int32)
    ranks = jnp.sum(jnp.cumsum(onehot, axis=0) * onehot, axis=1) - 1
    target = flat_ids * slots + ranks
    token_rows = jnp.repeat(tokens, top, axis=0)
    outbound = jnp.zeros((experts * slots, width), tokens.dtype).at[target].set(token_rows)
    outbound = outbound.reshape(experts, slots, width)
    gate_mat = w_gate[0]
    up_mat = w_up[0]
    down_mat = w_down[0]
    hidden_width = gate_mat.shape[1]
    arrived = lax.all_to_all(outbound, "expert", split_axis=0, concat_axis=0, tiled=True)
    sources = arrived.shape[0]
    count = arrived.shape[1]
    rows = arrived.reshape(-1, width)
    gate_pre = jnp.dot(rows, gate_mat, preferred_element_type=jnp.float32)
    up_pre = jnp.dot(rows, up_mat, preferred_element_type=jnp.float32)
    hidden = (gate_pre * jax.nn.sigmoid(gate_pre) * up_pre).astype(jnp.bfloat16)
    result = jnp.dot(hidden, down_mat, preferred_element_type=jnp.float32).astype(jnp.bfloat16)
    expert_out, hidden, gate_pre, up_pre, arrived = (
        result.reshape(sources, count, width),
        hidden.reshape(sources, count, hidden_width),
        gate_pre.reshape(sources, count, hidden_width),
        up_pre.reshape(sources, count, hidden_width),
        arrived,
    )
    returned = lax.all_to_all(expert_out, "expert", split_axis=0, concat_axis=0, tiled=True)
    picked = returned.reshape(-1, width)[target].reshape(tok_count, top, width)
    layer_out = jnp.sum(gate_probs[:, :, None] * picked.astype(jnp.float32), axis=1).astype(
        jnp.bfloat16
    )
    out_grad = (gate_probs[:, :, None] * out_cot[:, None, :].astype(jnp.float32)).astype(
        jnp.bfloat16
    )
    outbound_grad = (
        jnp.zeros((experts * slots, width), tokens.dtype)
        .at[target]
        .set(out_grad.reshape(-1, width))
    )
    arrived_grad = lax.all_to_all(
        outbound_grad.reshape(experts, slots, width),
        "expert",
        split_axis=0,
        concat_axis=0,
        tiled=True,
    ).reshape(-1, width)
    x_rows = arrived.reshape(-1, width)
    hidden_rows = hidden.reshape(-1, hidden_width)
    gate_rows = gate_pre.reshape(-1, hidden_width)
    up_rows = up_pre.reshape(-1, hidden_width)
    hidden_grad = contract_cols(arrived_grad, down_mat)
    sigma = jax.nn.sigmoid(gate_rows)
    gate_grad = (hidden_grad * up_rows * sigma * (1.0 + gate_rows * (1.0 - sigma))).astype(
        jnp.bfloat16
    )
    up_grad = (hidden_grad * gate_rows * sigma).astype(jnp.bfloat16)
    row_grad = (contract_cols(gate_grad, gate_mat) + contract_cols(up_grad, up_mat)).astype(
        jnp.bfloat16
    )
    back_grad = lax.all_to_all(
        row_grad.reshape(experts, slots, width), "expert", split_axis=0, concat_axis=0, tiled=True
    )
    gathered = back_grad.reshape(-1, width)[target].reshape(tok_count, top, width)
    input_grad = jnp.sum(gathered.astype(jnp.float32), axis=1).astype(jnp.bfloat16)
    down_grad = lax.psum_scatter(
        contract_rows(hidden_rows, arrived_grad).astype(jnp.bfloat16),
        "dp",
        scatter_dimension=0,
        tiled=True,
    ).astype(jnp.float32)
    gate_part = lax.psum_scatter(
        contract_rows(x_rows, gate_grad).astype(jnp.bfloat16), "dp", scatter_dimension=0, tiled=True
    ).astype(jnp.float32)
    up_part = lax.psum_scatter(
        contract_rows(x_rows, up_grad).astype(jnp.bfloat16), "dp", scatter_dimension=0, tiled=True
    ).astype(jnp.float32)
    return (layer_out, input_grad, gate_part[None], up_part[None], down_grad[None])


BF16, F32 = jnp.bfloat16, jnp.float32
VMEM, SMEM, HBM, ANY = pltpu.VMEM, pltpu.SMEM, pltpu.HBM, pl.ANY
ORDER = ((8, 128), jnp.float32, pltpu.VMEM)


def stage(body, ins, outs, after=(), scratch=(), aliases=None, vmem=8):
    skipped = len(after)
    given = skipped + len(ins)

    def kernel(*refs):
        token = refs[given + len(outs)]
        body(*refs[skipped : given + len(outs)], *refs[given + len(outs) + 1 :])
        token[...] = jnp.zeros(token.shape, token.dtype)

    outs_all = list(outs) + [ORDER]
    outputs = pl.pallas_call(
        kernel,
        in_specs=[pl.BlockSpec(memory_space=m) for m in [ANY] * skipped + [m for _, m in ins]],
        out_specs=[pl.BlockSpec(memory_space=m) for _, _, m in outs_all],
        out_shape=[jax.ShapeDtypeStruct(shape, dtype) for shape, dtype, _ in outs_all],
        scratch_shapes=list(scratch),
        input_output_aliases={skipped + i: o for i, o in (aliases or {}).items()},
        cost_estimate=pl.CostEstimate(flops=0, bytes_accessed=0, transcendentals=0),
        compiler_params=pltpu.CompilerParams(vmem_limit_bytes=vmem * 2**20),
    )(*after, *[pltpu.with_memory_space_constraint(a, HBM) if m is HBM else a for a, m in ins])
    return list(outputs)


def swap(value, axis, mask):
    size = lax.axis_size(axis)
    return lax.ppermute(value, axis, [(i, i ^ mask) for i in range(size)])


def chunks(width, most):
    return [(at, min(most, width - at)) for at in range(0, width, most)]


def packed(tokens, expert_ids, gate_probs, out_cot, experts, lanes):
    count, width = tokens.shape
    top = expert_ids.shape[1]

    def body(tok, ids, given, cot, alone, both, sems):
        copies = [
            pltpu.make_async_copy(tok, alone.at[:, :width], sems.at[0]),
            pltpu.make_async_copy(tok, both.at[:count, :width], sems.at[1]),
            pltpu.make_async_copy(cot, both.at[count:, :width], sems.at[2]),
        ]
        for copy in copies:
            copy.start()
        names = ids[...].T
        values = given[...].T
        column = lax.broadcasted_iota(jnp.int32, (count, lanes), 1)
        total = jnp.zeros((count, lanes), F32)
        for k in range(top):
            named = (names[:, k : k + 1] == column) | (names[:, k : k + 1] + experts == column)
            total = total + jnp.where(named, values[:, k : k + 1], 0.0)
        high = total.astype(BF16).astype(F32)
        side = jnp.where(column < experts, high, total - high).astype(BF16)
        alone[:, width:] = side
        both[:count, width:] = side
        both[count:, width:] = jnp.zeros((count, lanes), BF16)
        for copy in copies:
            copy.wait()

    return stage(
        body,
        [(tokens, HBM), (expert_ids.T, VMEM), (gate_probs.T, VMEM), (out_cot, HBM)],
        [((count, width + lanes), BF16, VMEM), ((2 * count, width + lanes), BF16, VMEM)],
        scratch=[pltpu.SemaphoreType.DMA((3,))],
            )


def products(places, left, right, outs, own, tile=512):
    size = left.shape[0] // (1 + max(p | 1 for p in places))
    width = right.shape[1]
    for start, some in chunks(width, tile):
        piece = right[:, start : start + some]
        for m, (out, row) in zip(places, outs):
            part = left[pl.ds(pl.multiple_of((own ^ m) * size, size), size), :]
            out[row : row + size, start : start + some] = jnp.dot(
                part, piece, preferred_element_type=F32
            ).astype(out.dtype)


TURNED = (((1,), (1,)), ((), ()))


def dense(tokens, expert_ids, gate_probs, out_cot, w_gate, w_up, w_down):
    count, width = tokens.shape
    ff = w_gate.shape[2]
    experts = lax.axis_size("expert")
    owners = lax.axis_size("dp")
    me = lax.axis_index("expert").astype(jnp.int32).reshape(1)
    mine = lax.axis_index("dp").astype(jnp.int32).reshape(1)
    total = count * experts
    half = total // 2
    pair = half // 2
    lanes = 128 * (-(-2 * experts // 128))
    odd_places = list(range(owners - 1, 0, -2))
    even_places = [m - 1 for m in odd_places]
    slab, band = ff // owners, width // owners

    near_bit, far_bit = 2, 4
    wide = width + lanes
    tok_own, both, done = packed(tokens, expert_ids, gate_probs, out_cot, experts, lanes)
    tok_far = swap(tok_own, "expert", far_bit)
    tok_near = swap(tok_own, "expert", near_bit)
    next_both = swap(both, "expert", 1)
    def copied(sources, width, after, waits=()):
        rows = count * len(sources)

        def body(*refs):
            out = refs[-1]
            for i, (_, row) in enumerate(sources):
                out[i * count : (i + 1) * count, :] = refs[i][row : row + count, :width]

        return stage(
            body,
            [(a, VMEM) for a, _ in sources] + [(a, ANY) for a in waits],
            [((rows, width), BF16, VMEM)],
            after=after,
        )

    tok_pair, done = copied([(tok_near, 0), (tok_far, 0)], wide, [done], [next_both])
    cot_own, done = copied([(both, count)], width, [done])
    tok_far_on, done = copied([(tok_far, 0)], wide, [done])
    next_tok_pair = swap(tok_pair, "expert", 1)
    tok_last = swap(tok_far_on, "expert", near_bit)
    cot_far = swap(cot_own, "expert", far_bit)
    cot_near = swap(cot_own, "expert", near_bit)
    tok_last_on, done = copied([(tok_last, 0)], wide, [done])
    next_tok_last = swap(tok_last_on, "expert", 1)
    cot_pair, done = copied([(cot_near, 0), (cot_far, 0)], width, [done])
    cot_far_on, done = copied([(cot_far, 0)], width, [done])
    next_cot_pair = swap(cot_pair, "expert", 1)
    cot_last = swap(cot_far_on, "expert", near_bit)
    tok_pieces = [(tok_own, 0), (tok_pair, count), (tok_pair, 0), (tok_last_on, 0)]
    tok_pieces += [(next_both, 0), (next_tok_pair, count), (next_tok_pair, 0), (next_tok_last, 0)]

    def refs_of(pieces):
        arrays = []
        for a, _ in pieces:
            if not any(a is b for b in arrays):
                arrays.append(a)
        where = [next(i for i, b in enumerate(arrays) if b is a) for a, _ in pieces]
        return arrays, [(i, row) for i, (_, row) in zip(where, pieces)]

    tok_arrays, tok_where = refs_of(tok_pieces)

    cot_last_on, done = copied([(cot_last, 0)], width, [done], [next_tok_last])
    next_cot_last = swap(cot_last_on, "expert", 1)
    cot_pieces = [(cot_own, 0), (cot_pair, count), (cot_pair, 0), (cot_last_on, 0)]
    cot_pieces += [(next_both, count), (next_cot_pair, count), (next_cot_pair, 0), (next_cot_last, 0)]
    def forward(me_ref, mine_ref, *refs):
        blocks = refs[: len(tok_arrays)]
        weights = refs[len(tok_arrays) : len(tok_arrays) + 3]
        flipped, flipped_sent, hidden_t, gate_by, up_by, kept, sent = refs[
            len(tok_arrays) + 3 : len(tok_arrays) + 10
        ]
        rows, probs, hidden, gate, up, down, sems = refs[len(tok_arrays) + 10 :]
        steps = chunks(ff, 256)
        copies = []
        for i, (start, size) in enumerate(steps):
            place = slice(start, start + size)
            for j, (far_ref, near_ref) in enumerate([(weights[0], gate), (weights[1], up)]):
                copies.append(
                    pltpu.make_async_copy(far_ref.at[:, place], near_ref.at[:, place], sems.at[2 * i + j])
                )
        copies.append(pltpu.make_async_copy(weights[2], down, sems.at[2 * len(steps)]))
        for copy in copies:
            copy.start()
        own = me_ref[0]
        column = lax.broadcasted_iota(jnp.int32, (count, lanes), 1)
        chosen = (column == own) | (column == own + experts)
        for b, (i, row) in enumerate(tok_where):
            place = pl.ds(b * count, count)
            rows[place, :] = blocks[i][row : row + count, :width]
            side = jnp.where(chosen, blocks[i][row : row + count, width:].astype(F32), 0.0)
            probs[place, :] = jnp.sum(side, axis=1, keepdims=True)
        weight = probs[...]
        for out, places in ((flipped, even_places), (flipped_sent, odd_places)):
            for i, m in enumerate(places):
                start = pl.multiple_of((mine_ref[0] ^ m) * band, band)
                out[i * band : (i + 1) * band, :] = rows[:, pl.ds(start, band)].T
        for i, (start, size) in enumerate(steps):
            place = slice(start, start + size)
            copies[2 * i].wait()
            gate_pre = jnp.dot(rows[...], gate[:, place], preferred_element_type=F32)
            copies[2 * i + 1].wait()
            up_pre = jnp.dot(rows[...], up[:, place], preferred_element_type=F32)
            sigma = jax.nn.sigmoid(gate_pre)
            silu = gate_pre * sigma
            scaled = weight * up_pre
            hidden[:, place] = (silu * scaled).astype(BF16)
            gate_by[:, place] = scaled * sigma * (1.0 + gate_pre * (1.0 - sigma))
            up_by[:, place] = weight * silu
            hidden_t[place, :] = hidden[:, place].T
        copies[-1].wait()
        for start, size in chunks(width, 512):
            place = slice(start, start + size)
            part = jnp.dot(hidden[...], down[:, place], preferred_element_type=F32).astype(BF16)
            for i in range(2):
                low, high = slice(i * pair, (i + 1) * pair), i * half
                kept[low, place] = part[high : high + pair]
                sent[low, place] = part[high + pair : high + half]

    flipped, flipped_sent, hidden_t, gate_by, up_by, out_kept, out_sent, done = stage(
        forward,
        [(me, SMEM), (mine, SMEM)] + [(a, VMEM) for a in tok_arrays] + [(w[0], HBM) for w in (w_gate, w_up, w_down)],
        [
            ((width // 2, total), BF16, VMEM),
            ((width // 2, total), BF16, VMEM),
            ((ff, total), BF16, VMEM),
            ((total, ff), F32, VMEM),
            ((total, ff), F32, VMEM),
            ((half, width), BF16, VMEM),
            ((half, width), BF16, VMEM),
        ],
        scratch=[
            VMEM((total, width), BF16),
            VMEM((total, 1), F32),
            VMEM((total, ff), BF16),
            VMEM((width, ff), BF16),
            VMEM((width, ff), BF16),
            VMEM((ff, width), BF16),
            pltpu.SemaphoreType.DMA((2 * len(chunks(ff, 256)) + 1,)),
        ],
        after=[done],
        vmem=16,
    )
    flipped_came = swap(flipped_sent, "dp", 1)
    cot_arrays, cot_where = refs_of(cot_pieces)

    def down_odd(own_ref, *refs):
        blocks = refs[: len(cot_arrays)]
        left, rows, away = refs[len(cot_arrays) :]
        for b, (i, row) in enumerate(cot_where):
            rows[b * count : (b + 1) * count, :] = blocks[i][row : row + count, :width]
        outs = [(away, i * slab) for i in range(len(odd_places))]
        products(odd_places, left, rows, outs, own_ref[0])

    cot_rows, down_away, done = stage(
        down_odd,
        [(mine, SMEM)] + [(a, VMEM) for a in cot_arrays] + [(hidden_t, VMEM)],
        [((total, width), BF16, VMEM), ((slab * len(odd_places), width), BF16, VMEM)],
        after=[done],
    )
    down_came = swap(down_away, "dp", 1)
    out_came = swap(out_sent, "expert", near_bit)

    def backward(own_ref, cot, left, down, gate_ref, up_ref, grads, *refs):
        *kept, near, sem = refs
        copy = pltpu.make_async_copy(down, near, sem)
        copy.start()
        products(even_places, left, cot, [(k, 0) for k in kept], own_ref[0])
        copy.wait()
        for start, size in chunks(ff, 256):
            place = slice(start, start + size)
            grad = lax.dot_general(cot[...], near[place, :], TURNED, preferred_element_type=F32)
            grads[:, place] = (grad * gate_ref[:, place]).astype(BF16)
            grads[:, ff + start : ff + start + size] = (grad * up_ref[:, place]).astype(BF16)

    grads, *down_kept, done = stage(
        backward,
        [(mine, SMEM), (cot_rows, VMEM), (hidden_t, VMEM), (w_down[0], HBM)]
        + [(gate_by, VMEM), (up_by, VMEM)],
        [((total, 2 * ff), BF16, VMEM)] + [((slab, width), BF16, VMEM)] * len(even_places),
        scratch=[VMEM((ff, width), BF16), pltpu.SemaphoreType.DMA],
        after=[done],
    )

    grads_came = swap(grads, "dp", 1)

    def added(kept, came, after=()):
        n, size = len(kept), kept[0].shape[0]

        def body(*refs):
            for i in range(n):
                other = refs[n][i * size : (i + 1) * size, :].astype(F32)
                refs[n + 1 + i][...] = (refs[i][...].astype(F32) + other).astype(BF16)

        return stage(
            body,
            [(a, VMEM) for a in [*kept, came]],
            [(a.shape, BF16, VMEM) for a in kept],
            after=after,
        )

    *down_send, done = added(down_kept[:-1], down_came, [done])
    down_got = [swap(a, "dp", m) for a, m in zip(down_send, even_places)]

    def input_rows(grad, gate_far, up_far, even, odd, gate, up, sems):
        steps = chunks(width, 512)
        copies = []
        for i, (start, size) in enumerate(steps):
            place = slice(start, start + size)
            for j, (far_ref, near_ref) in enumerate([(gate_far, gate), (up_far, up)]):
                copies.append(
                    pltpu.make_async_copy(far_ref.at[place], near_ref.at[place], sems.at[2 * i + j])
                )
        for copy in copies:
            copy.start()
        for i, (start, size) in enumerate(steps):
            place = slice(start, start + size)
            copies[2 * i].wait()
            rows = lax.dot_general(grad[:, :ff], gate[place, :], TURNED, preferred_element_type=F32)
            copies[2 * i + 1].wait()
            rows = rows + lax.dot_general(
                grad[:, ff:], up[place, :], TURNED, preferred_element_type=F32
            )
            rows = rows.astype(BF16)
            even[:, place] = rows[:half]
            odd[:, place] = rows[half:]

    in_even, in_odd, done = stage(
        input_rows,
        [(grads, VMEM), (w_gate[0], HBM), (w_up[0], HBM)],
        [((half, width), BF16, VMEM)] * 2,
        scratch=[VMEM((width, ff), BF16)] * 2
        + [pltpu.SemaphoreType.DMA((2 * len(chunks(width, 512)),))],
        after=[done],
        vmem=10,
    )
    in_came = swap(in_odd, "expert", 1)

    def both_parts(left, left_came, grad, grad_came, *outs):
        n = len(even_places)
        for i in range(n):
            place = slice(i * band, (i + 1) * band)
            for start, size in chunks(2 * ff, 256):
                column = slice(start, start + size)
                value = jnp.dot(left[place, :], grad[:, column], preferred_element_type=F32)
                value += jnp.dot(left_came[place, :], grad_came[:, column], preferred_element_type=F32)
                out = outs[2 * i + start // ff]
                out[:, start % ff : start % ff + size] = value.astype(out.dtype)

    *both_kept, done = stage(
        both_parts,
        [(a, VMEM) for a in (flipped, flipped_came, grads, grads_came)],
        [((band, ff), BF16, VMEM)] * (2 * len(even_places) - 2) + [((band, ff), F32, VMEM)] * 2,
        after=[done],
    )
    gate_sums, up_sums = both_kept[0::2], both_kept[1::2]
    gate_got = [swap(a, "dp", m) for a, m in zip(gate_sums[:-1], even_places)]

    def folded(held, came, after):
        rows = held.shape[0]
        parts = 1 if rows == count else 2

        def body(a, b, *outs):
            for i, out in enumerate(outs):
                place = slice(i * rows // parts, (i + 1) * rows // parts)
                out[...] = (a[place, :].astype(F32) + b[place, :].astype(F32)).astype(BF16)

        return stage(
            body,
            [(held, VMEM), (came, VMEM)],
            [((rows // parts, width), BF16, VMEM)] * parts,
            after=after,
        )

    def owned(parts, after):
        size, wide = parts[-1].shape
        step = size // 4

        def body(*refs):
            *others, out, total, sems = refs
            copies = []
            for i in range(4):
                at = slice(i * step, (i + 1) * step)
                value = jnp.zeros((step, wide), F32)
                for ref in others:
                    first = ref.shape[0] - size + i * step
                    value = value + ref[first : first + step, :].astype(F32)
                total[at, :] = value
                copies.append(pltpu.make_async_copy(total.at[at], out.at[at], sems.at[i]))
                copies[-1].start()
            for copy in copies:
                copy.wait()

        return stage(
            body,
            [(a, VMEM) for a in parts],
            [((size, wide), F32, HBM)],
            scratch=[VMEM((size, wide), F32), pltpu.SemaphoreType.DMA((4,))],
            after=after,
        )

    def fold_on(held, came, bit, after):
        held, send, done = folded(held, came, after)
        return held, swap(send, "expert", bit), done

    down_grad, done = owned([down_kept[-1], down_came, *down_got], [done])
    up_send = []
    for a in up_sums[:-1]:
        a, done = stage(
            lambda *_: None, [(a, ANY)], [(a.shape, BF16, ANY)], after=[done], aliases={0: 0}
        )
        up_send.append(a)
    up_got = [swap(a, "dp", m) for a, m in zip(up_send, even_places)]
    out_held, out_came, done = fold_on(out_kept, out_came, 1, [done])
    in_held, in_came, done = fold_on(in_even, in_came, near_bit, [done])
    out_held, out_came, done = fold_on(out_held, out_came, far_bit, [done])
    gate_part, done = owned([gate_sums[-1], *gate_got], [done])
    in_held, in_came, done = fold_on(in_held, in_came, far_bit, [done])
    layer_out, done = folded(out_held, out_came, [done])
    input_grad, done = folded(in_held, in_came, [done])
    up_part, _ = owned([up_sums[-1], *up_got], [done])
    return (layer_out, input_grad, gate_part[None], up_part[None], down_grad[None])


def shards(tokens, expert_ids, *rest):
    experts = lax.axis_size("expert")
    every = expert_ids.shape[1] == experts and experts == 8
    return (dense if every else routed)(tokens, expert_ids, *rest)


def solution(mesh):
    placed = (
        P(("dp", "expert"), None),
        P(("dp", "expert"), None),
        P(("dp", "expert"), None),
        P(("dp", "expert"), None),
        P("expert", None, None),
        P("expert", None, None),
        P("expert", None, None),
    )
    return jax.shard_map(
        shards,
        mesh=mesh,
        in_specs=placed,
        out_specs=(
            P(("dp", "expert"), None),
            P(("dp", "expert"), None),
            P("expert", "dp", None),
            P("expert", "dp", None),
            P("expert", "dp", None),
        ),
        check_vma=False,
    )
```

```python
import jax
import jax.numpy as jnp
from jax import lax
from jax.experimental import pallas as pl
from jax.experimental.pallas import tpu as pltpu
from jax.sharding import PartitionSpec as P


def contract_rows(left, right):
    return lax.dot_general(
        left, right, (((0,), (0,)), ((), ())), preferred_element_type=jnp.float32
    )


def contract_cols(left, right):
    return lax.dot_general(
        left, right, (((1,), (1,)), ((), ())), preferred_element_type=jnp.float32
    )


def routed(tokens, expert_ids, gate_probs, out_cot, w_gate, w_up, w_down):
    tok_count, width = tokens.shape
    top = expert_ids.shape[1]
    experts = lax.axis_size("expert")
    slots = min(tok_count, 4 * tok_count * top // (3 * experts))
    flat_ids = expert_ids.reshape(-1)
    onehot = (flat_ids[:, None] == jnp.arange(experts, dtype=jnp.int32)[None, :]).astype(jnp.int32)
    ranks = jnp.sum(jnp.cumsum(onehot, axis=0) * onehot, axis=1) - 1
    target = flat_ids * slots + ranks
    token_rows = jnp.repeat(tokens, top, axis=0)
    outbound = jnp.zeros((experts * slots, width), tokens.dtype).at[target].set(token_rows)
    outbound = outbound.reshape(experts, slots, width)
    gate_mat = w_gate[0]
    up_mat = w_up[0]
    down_mat = w_down[0]
    hidden_width = gate_mat.shape[1]
    arrived = lax.all_to_all(outbound, "expert", split_axis=0, concat_axis=0, tiled=True)
    sources = arrived.shape[0]
    count = arrived.shape[1]
    rows = arrived.reshape(-1, width)
    gate_pre = jnp.dot(rows, gate_mat, preferred_element_type=jnp.float32)
    up_pre = jnp.dot(rows, up_mat, preferred_element_type=jnp.float32)
    hidden = (gate_pre * jax.nn.sigmoid(gate_pre) * up_pre).astype(jnp.bfloat16)
    result = jnp.dot(hidden, down_mat, preferred_element_type=jnp.float32).astype(jnp.bfloat16)
    expert_out, hidden, gate_pre, up_pre, arrived = (
        result.reshape(sources, count, width),
        hidden.reshape(sources, count, hidden_width),
        gate_pre.reshape(sources, count, hidden_width),
        up_pre.reshape(sources, count, hidden_width),
        arrived,
    )
    returned = lax.all_to_all(expert_out, "expert", split_axis=0, concat_axis=0, tiled=True)
    picked = returned.reshape(-1, width)[target].reshape(tok_count, top, width)
    layer_out = jnp.sum(gate_probs[:, :, None] * picked.astype(jnp.float32), axis=1).astype(
        jnp.bfloat16
    )
    out_grad = (gate_probs[:, :, None] * out_cot[:, None, :].astype(jnp.float32)).astype(
        jnp.bfloat16
    )
    outbound_grad = (
        jnp.zeros((experts * slots, width), tokens.dtype)
        .at[target]
        .set(out_grad.reshape(-1, width))
    )
    arrived_grad = lax.all_to_all(
        outbound_grad.reshape(experts, slots, width),
        "expert",
        split_axis=0,
        concat_axis=0,
        tiled=True,
    ).reshape(-1, width)
    x_rows = arrived.reshape(-1, width)
    hidden_rows = hidden.reshape(-1, hidden_width)
    gate_rows = gate_pre.reshape(-1, hidden_width)
    up_rows = up_pre.reshape(-1, hidden_width)
    hidden_grad = contract_cols(arrived_grad, down_mat)
    sigma = jax.nn.sigmoid(gate_rows)
    gate_grad = (hidden_grad * up_rows * sigma * (1.0 + gate_rows * (1.0 - sigma))).astype(
        jnp.bfloat16
    )
    up_grad = (hidden_grad * gate_rows * sigma).astype(jnp.bfloat16)
    row_grad = (contract_cols(gate_grad, gate_mat) + contract_cols(up_grad, up_mat)).astype(
        jnp.bfloat16
    )
    back_grad = lax.all_to_all(
        row_grad.reshape(experts, slots, width), "expert", split_axis=0, concat_axis=0, tiled=True
    )
    gathered = back_grad.reshape(-1, width)[target].reshape(tok_count, top, width)
    input_grad = jnp.sum(gathered.astype(jnp.float32), axis=1).astype(jnp.bfloat16)
    down_grad = lax.psum_scatter(
        contract_rows(hidden_rows, arrived_grad).astype(jnp.bfloat16),
        "dp",
        scatter_dimension=0,
        tiled=True,
    ).astype(jnp.float32)
    gate_part = lax.psum_scatter(
        contract_rows(x_rows, gate_grad).astype(jnp.bfloat16), "dp", scatter_dimension=0, tiled=True
    ).astype(jnp.float32)
    up_part = lax.psum_scatter(
        contract_rows(x_rows, up_grad).astype(jnp.bfloat16), "dp", scatter_dimension=0, tiled=True
    ).astype(jnp.float32)
    return (layer_out, input_grad, gate_part[None], up_part[None], down_grad[None])


BF16, F32 = jnp.bfloat16, jnp.float32
VMEM, SMEM, HBM, ANY = pltpu.VMEM, pltpu.SMEM, pltpu.HBM, pl.ANY
PINNED = "pinned"
ORDER = ((8, 128), jnp.float32, pltpu.VMEM)


def stage(body, ins, outs, after=(), scratch=(), aliases=None, vmem=8):
    skipped = len(after)
    given = skipped + len(ins)

    def kernel(*refs):
        token = refs[given + len(outs)]
        body(*refs[skipped : given + len(outs)], *refs[given + len(outs) + 1 :])
        token[...] = jnp.zeros(token.shape, token.dtype)

    outs_all = [(shape, dtype, VMEM if m == PINNED else m) for shape, dtype, m in outs] + [ORDER]
    shapes = [
        pltpu.VMEM(shape, dtype) if m == PINNED else jax.ShapeDtypeStruct(shape, dtype)
        for shape, dtype, m in [*outs, ORDER]
    ]
    fixed = {HBM: HBM, PINNED: VMEM}
    outputs = pl.pallas_call(
        kernel,
        in_specs=[
            pl.BlockSpec(memory_space=VMEM if m == PINNED else m)
            for m in [ANY] * skipped + [m for _, m in ins]
        ],
        out_specs=[pl.BlockSpec(memory_space=m) for _, _, m in outs_all],
        out_shape=shapes,
        scratch_shapes=list(scratch),
        input_output_aliases={skipped + i: o for i, o in (aliases or {}).items()},
        cost_estimate=pl.CostEstimate(flops=0, bytes_accessed=0, transcendentals=0),
        compiler_params=pltpu.CompilerParams(vmem_limit_bytes=vmem * 2**20),
    )(*after, *[pltpu.with_memory_space_constraint(a, fixed[m]) if m in fixed else a for a, m in ins])
    return list(outputs)


def swap(value, axis, mask):
    size = lax.axis_size(axis)
    return lax.ppermute(value, axis, [(i, i ^ mask) for i in range(size)])


def chunks(width, most):
    return [(at, min(most, width - at)) for at in range(0, width, most)]


def packed(tokens, expert_ids, gate_probs, out_cot, experts, lanes):
    count, width = tokens.shape
    top = expert_ids.shape[1]

    def body(tok, ids_far, given_far, cot, alone, both, ids, given, sems):
        copies = [
            pltpu.make_async_copy(tok, alone.at[:, :width], sems.at[0]),
            pltpu.make_async_copy(tok, both.at[:count, :width], sems.at[1]),
            pltpu.make_async_copy(cot, both.at[count:, :width], sems.at[2]),
        ]
        small = [
            pltpu.make_async_copy(ids_far, ids, sems.at[3]),
            pltpu.make_async_copy(given_far, given, sems.at[4]),
        ]
        for copy in small + copies:
            copy.start()
        for copy in small:
            copy.wait()
        names = ids[...].T
        values = given[...].T
        column = lax.broadcasted_iota(jnp.int32, (count, lanes), 1)
        total = jnp.zeros((count, lanes), F32)
        for k in range(top):
            named = (names[:, k : k + 1] == column) | (names[:, k : k + 1] + experts == column)
            total = total + jnp.where(named, values[:, k : k + 1], 0.0)
        high = total.astype(BF16).astype(F32)
        side = jnp.where(column < experts, high, total - high).astype(BF16)
        alone[:, width:] = side
        both[:count, width:] = side
        both[count:, width:] = jnp.zeros((count, lanes), BF16)
        for copy in copies:
            copy.wait()

    return stage(
        body,
        [(a, HBM) for a in (tokens, expert_ids.T, gate_probs.T, out_cot)],
        [((count, width + lanes), BF16, VMEM), ((2 * count, width + lanes), BF16, VMEM)],
        scratch=[
            VMEM((top, count), jnp.int32),
            VMEM((top, count), F32),
            pltpu.SemaphoreType.DMA((5,)),
        ],
            )


def products(places, left, right, outs, own, tile=512):
    size = left.shape[0] // 4
    width = right.shape[1]
    for start, some in chunks(width, tile):
        piece = right[:, start : start + some]
        for m, (out, row) in zip(places, outs):
            part = left[pl.ds(pl.multiple_of((own ^ m) * size, size), size), :]
            out[row : row + size, start : start + some] = jnp.dot(
                part, piece, preferred_element_type=F32
            ).astype(out.dtype)


TURNED = (((1,), (1,)), ((), ()))


def dense(tokens, expert_ids, gate_probs, out_cot, w_gate, w_up, w_down):
    count, width = tokens.shape
    ff = w_gate.shape[2]
    experts = lax.axis_size("expert")
    owners = lax.axis_size("dp")
    me = lax.axis_index("expert").astype(jnp.int32).reshape(1)
    mine = lax.axis_index("dp").astype(jnp.int32).reshape(1)
    total = count * experts
    half = total // 2
    pair = half // 2
    lanes = 128 * (-(-2 * experts // 128))
    odd_places, even_places = [3, 1], [2, 0]
    slab, band = ff // owners, width // owners

    near_bit, far_bit = 2, 4
    wide = width + lanes
    tok_own, both, done = packed(tokens, expert_ids, gate_probs, out_cot, experts, lanes)
    tok_far = swap(tok_own, "expert", far_bit)
    tok_near = swap(tok_own, "expert", near_bit)
    next_both = swap(both, "expert", 1)
    def copied(sources, width, after, waits=()):
        rows = count * len(sources)

        def body(*refs):
            out = refs[-1]
            for i, (_, row) in enumerate(sources):
                out[i * count : (i + 1) * count, :] = refs[i][row : row + count, :width]

        return stage(
            body,
            [(a, VMEM) for a, _ in sources] + [(a, ANY) for a in waits],
            [((rows, width), BF16, VMEM)],
            after=after,
        )

    tok_pair, done = copied([(tok_near, 0), (tok_far, 0)], wide, [done], [next_both])
    cot_own, done = copied([(both, count)], width, [done])
    tok_far_on, done = copied([(tok_far, 0)], wide, [done])
    next_tok_pair = swap(tok_pair, "expert", 1)
    tok_last = swap(tok_far_on, "expert", near_bit)
    cot_far = swap(cot_own, "expert", far_bit)
    cot_near = swap(cot_own, "expert", near_bit)
    tok_last_on, done = copied([(tok_last, 0)], wide, [done])
    next_tok_last = swap(tok_last_on, "expert", 1)
    cot_pair, done = copied([(cot_near, 0), (cot_far, 0)], width, [done])
    cot_far_on, done = copied([(cot_far, 0)], width, [done])
    next_cot_pair = swap(cot_pair, "expert", 1)
    cot_last = swap(cot_far_on, "expert", near_bit)
    tok_pieces = [(tok_own, 0), (tok_pair, count), (tok_pair, 0), (tok_last_on, 0)]
    tok_pieces += [(next_both, 0), (next_tok_pair, count), (next_tok_pair, 0), (next_tok_last, 0)]

    def refs_of(pieces):
        arrays = []
        for a, _ in pieces:
            if not any(a is b for b in arrays):
                arrays.append(a)
        where = [next(i for i, b in enumerate(arrays) if b is a) for a, _ in pieces]
        return arrays, [(i, row) for i, (_, row) in zip(where, pieces)]

    tok_arrays, tok_where = refs_of(tok_pieces)

    cot_last_on, done = copied([(cot_last, 0)], width, [done], [next_tok_last])
    next_cot_last = swap(cot_last_on, "expert", 1)
    cot_pieces = [(cot_own, 0), (cot_pair, count), (cot_pair, 0), (cot_last_on, 0)]
    cot_pieces += [(next_both, count), (next_cot_pair, count), (next_cot_pair, 0), (next_cot_last, 0)]
    def forward(me_ref, mine_ref, *refs):
        blocks = refs[: len(tok_arrays)]
        weights = refs[len(tok_arrays) : len(tok_arrays) + 3]
        flipped, flipped_sent, hidden_t, gate_by, up_by, kept, sent, gate, up, down = refs[
            len(tok_arrays) + 3 : len(tok_arrays) + 13
        ]
        rows, probs, hidden, sems = refs[len(tok_arrays) + 13 :]
        steps = chunks(ff, 256)
        copies = []
        for i, (start, size) in enumerate(steps):
            place = slice(start, start + size)
            for j, (far_ref, near_ref) in enumerate([(weights[0], gate), (weights[1], up)]):
                copies.append(
                    pltpu.make_async_copy(far_ref.at[:, place], near_ref.at[:, place], sems.at[2 * i + j])
                )
        copies.append(pltpu.make_async_copy(weights[2], down, sems.at[2 * len(steps)]))
        for copy in copies:
            copy.start()
        own = me_ref[0]
        column = lax.broadcasted_iota(jnp.int32, (count, lanes), 1)
        chosen = (column == own) | (column == own + experts)
        for b, (i, row) in enumerate(tok_where):
            place = pl.ds(b * count, count)
            rows[place, :] = blocks[i][row : row + count, :width]
            side = jnp.where(chosen, blocks[i][row : row + count, width:].astype(F32), 0.0)
            probs[place, :] = jnp.sum(side, axis=1, keepdims=True)
        weight = probs[...]
        for out, places in ((flipped, even_places), (flipped_sent, odd_places)):
            for i, m in enumerate(places):
                start = pl.multiple_of((mine_ref[0] ^ m) * band, band)
                out[i * band : (i + 1) * band, :] = rows[:, pl.ds(start, band)].T
        for i, (start, size) in enumerate(steps):
            place = slice(start, start + size)
            copies[2 * i].wait()
            gate_pre = jnp.dot(rows[...], gate[:, place], preferred_element_type=F32)
            copies[2 * i + 1].wait()
            up_pre = jnp.dot(rows[...], up[:, place], preferred_element_type=F32)
            sigma = jax.nn.sigmoid(gate_pre)
            silu = gate_pre * sigma
            scaled = weight * up_pre
            hidden[:, place] = (silu * scaled).astype(BF16)
            gate_by[:, place] = scaled * sigma * (1.0 + gate_pre * (1.0 - sigma))
            up_by[:, place] = weight * silu
            hidden_t[place, :] = hidden[:, place].T
        copies[-1].wait()
        for start, size in chunks(width, 512):
            place = slice(start, start + size)
            part = jnp.dot(hidden[...], down[:, place], preferred_element_type=F32).astype(BF16)
            kept[:, place] = part[:half]
            sent[:, place] = part[half:]

    (
        flipped, flipped_sent, hidden_t, gate_by, up_by, out_kept, out_sent,
        gate_near, up_near, down_near, done,
    ) = stage(
        forward,
        [(me, SMEM), (mine, SMEM)] + [(a, VMEM) for a in tok_arrays] + [(w[0], HBM) for w in (w_gate, w_up, w_down)],
        [
            ((width // 2, total), BF16, VMEM),
            ((width // 2, total), BF16, VMEM),
            ((ff, total), BF16, VMEM),
            ((total, ff), F32, VMEM),
            ((total, ff), F32, VMEM),
            ((half, width), BF16, VMEM),
            ((half, width), BF16, VMEM),
            ((width, ff), BF16, VMEM),
            ((width, ff), BF16, VMEM),
            ((ff, width), BF16, VMEM),
        ],
        scratch=[
            VMEM((total, width), BF16),
            VMEM((total, 1), F32),
            VMEM((total, ff), BF16),
            pltpu.SemaphoreType.DMA((2 * len(chunks(ff, 256)) + 1,)),
        ],
        after=[done],
        vmem=8,
    )

    cot_arrays, cot_where = refs_of(cot_pieces)

    def down_first(own_ref, *refs):
        blocks = refs[: len(cot_arrays)]
        left, _, rows, away, _ = refs[len(cot_arrays) :]
        for b, (i, row) in enumerate(cot_where):
            rows[b * count : (b + 1) * count, :] = blocks[i][row : row + count, :width]
        products([3], left, rows, [(away, 0)], own_ref[0])

    cot_rows, down_away, flipped_sent, done = stage(
        down_first,
        [(mine, SMEM)] + [(a, VMEM) for a in [*cot_arrays, hidden_t]] + [(flipped_sent, ANY)],
        [
            ((total, width), BF16, VMEM),
            ((slab, width), BF16, VMEM),
            (flipped_sent.shape, BF16, ANY),
        ],
        after=[done],
        aliases={len(cot_arrays) + 2: 2},
    )
    down_came = swap(down_away, "dp", 1)
    flipped_came = swap(flipped_sent, "dp", 1)

    def down_rest(own_ref, left, cot, away, send, kept):
        products([1, 2, 0], left, cot, [(away, 0), (send, 0), (kept, 0)], own_ref[0])

    last_away, down_send, down_kept, done = stage(
        down_rest,
        [(mine, SMEM), (hidden_t, VMEM), (cot_rows, VMEM)],
        [((slab, width), BF16, VMEM)] * 3,
        after=[done],
    )
    last_came = swap(last_away, "dp", 1)
    out_came = swap(out_sent, "expert", 1)

    def backward(cot, down, gate_ref, up_ref, grads):
        for start, size in chunks(ff, 256):
            place = slice(start, start + size)
            grad = lax.dot_general(cot[...], down[place, :], TURNED, preferred_element_type=F32)
            grads[:, place] = (grad * gate_ref[:, place]).astype(BF16)
            grads[:, ff + start : ff + start + size] = (grad * up_ref[:, place]).astype(BF16)

    grads, done = stage(
        backward,
        [(a, VMEM) for a in (cot_rows, down_near, gate_by, up_by)],
        [((total, 2 * ff), BF16, VMEM)],
        after=[done],
    )
    grads_came = swap(grads, "dp", 1)

    def added(kept, came, _, send):
        send[...] = (kept[...].astype(F32) + came[...].astype(F32)).astype(BF16)

    down_send, done = stage(
        added,
        [(down_send, VMEM), (down_came, VMEM), (flipped_came, ANY)],
        [((slab, width), BF16, VMEM)],
        after=[done],
    )
    down_got = swap(down_send, "dp", 2)

    def input_rows(grad, gate, up, kept, sent):
        for start, size in chunks(width, 512):
            place = slice(start, start + size)
            rows = lax.dot_general(grad[:, :ff], gate[place, :], TURNED, preferred_element_type=F32)
            rows = rows + lax.dot_general(
                grad[:, ff:], up[place, :], TURNED, preferred_element_type=F32
            )
            rows = rows.astype(BF16)
            for i in range(2):
                low, high = slice(i * pair, (i + 1) * pair), i * half
                kept[low, place] = rows[high : high + pair]
                sent[low, place] = rows[high + pair : high + half]

    in_kept, in_sent, done = stage(
        input_rows,
        [(grads, VMEM), (gate_near, VMEM), (up_near, VMEM)],
        [((half, width), BF16, VMEM)] * 2,
        after=[done],
    )
    in_came = swap(in_sent, "expert", near_bit)

    def both_parts(left, left_came, grad, grad_came, _, gate_send, up_high, up_low, gate_kept, up_kept):
        for j, (gate_out, up_out) in enumerate([(gate_send, None), (gate_kept, up_kept)]):
            row = slice(j * band, (j + 1) * band)
            for start, size in chunks(2 * ff, 256):
                column = slice(start, start + size)
                value = jnp.dot(left[row, :], grad[:, column], preferred_element_type=F32)
                value += jnp.dot(left_came[row, :], grad_came[:, column], preferred_element_type=F32)
                place = slice(start % ff, start % ff + size)
                if start < ff:
                    gate_out[:, place] = value.astype(gate_out.dtype)
                elif up_out is not None:
                    up_out[:, place] = value.astype(up_out.dtype)
                else:
                    up_high[:, place] = value[: band // 2].astype(BF16)
                    up_low[:, place] = value[band // 2 :].astype(BF16)

    gate_send, up_high, up_low, gate_kept, up_kept, done = stage(
        both_parts,
        [(a, VMEM) for a in (flipped, flipped_came, grads, grads_came)] + [(last_came, ANY)],
        [((band, ff), BF16, VMEM)]
        + [((band // 2, ff), BF16, VMEM)] * 2
        + [((band, ff), F32, VMEM)] * 2,
        after=[done],
    )
    gate_got = swap(gate_send, "dp", 2)
    up_got = [swap(a, "dp", 2) for a in (up_high, up_low)]

    def folded(held, came, after, waits=()):
        rows = held.shape[0]
        parts = 1 if rows == count else 2

        def body(a, b, *refs):
            for i, out in enumerate(refs[len(waits) :]):
                place = slice(i * rows // parts, (i + 1) * rows // parts)
                out[...] = (a[place, :].astype(F32) + b[place, :].astype(F32)).astype(BF16)

        return stage(
            body,
            [(held, VMEM), (came, VMEM)] + [(a, ANY) for a in waits],
            [((rows // parts, width), BF16, VMEM)] * parts,
            after=after,
        )

    def owned(parts, after):
        size = sum(a.shape[0] for a in parts[0])
        wide = parts[0][0].shape[1]
        step = size // 4
        where = []
        for arrays in parts:
            first = len([i for w in where for i in w])
            where.append(range(first, first + len(arrays)))

        def body(*refs):
            ins, (out, total, sems) = refs[:-3], refs[-3:]
            copies = []
            for i in range(4):
                at = slice(i * step, (i + 1) * step)
                value = jnp.zeros((step, wide), F32)
                for places in where:
                    each = size // len(places)
                    ref, row = ins[places[i * step // each]], i * step % each
                    value = value + ref[row : row + step, :].astype(F32)
                total[at, :] = value
                copies.append(pltpu.make_async_copy(total.at[at], out.at[at], sems.at[i]))
                copies[-1].start()
            for copy in copies:
                copy.wait()

        return stage(
            body,
            [(a, VMEM) for arrays in parts for a in arrays],
            [((size, wide), F32, HBM)],
            scratch=[VMEM((size, wide), F32), pltpu.SemaphoreType.DMA((4,))],
            after=after,
        )

    def fold_on(held, came, bit, after, waits=()):
        held, send, done = folded(held, came, after, waits)
        return held, swap(send, "expert", bit), done

    out_held, out_came, done = fold_on(out_kept, out_came, near_bit, [done])
    down_grad, done = owned([[down_kept], [last_came], [down_got]], [done])
    in_held, in_came, done = fold_on(in_kept, in_came, 1, [done])
    out_held, out_came, done = fold_on(out_held, out_came, far_bit, [done])
    in_held, in_came, done = fold_on(in_held, in_came, far_bit, [done])
    layer_out, done = folded(out_held, out_came, [done])
    gate_part, done = owned([[gate_kept], [gate_got]], [done])
    input_grad, done = folded(in_held, in_came, [done])
    up_part, _ = owned([[up_kept], up_got], [done])
    return (layer_out, input_grad, gate_part[None], up_part[None], down_grad[None])


def shards(tokens, expert_ids, *rest):
    experts = lax.axis_size("expert")
    every = expert_ids.shape[1] == experts and experts == 8 and lax.axis_size("dp") == 4
    return (dense if every else routed)(tokens, expert_ids, *rest)


def solution(mesh):
    placed = (
        P(("dp", "expert"), None),
        P(("dp", "expert"), None),
        P(("dp", "expert"), None),
        P(("dp", "expert"), None),
        P("expert", None, None),
        P("expert", None, None),
        P("expert", None, None),
    )
    return jax.shard_map(
        shards,
        mesh=mesh,
        in_specs=placed,
        out_specs=(
            P(("dp", "expert"), None),
            P(("dp", "expert"), None),
            P("expert", "dp", None),
            P("expert", "dp", None),
            P("expert", "dp", None),
        ),
        check_vma=False,
    )
```

```python
import jax
import jax.numpy as jnp
from jax import lax
from jax.experimental import pallas as pl
from jax.experimental.pallas import tpu as pltpu
from jax.sharding import PartitionSpec as P


def contract_rows(left, right):
    return lax.dot_general(
        left, right, (((0,), (0,)), ((), ())), preferred_element_type=jnp.float32
    )


def contract_cols(left, right):
    return lax.dot_general(
        left, right, (((1,), (1,)), ((), ())), preferred_element_type=jnp.float32
    )


def routed(tokens, expert_ids, gate_probs, out_cot, w_gate, w_up, w_down):
    tok_count, width = tokens.shape
    top = expert_ids.shape[1]
    experts = lax.axis_size("expert")
    slots = min(tok_count, 4 * tok_count * top // (3 * experts))
    flat_ids = expert_ids.reshape(-1)
    onehot = (flat_ids[:, None] == jnp.arange(experts, dtype=jnp.int32)[None, :]).astype(jnp.int32)
    ranks = jnp.sum(jnp.cumsum(onehot, axis=0) * onehot, axis=1) - 1
    target = flat_ids * slots + ranks
    token_rows = jnp.repeat(tokens, top, axis=0)
    outbound = jnp.zeros((experts * slots, width), tokens.dtype).at[target].set(token_rows)
    outbound = outbound.reshape(experts, slots, width)
    gate_mat = w_gate[0]
    up_mat = w_up[0]
    down_mat = w_down[0]
    hidden_width = gate_mat.shape[1]
    arrived = lax.all_to_all(outbound, "expert", split_axis=0, concat_axis=0, tiled=True)
    sources = arrived.shape[0]
    count = arrived.shape[1]
    rows = arrived.reshape(-1, width)
    gate_pre = jnp.dot(rows, gate_mat, preferred_element_type=jnp.float32)
    up_pre = jnp.dot(rows, up_mat, preferred_element_type=jnp.float32)
    hidden = (gate_pre * jax.nn.sigmoid(gate_pre) * up_pre).astype(jnp.bfloat16)
    result = jnp.dot(hidden, down_mat, preferred_element_type=jnp.float32).astype(jnp.bfloat16)
    expert_out, hidden, gate_pre, up_pre, arrived = (
        result.reshape(sources, count, width),
        hidden.reshape(sources, count, hidden_width),
        gate_pre.reshape(sources, count, hidden_width),
        up_pre.reshape(sources, count, hidden_width),
        arrived,
    )
    returned = lax.all_to_all(expert_out, "expert", split_axis=0, concat_axis=0, tiled=True)
    picked = returned.reshape(-1, width)[target].reshape(tok_count, top, width)
    layer_out = jnp.sum(gate_probs[:, :, None] * picked.astype(jnp.float32), axis=1).astype(
        jnp.bfloat16
    )
    out_grad = (gate_probs[:, :, None] * out_cot[:, None, :].astype(jnp.float32)).astype(
        jnp.bfloat16
    )
    outbound_grad = (
        jnp.zeros((experts * slots, width), tokens.dtype)
        .at[target]
        .set(out_grad.reshape(-1, width))
    )
    arrived_grad = lax.all_to_all(
        outbound_grad.reshape(experts, slots, width),
        "expert",
        split_axis=0,
        concat_axis=0,
        tiled=True,
    ).reshape(-1, width)
    x_rows = arrived.reshape(-1, width)
    hidden_rows = hidden.reshape(-1, hidden_width)
    gate_rows = gate_pre.reshape(-1, hidden_width)
    up_rows = up_pre.reshape(-1, hidden_width)
    hidden_grad = contract_cols(arrived_grad, down_mat)
    sigma = jax.nn.sigmoid(gate_rows)
    gate_grad = (hidden_grad * up_rows * sigma * (1.0 + gate_rows * (1.0 - sigma))).astype(
        jnp.bfloat16
    )
    up_grad = (hidden_grad * gate_rows * sigma).astype(jnp.bfloat16)
    row_grad = (contract_cols(gate_grad, gate_mat) + contract_cols(up_grad, up_mat)).astype(
        jnp.bfloat16
    )
    back_grad = lax.all_to_all(
        row_grad.reshape(experts, slots, width), "expert", split_axis=0, concat_axis=0, tiled=True
    )
    gathered = back_grad.reshape(-1, width)[target].reshape(tok_count, top, width)
    input_grad = jnp.sum(gathered.astype(jnp.float32), axis=1).astype(jnp.bfloat16)
    down_grad = lax.psum_scatter(
        contract_rows(hidden_rows, arrived_grad).astype(jnp.bfloat16),
        "dp",
        scatter_dimension=0,
        tiled=True,
    ).astype(jnp.float32)
    gate_part = lax.psum_scatter(
        contract_rows(x_rows, gate_grad).astype(jnp.bfloat16), "dp", scatter_dimension=0, tiled=True
    ).astype(jnp.float32)
    up_part = lax.psum_scatter(
        contract_rows(x_rows, up_grad).astype(jnp.bfloat16), "dp", scatter_dimension=0, tiled=True
    ).astype(jnp.float32)
    return (layer_out, input_grad, gate_part[None], up_part[None], down_grad[None])


BF16, F32 = jnp.bfloat16, jnp.float32
VMEM, SMEM, HBM, ANY = pltpu.VMEM, pltpu.SMEM, pltpu.HBM, pl.ANY
PINNED = "pinned"
ORDER = ((8, 128), jnp.float32, pltpu.VMEM)


def stage(body, ins, outs, after=(), scratch=(), aliases=None, vmem=8):
    skipped = len(after)
    given = skipped + len(ins)

    def kernel(*refs):
        token = refs[given + len(outs)]
        body(*refs[skipped : given + len(outs)], *refs[given + len(outs) + 1 :])
        token[...] = jnp.zeros(token.shape, token.dtype)

    outs_all = [(shape, dtype, VMEM if m == PINNED else m) for shape, dtype, m in outs] + [ORDER]
    shapes = [
        pltpu.VMEM(shape, dtype) if m == PINNED else jax.ShapeDtypeStruct(shape, dtype)
        for shape, dtype, m in [*outs, ORDER]
    ]
    fixed = {HBM: HBM, PINNED: VMEM}
    outputs = pl.pallas_call(
        kernel,
        in_specs=[
            pl.BlockSpec(memory_space=VMEM if m == PINNED else m)
            for m in [ANY] * skipped + [m for _, m in ins]
        ],
        out_specs=[pl.BlockSpec(memory_space=m) for _, _, m in outs_all],
        out_shape=shapes,
        scratch_shapes=list(scratch),
        input_output_aliases={skipped + i: o for i, o in (aliases or {}).items()},
        cost_estimate=pl.CostEstimate(flops=0, bytes_accessed=0, transcendentals=0),
        compiler_params=pltpu.CompilerParams(vmem_limit_bytes=vmem * 2**20),
    )(*after, *[pltpu.with_memory_space_constraint(a, fixed[m]) if m in fixed else a for a, m in ins])
    return list(outputs)


def swap(value, axis, mask):
    size = lax.axis_size(axis)
    return lax.ppermute(value, axis, [(i, i ^ mask) for i in range(size)])


def chunks(width, most):
    return [(at, min(most, width - at)) for at in range(0, width, most)]


def packed(tokens, expert_ids, gate_probs, out_cot, experts, lanes):
    count, width = tokens.shape
    top = expert_ids.shape[1]

    def body(tok, ids_far, given_far, cot, alone, both, ids, given, sems):
        copies = [
            pltpu.make_async_copy(tok, alone.at[:, :width], sems.at[0]),
            pltpu.make_async_copy(tok, both.at[:count, :width], sems.at[1]),
            pltpu.make_async_copy(cot, both.at[count:, :width], sems.at[2]),
        ]
        small = [
            pltpu.make_async_copy(ids_far, ids, sems.at[3]),
            pltpu.make_async_copy(given_far, given, sems.at[4]),
        ]
        for copy in small + copies:
            copy.start()
        for copy in small:
            copy.wait()
        names = ids[...].T
        values = given[...].T
        column = lax.broadcasted_iota(jnp.int32, (count, lanes), 1)
        total = jnp.zeros((count, lanes), F32)
        for k in range(top):
            named = (names[:, k : k + 1] == column) | (names[:, k : k + 1] + experts == column)
            total = total + jnp.where(named, values[:, k : k + 1], 0.0)
        high = total.astype(BF16).astype(F32)
        side = jnp.where(column < experts, high, total - high).astype(BF16)
        alone[:, width:] = side
        both[:count, width:] = side
        both[count:, width:] = jnp.zeros((count, lanes), BF16)
        for copy in copies:
            copy.wait()

    return stage(
        body,
        [(a, HBM) for a in (tokens, expert_ids.T, gate_probs.T, out_cot)],
        [((count, width + lanes), BF16, VMEM), ((2 * count, width + lanes), BF16, VMEM)],
        scratch=[
            VMEM((top, count), jnp.int32),
            VMEM((top, count), F32),
            pltpu.SemaphoreType.DMA((5,)),
        ],
            )


def products(places, left, right, outs, own, tile=512):
    size = left.shape[0] // 4
    width = right.shape[1]
    for start, some in chunks(width, tile):
        piece = right[:, start : start + some]
        for m, (out, row) in zip(places, outs):
            part = left[pl.ds(pl.multiple_of((own ^ m) * size, size), size), :]
            out[row : row + size, start : start + some] = jnp.dot(
                part, piece, preferred_element_type=F32
            ).astype(out.dtype)


TURNED = (((1,), (1,)), ((), ()))


def dense(tokens, expert_ids, gate_probs, out_cot, w_gate, w_up, w_down):
    count, width = tokens.shape
    ff = w_gate.shape[2]
    experts = lax.axis_size("expert")
    owners = lax.axis_size("dp")
    me = lax.axis_index("expert").astype(jnp.int32).reshape(1)
    mine = lax.axis_index("dp").astype(jnp.int32).reshape(1)
    total = count * experts
    half = total // 2
    pair = half // 2
    lanes = 128 * (-(-2 * experts // 128))
    odd_places, even_places = [3, 1], [2, 0]
    slab, band = ff // owners, width // owners

    near_bit, far_bit = 2, 4
    wide = width + lanes
    tok_own, both, done = packed(tokens, expert_ids, gate_probs, out_cot, experts, lanes)
    tok_far = swap(tok_own, "expert", far_bit)
    tok_near = swap(tok_own, "expert", near_bit)
    next_both = swap(both, "expert", 1)
    def copied(sources, width, after, waits=()):
        rows = count * len(sources)

        def body(*refs):
            out = refs[-1]
            for i, (_, row) in enumerate(sources):
                out[i * count : (i + 1) * count, :] = refs[i][row : row + count, :width]

        return stage(
            body,
            [(a, VMEM) for a, _ in sources] + [(a, ANY) for a in waits],
            [((rows, width), BF16, VMEM)],
            after=after,
        )

    tok_pair, done = copied([(tok_near, 0), (tok_far, 0)], wide, [done], [next_both])
    cot_own, done = copied([(both, count)], width, [done])
    tok_far_on, done = copied([(tok_far, 0)], wide, [done])
    next_tok_pair = swap(tok_pair, "expert", 1)
    tok_last = swap(tok_far_on, "expert", near_bit)
    cot_far = swap(cot_own, "expert", far_bit)
    cot_near = swap(cot_own, "expert", near_bit)
    tok_last_on, done = copied([(tok_last, 0)], wide, [done])
    next_tok_last = swap(tok_last_on, "expert", 1)
    cot_pair, done = copied([(cot_near, 0), (cot_far, 0)], width, [done], [next_tok_pair])
    cot_far_on, done = copied([(cot_far, 0)], width, [done])
    next_cot_pair = swap(cot_pair, "expert", 1)
    cot_last = swap(cot_far_on, "expert", near_bit)
    tok_pieces = [(tok_own, 0), (tok_pair, count), (tok_pair, 0), (tok_last_on, 0)]
    tok_pieces += [(next_both, 0), (next_tok_pair, count), (next_tok_pair, 0), (next_tok_last, 0)]

    def refs_of(pieces):
        arrays = []
        for a, _ in pieces:
            if not any(a is b for b in arrays):
                arrays.append(a)
        where = [next(i for i, b in enumerate(arrays) if b is a) for a, _ in pieces]
        return arrays, [(i, row) for i, (_, row) in zip(where, pieces)]

    tok_arrays, tok_where = refs_of(tok_pieces)

    cot_last_on, done = copied([(cot_last, 0)], width, [done], [next_tok_last])
    next_cot_last = swap(cot_last_on, "expert", 1)
    cot_pieces = [(cot_own, 0), (cot_pair, count), (cot_pair, 0), (cot_last_on, 0)]
    cot_pieces += [(next_both, count), (next_cot_pair, count), (next_cot_pair, 0), (next_cot_last, 0)]
    def forward(me_ref, mine_ref, *refs):
        blocks = refs[: len(tok_arrays)]
        weights = refs[len(tok_arrays) : len(tok_arrays) + 3]
        flipped, flipped_sent, hidden_t, gate_by, up_by, kept, sent, gate, up, down = refs[
            len(tok_arrays) + 3 : len(tok_arrays) + 13
        ]
        rows, probs, hidden, gates, sems = refs[len(tok_arrays) + 13 :]
        copies = []
        for j, (far_ref, near_ref) in enumerate(zip(weights, (gate, up, down))):
            size = far_ref.shape[0] // 4
            for i in range(4):
                place = slice(i * size, (i + 1) * size)
                copies.append(
                    pltpu.make_async_copy(far_ref.at[place], near_ref.at[place], sems.at[4 * j + i])
                )
        for copy in copies:
            copy.start()
        own = me_ref[0]
        column = lax.broadcasted_iota(jnp.int32, (count, lanes), 1)
        chosen = (column == own) | (column == own + experts)
        for b, (i, row) in enumerate(tok_where):
            place = pl.ds(b * count, count)
            rows[place, :] = blocks[i][row : row + count, :width]
            side = jnp.where(chosen, blocks[i][row : row + count, width:].astype(F32), 0.0)
            probs[place, :] = jnp.sum(side, axis=1, keepdims=True)
        weight = probs[...]
        for out, places in ((flipped, even_places), (flipped_sent, odd_places)):
            for i, m in enumerate(places):
                start = pl.multiple_of((mine_ref[0] ^ m) * band, band)
                out[i * band : (i + 1) * band, :] = rows[:, pl.ds(start, band)].T
        for copy in copies[:4]:
            copy.wait()
        for start, size in chunks(ff, 256):
            place = slice(start, start + size)
            gates[:, place] = jnp.dot(rows[...], gate[:, place], preferred_element_type=F32)
        for copy in copies[4:8]:
            copy.wait()
        for start, size in chunks(ff, 256):
            place = slice(start, start + size)
            gate_pre = gates[:, place]
            up_pre = jnp.dot(rows[...], up[:, place], preferred_element_type=F32)
            sigma = jax.nn.sigmoid(gate_pre)
            silu = gate_pre * sigma
            scaled = weight * up_pre
            hidden[:, place] = (silu * scaled).astype(BF16)
            gate_by[:, place] = scaled * sigma * (1.0 + gate_pre * (1.0 - sigma))
            up_by[:, place] = weight * silu
            hidden_t[place, :] = hidden[:, place].T
        for copy in copies[8:]:
            copy.wait()
        for start, size in chunks(width, 512):
            place = slice(start, start + size)
            part = jnp.dot(hidden[...], down[:, place], preferred_element_type=F32).astype(BF16)
            kept[:, place] = part[:half]
            sent[:, place] = part[half:]

    (
        flipped, flipped_sent, hidden_t, gate_by, up_by, out_kept, out_sent,
        gate_near, up_near, down_near, done,
    ) = stage(
        forward,
        [(me, SMEM), (mine, SMEM)] + [(a, VMEM) for a in tok_arrays] + [(w[0], HBM) for w in (w_gate, w_up, w_down)],
        [
            ((width // 2, total), BF16, VMEM),
            ((width // 2, total), BF16, VMEM),
            ((ff, total), BF16, VMEM),
            ((total, ff), F32, VMEM),
            ((total, ff), F32, VMEM),
            ((half, width), BF16, VMEM),
            ((half, width), BF16, VMEM),
            ((width, ff), BF16, VMEM),
            ((width, ff), BF16, VMEM),
            ((ff, width), BF16, VMEM),
        ],
        scratch=[
            VMEM((total, width), BF16),
            VMEM((total, 1), F32),
            VMEM((total, ff), BF16),
            VMEM((total, ff), F32),
            pltpu.SemaphoreType.DMA((12,)),
        ],
        after=[done],
        vmem=8,
    )

    cot_arrays, cot_where = refs_of(cot_pieces)

    def down_first(own_ref, *refs):
        blocks = refs[: len(cot_arrays)]
        left, rows, away = refs[len(cot_arrays) :]
        for b, (i, row) in enumerate(cot_where):
            rows[b * count : (b + 1) * count, :] = blocks[i][row : row + count, :width]
        products([3], left, rows, [(away, 0)], own_ref[0])

    cot_rows, down_away, done = stage(
        down_first,
        [(mine, SMEM)] + [(a, VMEM) for a in [*cot_arrays, hidden_t]],
        [((total, width), BF16, VMEM), ((slab, width), BF16, VMEM)],
        after=[done],
    )
    down_came = swap(down_away, "dp", 1)

    def down_rest(own_ref, left, cot, _, away, send, kept, same):
        products([1, 2, 0], left, cot, [(away, 0), (send, 0), (kept, 0)], own_ref[0])

    last_away, down_send, down_kept, flipped_sent, done = stage(
        down_rest,
        [(mine, SMEM), (hidden_t, VMEM), (cot_rows, VMEM), (flipped_sent, ANY)],
        [((slab, width), BF16, VMEM)] * 3 + [(flipped_sent.shape, BF16, ANY)],
        after=[done],
        aliases={3: 3},
    )
    flipped_came = swap(flipped_sent, "dp", 1)
    last_came = swap(last_away, "dp", 1)
    out_came = swap(out_sent, "expert", 1)

    def backward(cot, down, gate_ref, up_ref, grads):
        for start, size in chunks(ff, 256):
            place = slice(start, start + size)
            grad = lax.dot_general(cot[...], down[place, :], TURNED, preferred_element_type=F32)
            grads[:, place] = (grad * gate_ref[:, place]).astype(BF16)
            grads[:, ff + start : ff + start + size] = (grad * up_ref[:, place]).astype(BF16)

    grads, done = stage(
        backward,
        [(a, VMEM) for a in (cot_rows, down_near, gate_by, up_by)],
        [((total, 2 * ff), BF16, VMEM)],
        after=[done],
    )
    grads_came = swap(grads, "dp", 1)

    def added(kept, came, _, send):
        send[...] = (kept[...].astype(F32) + came[...].astype(F32)).astype(BF16)

    down_send, done = stage(
        added,
        [(down_send, VMEM), (down_came, VMEM), (flipped_came, ANY)],
        [((slab, width), BF16, VMEM)],
        after=[done],
    )
    down_got = swap(down_send, "dp", 2)

    def input_rows(grad, gate, up, kept, sent):
        for start, size in chunks(width, 512):
            place = slice(start, start + size)
            rows = lax.dot_general(grad[:, :ff], gate[place, :], TURNED, preferred_element_type=F32)
            rows = rows + lax.dot_general(
                grad[:, ff:], up[place, :], TURNED, preferred_element_type=F32
            )
            rows = rows.astype(BF16)
            for i in range(2):
                low, high = slice(i * pair, (i + 1) * pair), i * half
                kept[low, place] = rows[high : high + pair]
                sent[low, place] = rows[high + pair : high + half]

    in_kept, in_sent, done = stage(
        input_rows,
        [(grads, VMEM), (gate_near, VMEM), (up_near, VMEM)],
        [((half, width), BF16, VMEM)] * 2,
        after=[done],
    )
    in_came = swap(in_sent, "expert", near_bit)

    def both_parts(left, left_came, grad, grad_came, _, gate_send, up_high, up_low, gate_kept, up_kept):
        for j, (gate_out, up_out) in enumerate([(gate_send, None), (gate_kept, up_kept)]):
            row = slice(j * band, (j + 1) * band)
            for start, size in chunks(2 * ff, 256):
                column = slice(start, start + size)
                value = jnp.dot(left[row, :], grad[:, column], preferred_element_type=F32)
                value += jnp.dot(left_came[row, :], grad_came[:, column], preferred_element_type=F32)
                place = slice(start % ff, start % ff + size)
                if start < ff:
                    gate_out[:, place] = value.astype(gate_out.dtype)
                elif up_out is not None:
                    up_out[:, place] = value.astype(up_out.dtype)
                else:
                    up_high[:, place] = value[: band // 2].astype(BF16)
                    up_low[:, place] = value[band // 2 :].astype(BF16)

    gate_send, up_high, up_low, gate_kept, up_kept, done = stage(
        both_parts,
        [(a, VMEM) for a in (flipped, flipped_came, grads, grads_came)] + [(last_came, ANY)],
        [((band, ff), BF16, VMEM)]
        + [((band // 2, ff), BF16, VMEM)] * 2
        + [((band, ff), F32, VMEM)] * 2,
        after=[done],
    )
    gate_got = swap(gate_send, "dp", 2)
    high_got = swap(up_high, "dp", 2)

    def folded(held, came, after, waits=()):
        rows = held.shape[0]
        parts = 1 if rows == count else 2

        def body(a, b, *refs):
            for i, out in enumerate(refs[len(waits) :]):
                place = slice(i * rows // parts, (i + 1) * rows // parts)
                out[...] = (a[place, :].astype(F32) + b[place, :].astype(F32)).astype(BF16)

        return stage(
            body,
            [(held, VMEM), (came, VMEM)] + [(a, ANY) for a in waits],
            [((rows // parts, width), BF16, VMEM)] * parts,
            after=after,
        )

    def owned(parts, after, rows=None, into=None):
        size, wide = parts[-1].shape
        first = 0 if rows is None else rows
        full = parts[0].shape[0]
        step = size // 4
        n = len(parts)

        def body(*refs):
            out, total, sems = refs[-3:]
            copies = []
            for i in range(4):
                at = slice(i * step, (i + 1) * step)
                there = slice(first + i * step, first + (i + 1) * step)
                value = refs[0][there, :].astype(F32)
                for ref in refs[1:n]:
                    value = value + ref[at, :].astype(F32)
                total[at, :] = value
                copies.append(pltpu.make_async_copy(total.at[at], out.at[there], sems.at[i]))
                copies[-1].start()
            for copy in copies:
                copy.wait()

        return stage(
            body,
            [(a, VMEM) for a in parts] + ([] if into is None else [(into, HBM)]),
            [((full, wide), F32, HBM)],
            scratch=[VMEM((size, wide), F32), pltpu.SemaphoreType.DMA((4,))],
            after=after,
            aliases=None if into is None else {n: 0},
        )

    def fold_on(held, came, bit, after):
        held, send, done = folded(held, came, after)
        return held, swap(send, "expert", bit), done

    down_grad, done = owned([down_kept, last_came, down_got], [done])
    out_held, out_came, done = fold_on(out_kept, out_came, near_bit, [done])
    in_held, in_came, done = fold_on(in_kept, in_came, 1, [done])
    out_held, out_came, done = fold_on(out_held, out_came, far_bit, [done])
    up_low, done = stage(
        lambda *_: None, [(up_low, ANY)], [(up_low.shape, BF16, ANY)], after=[done], aliases={0: 0}
    )
    low_got = swap(up_low, "dp", 2)
    in_held, in_came, done = fold_on(in_held, in_came, far_bit, [done])
    gate_part, done = owned([gate_kept, gate_got], [done])
    up_part, done = owned([up_kept, high_got], [done])
    layer_out, done = folded(out_held, out_came, [done])
    input_grad, done = folded(in_held, in_came, [done])
    up_part, _ = owned([up_kept, low_got], [done], band // 2, up_part)
    return (layer_out, input_grad, gate_part[None], up_part[None], down_grad[None])


def shards(tokens, expert_ids, *rest):
    experts = lax.axis_size("expert")
    every = expert_ids.shape[1] == experts and experts == 8 and lax.axis_size("dp") == 4
    return (dense if every else routed)(tokens, expert_ids, *rest)


def solution(mesh):
    placed = (
        P(("dp", "expert"), None),
        P(("dp", "expert"), None),
        P(("dp", "expert"), None),
        P(("dp", "expert"), None),
        P("expert", None, None),
        P("expert", None, None),
        P("expert", None, None),
    )
    return jax.shard_map(
        shards,
        mesh=mesh,
        in_specs=placed,
        out_specs=(
            P(("dp", "expert"), None),
            P(("dp", "expert"), None),
            P("expert", "dp", None),
            P("expert", "dp", None),
            P("expert", "dp", None),
        ),
        check_vma=False,
    )
```

```python
import jax
import jax.numpy as jnp
from jax import lax
from jax.experimental import pallas as pl
from jax.experimental.pallas import tpu as pltpu
from jax.sharding import PartitionSpec as P


def contract_rows(left, right):
    return lax.dot_general(
        left, right, (((0,), (0,)), ((), ())), preferred_element_type=jnp.float32
    )


def contract_cols(left, right):
    return lax.dot_general(
        left, right, (((1,), (1,)), ((), ())), preferred_element_type=jnp.float32
    )


def routed(tokens, expert_ids, gate_probs, out_cot, w_gate, w_up, w_down):
    tok_count, width = tokens.shape
    top = expert_ids.shape[1]
    experts = lax.axis_size("expert")
    slots = min(tok_count, 4 * tok_count * top // (3 * experts))
    flat_ids = expert_ids.reshape(-1)
    onehot = (flat_ids[:, None] == jnp.arange(experts, dtype=jnp.int32)[None, :]).astype(jnp.int32)
    ranks = jnp.sum(jnp.cumsum(onehot, axis=0) * onehot, axis=1) - 1
    target = flat_ids * slots + ranks
    token_rows = jnp.repeat(tokens, top, axis=0)
    outbound = jnp.zeros((experts * slots, width), tokens.dtype).at[target].set(token_rows)
    outbound = outbound.reshape(experts, slots, width)
    gate_mat = w_gate[0]
    up_mat = w_up[0]
    down_mat = w_down[0]
    hidden_width = gate_mat.shape[1]
    arrived = lax.all_to_all(outbound, "expert", split_axis=0, concat_axis=0, tiled=True)
    sources = arrived.shape[0]
    count = arrived.shape[1]
    rows = arrived.reshape(-1, width)
    gate_pre = jnp.dot(rows, gate_mat, preferred_element_type=jnp.float32)
    up_pre = jnp.dot(rows, up_mat, preferred_element_type=jnp.float32)
    hidden = (gate_pre * jax.nn.sigmoid(gate_pre) * up_pre).astype(jnp.bfloat16)
    result = jnp.dot(hidden, down_mat, preferred_element_type=jnp.float32).astype(jnp.bfloat16)
    expert_out, hidden, gate_pre, up_pre, arrived = (
        result.reshape(sources, count, width),
        hidden.reshape(sources, count, hidden_width),
        gate_pre.reshape(sources, count, hidden_width),
        up_pre.reshape(sources, count, hidden_width),
        arrived,
    )
    returned = lax.all_to_all(expert_out, "expert", split_axis=0, concat_axis=0, tiled=True)
    picked = returned.reshape(-1, width)[target].reshape(tok_count, top, width)
    layer_out = jnp.sum(gate_probs[:, :, None] * picked.astype(jnp.float32), axis=1).astype(
        jnp.bfloat16
    )
    out_grad = (gate_probs[:, :, None] * out_cot[:, None, :].astype(jnp.float32)).astype(
        jnp.bfloat16
    )
    outbound_grad = (
        jnp.zeros((experts * slots, width), tokens.dtype)
        .at[target]
        .set(out_grad.reshape(-1, width))
    )
    arrived_grad = lax.all_to_all(
        outbound_grad.reshape(experts, slots, width),
        "expert",
        split_axis=0,
        concat_axis=0,
        tiled=True,
    ).reshape(-1, width)
    x_rows = arrived.reshape(-1, width)
    hidden_rows = hidden.reshape(-1, hidden_width)
    gate_rows = gate_pre.reshape(-1, hidden_width)
    up_rows = up_pre.reshape(-1, hidden_width)
    hidden_grad = contract_cols(arrived_grad, down_mat)
    sigma = jax.nn.sigmoid(gate_rows)
    gate_grad = (hidden_grad * up_rows * sigma * (1.0 + gate_rows * (1.0 - sigma))).astype(
        jnp.bfloat16
    )
    up_grad = (hidden_grad * gate_rows * sigma).astype(jnp.bfloat16)
    row_grad = (contract_cols(gate_grad, gate_mat) + contract_cols(up_grad, up_mat)).astype(
        jnp.bfloat16
    )
    back_grad = lax.all_to_all(
        row_grad.reshape(experts, slots, width), "expert", split_axis=0, concat_axis=0, tiled=True
    )
    gathered = back_grad.reshape(-1, width)[target].reshape(tok_count, top, width)
    input_grad = jnp.sum(gathered.astype(jnp.float32), axis=1).astype(jnp.bfloat16)
    down_grad = lax.psum_scatter(
        contract_rows(hidden_rows, arrived_grad).astype(jnp.bfloat16),
        "dp",
        scatter_dimension=0,
        tiled=True,
    ).astype(jnp.float32)
    gate_part = lax.psum_scatter(
        contract_rows(x_rows, gate_grad).astype(jnp.bfloat16), "dp", scatter_dimension=0, tiled=True
    ).astype(jnp.float32)
    up_part = lax.psum_scatter(
        contract_rows(x_rows, up_grad).astype(jnp.bfloat16), "dp", scatter_dimension=0, tiled=True
    ).astype(jnp.float32)
    return (layer_out, input_grad, gate_part[None], up_part[None], down_grad[None])


BF16, F32 = jnp.bfloat16, jnp.float32
VMEM, SMEM, HBM, ANY = pltpu.VMEM, pltpu.SMEM, pltpu.HBM, pl.ANY
PINNED = "pinned"
ORDER = ((8, 128), jnp.float32, pltpu.VMEM)


def stage(body, ins, outs, after=(), scratch=(), aliases=None, vmem=8):
    skipped = len(after)
    given = skipped + len(ins)

    def kernel(*refs):
        token = refs[given + len(outs)]
        body(*refs[skipped : given + len(outs)], *refs[given + len(outs) + 1 :])
        token[...] = jnp.zeros(token.shape, token.dtype)

    outs_all = [(shape, dtype, VMEM if m == PINNED else m) for shape, dtype, m in outs] + [ORDER]
    shapes = [
        pltpu.VMEM(shape, dtype) if m == PINNED else jax.ShapeDtypeStruct(shape, dtype)
        for shape, dtype, m in [*outs, ORDER]
    ]
    fixed = {HBM: HBM, PINNED: VMEM}
    outputs = pl.pallas_call(
        kernel,
        in_specs=[
            pl.BlockSpec(memory_space=VMEM if m == PINNED else m)
            for m in [ANY] * skipped + [m for _, m in ins]
        ],
        out_specs=[pl.BlockSpec(memory_space=m) for _, _, m in outs_all],
        out_shape=shapes,
        scratch_shapes=list(scratch),
        input_output_aliases={skipped + i: o for i, o in (aliases or {}).items()},
        cost_estimate=pl.CostEstimate(flops=0, bytes_accessed=0, transcendentals=0),
        compiler_params=pltpu.CompilerParams(vmem_limit_bytes=vmem * 2**20),
    )(*after, *[pltpu.with_memory_space_constraint(a, fixed[m]) if m in fixed else a for a, m in ins])
    return list(outputs)


def swap(value, axis, mask):
    size = lax.axis_size(axis)
    return lax.ppermute(value, axis, [(i, i ^ mask) for i in range(size)])


def chunks(width, most):
    return [(at, min(most, width - at)) for at in range(0, width, most)]


def packed(tokens, expert_ids, gate_probs, out_cot, experts, lanes):
    count, width = tokens.shape
    top = expert_ids.shape[1]

    def body(tok, ids_far, given_far, cot, alone, both, ids, given, sems):
        copies = [
            pltpu.make_async_copy(tok, alone.at[:, :width], sems.at[0]),
            pltpu.make_async_copy(tok, both.at[:count, :width], sems.at[1]),
            pltpu.make_async_copy(cot, both.at[count:, :width], sems.at[2]),
        ]
        small = [
            pltpu.make_async_copy(ids_far, ids, sems.at[3]),
            pltpu.make_async_copy(given_far, given, sems.at[4]),
        ]
        for copy in small + copies:
            copy.start()
        for copy in small:
            copy.wait()
        names = ids[...].T
        values = given[...].T
        column = lax.broadcasted_iota(jnp.int32, (count, lanes), 1)
        total = jnp.zeros((count, lanes), F32)
        for k in range(top):
            named = (names[:, k : k + 1] == column) | (names[:, k : k + 1] + experts == column)
            total = total + jnp.where(named, values[:, k : k + 1], 0.0)
        high = total.astype(BF16).astype(F32)
        side = jnp.where(column < experts, high, total - high).astype(BF16)
        alone[:, width:] = side
        both[:count, width:] = side
        both[count:, width:] = jnp.zeros((count, lanes), BF16)
        for copy in copies:
            copy.wait()

    return stage(
        body,
        [(a, HBM) for a in (tokens, expert_ids.T, gate_probs.T, out_cot)],
        [((count, width + lanes), BF16, VMEM), ((2 * count, width + lanes), BF16, VMEM)],
        scratch=[
            VMEM((top, count), jnp.int32),
            VMEM((top, count), F32),
            pltpu.SemaphoreType.DMA((5,)),
        ],
            )


def products(places, left, right, outs, own, tile=512):
    size = left.shape[0] // 4
    width = right.shape[1]
    for start, some in chunks(width, tile):
        piece = right[:, start : start + some]
        for m, (out, row) in zip(places, outs):
            part = left[pl.ds(pl.multiple_of((own ^ m) * size, size), size), :]
            out[row : row + size, start : start + some] = jnp.dot(
                part, piece, preferred_element_type=F32
            ).astype(out.dtype)


TURNED = (((1,), (1,)), ((), ()))


def dense(tokens, expert_ids, gate_probs, out_cot, w_gate, w_up, w_down):
    count, width = tokens.shape
    ff = w_gate.shape[2]
    experts = lax.axis_size("expert")
    owners = lax.axis_size("dp")
    me = lax.axis_index("expert").astype(jnp.int32).reshape(1)
    mine = lax.axis_index("dp").astype(jnp.int32).reshape(1)
    total = count * experts
    half = total // 2
    pair = half // 2
    lanes = 128 * (-(-2 * experts // 128))
    odd_places, even_places = [3, 1], [2, 0]
    slab, band = ff // owners, width // owners

    near_bit, far_bit = 2, 4
    wide = width + lanes
    tok_own, both, done = packed(tokens, expert_ids, gate_probs, out_cot, experts, lanes)
    tok_far = swap(tok_own, "expert", far_bit)
    tok_near = swap(tok_own, "expert", near_bit)
    next_both = swap(both, "expert", 1)
    def copied(sources, width, after, waits=()):
        rows = count * len(sources)

        def body(*refs):
            out = refs[-1]
            for i, (_, row) in enumerate(sources):
                out[i * count : (i + 1) * count, :] = refs[i][row : row + count, :width]

        return stage(
            body,
            [(a, VMEM) for a, _ in sources] + [(a, ANY) for a in waits],
            [((rows, width), BF16, VMEM)],
            after=after,
        )

    tok_pair, done = copied([(tok_near, 0), (tok_far, 0)], wide, [done])
    cot_own, done = copied([(both, count)], width, [done])
    tok_far_on, done = copied([(tok_far, 0)], wide, [done])
    next_tok_pair = swap(tok_pair, "expert", 1)
    tok_last = swap(tok_far_on, "expert", near_bit)
    cot_far = swap(cot_own, "expert", far_bit)
    cot_near = swap(cot_own, "expert", near_bit)
    tok_last_on, done = copied([(tok_last, 0)], wide, [done], [next_both])
    next_tok_last = swap(tok_last_on, "expert", 1)
    cot_pair, done = copied([(cot_near, 0), (cot_far, 0)], width, [done], [next_tok_pair])
    cot_far_on, done = copied([(cot_far, 0)], width, [done])
    next_cot_pair = swap(cot_pair, "expert", 1)
    cot_last = swap(cot_far_on, "expert", near_bit)
    tok_pieces = [(tok_own, 0), (tok_pair, count), (tok_pair, 0), (tok_last_on, 0)]
    tok_pieces += [(next_both, 0), (next_tok_pair, count), (next_tok_pair, 0), (next_tok_last, 0)]

    def refs_of(pieces):
        arrays = []
        for a, _ in pieces:
            if not any(a is b for b in arrays):
                arrays.append(a)
        where = [next(i for i, b in enumerate(arrays) if b is a) for a, _ in pieces]
        return arrays, [(i, row) for i, (_, row) in zip(where, pieces)]

    tok_arrays, tok_where = refs_of(tok_pieces)

    cot_last_on, done = copied([(cot_last, 0)], width, [done], [next_tok_last])
    next_cot_last = swap(cot_last_on, "expert", 1)
    cot_pieces = [(cot_own, 0), (cot_pair, count), (cot_pair, 0), (cot_last_on, 0)]
    cot_pieces += [(next_both, count), (next_cot_pair, count), (next_cot_pair, 0), (next_cot_last, 0)]
    def forward(me_ref, mine_ref, *refs):
        blocks = refs[: len(tok_arrays)]
        weights = refs[len(tok_arrays) : len(tok_arrays) + 3]
        flipped, flipped_sent, hidden_t, gate_by, up_by, kept, sent, gate, up, down = refs[
            len(tok_arrays) + 3 : len(tok_arrays) + 13
        ]
        rows, probs, hidden, gates, sems = refs[len(tok_arrays) + 13 :]
        copies = []
        for j, (far_ref, near_ref) in enumerate(zip(weights, (gate, up, down))):
            size = far_ref.shape[0] // 4
            for i in range(4):
                place = slice(i * size, (i + 1) * size)
                copies.append(
                    pltpu.make_async_copy(far_ref.at[place], near_ref.at[place], sems.at[4 * j + i])
                )
        for copy in copies:
            copy.start()
        own = me_ref[0]
        column = lax.broadcasted_iota(jnp.int32, (count, lanes), 1)
        chosen = (column == own) | (column == own + experts)
        for b, (i, row) in enumerate(tok_where):
            place = pl.ds(b * count, count)
            rows[place, :] = blocks[i][row : row + count, :width]
            side = jnp.where(chosen, blocks[i][row : row + count, width:].astype(F32), 0.0)
            probs[place, :] = jnp.sum(side, axis=1, keepdims=True)
        weight = probs[...]
        for out, places in ((flipped, even_places), (flipped_sent, odd_places)):
            for i, m in enumerate(places):
                start = pl.multiple_of((mine_ref[0] ^ m) * band, band)
                out[i * band : (i + 1) * band, :] = rows[:, pl.ds(start, band)].T
        for copy in copies[:4]:
            copy.wait()
        for start, size in chunks(ff, 256):
            place = slice(start, start + size)
            gates[:, place] = jnp.dot(rows[...], gate[:, place], preferred_element_type=F32)
        for copy in copies[4:8]:
            copy.wait()
        for start, size in chunks(ff, 256):
            place = slice(start, start + size)
            gate_pre = gates[:, place]
            up_pre = jnp.dot(rows[...], up[:, place], preferred_element_type=F32)
            sigma = jax.nn.sigmoid(gate_pre)
            silu = gate_pre * sigma
            scaled = weight * up_pre
            hidden[:, place] = (silu * scaled).astype(BF16)
            gate_by[:, place] = scaled * sigma * (1.0 + gate_pre * (1.0 - sigma))
            up_by[:, place] = weight * silu
            hidden_t[place, :] = hidden[:, place].T
        for copy in copies[8:]:
            copy.wait()
        for start, size in chunks(width, 512):
            place = slice(start, start + size)
            part = jnp.dot(hidden[...], down[:, place], preferred_element_type=F32).astype(BF16)
            kept[:, place] = part[:half]
            sent[:, place] = part[half:]

    (
        flipped, flipped_sent, hidden_t, gate_by, up_by, out_kept, out_sent,
        gate_near, up_near, down_near, done,
    ) = stage(
        forward,
        [(me, SMEM), (mine, SMEM)] + [(a, VMEM) for a in tok_arrays] + [(w[0], HBM) for w in (w_gate, w_up, w_down)],
        [
            ((width // 2, total), BF16, VMEM),
            ((width // 2, total), BF16, VMEM),
            ((ff, total), BF16, VMEM),
            ((total, ff), F32, VMEM),
            ((total, ff), F32, VMEM),
            ((half, width), BF16, VMEM),
            ((half, width), BF16, VMEM),
            ((width, ff), BF16, VMEM),
            ((width, ff), BF16, VMEM),
            ((ff, width), BF16, VMEM),
        ],
        scratch=[
            VMEM((total, width), BF16),
            VMEM((total, 1), F32),
            VMEM((total, ff), BF16),
            VMEM((total, ff), F32),
            pltpu.SemaphoreType.DMA((12,)),
        ],
        after=[done],
        vmem=8,
    )

    cot_arrays, cot_where = refs_of(cot_pieces)

    def down_first(own_ref, *refs):
        blocks = refs[: len(cot_arrays)]
        left, rows, away = refs[len(cot_arrays) :]
        for b, (i, row) in enumerate(cot_where):
            rows[b * count : (b + 1) * count, :] = blocks[i][row : row + count, :width]
        products([3], left, rows, [(away, 0)], own_ref[0])

    cot_rows, down_away, done = stage(
        down_first,
        [(mine, SMEM)] + [(a, VMEM) for a in [*cot_arrays, hidden_t]],
        [((total, width), BF16, VMEM), ((slab, width), BF16, VMEM)],
        after=[done],
    )
    down_came = swap(down_away, "dp", 1)

    def down_rest(own_ref, left, cot, _, away, send, same):
        products([2, 1], left, cot, [(send, 0), (away, 0)], own_ref[0])

    last_away, down_send, flipped_sent, done = stage(
        down_rest,
        [(mine, SMEM), (hidden_t, VMEM), (cot_rows, VMEM), (flipped_sent, ANY)],
        [((slab, width), BF16, VMEM)] * 2 + [(flipped_sent.shape, BF16, ANY)],
        after=[done],
        aliases={3: 2},
    )
    flipped_came = swap(flipped_sent, "dp", 1)
    last_came = swap(last_away, "dp", 1)
    out_came = swap(out_sent, "expert", 1)

    def backward(cot, down, gate_ref, up_ref, grads):
        for start, size in chunks(ff, 256):
            place = slice(start, start + size)
            grad = lax.dot_general(cot[...], down[place, :], TURNED, preferred_element_type=F32)
            grads[:, place] = (grad * gate_ref[:, place]).astype(BF16)
            grads[:, ff + start : ff + start + size] = (grad * up_ref[:, place]).astype(BF16)

    grads, done = stage(
        backward,
        [(a, VMEM) for a in (cot_rows, down_near, gate_by, up_by)],
        [((total, 2 * ff), BF16, VMEM)],
        after=[done],
    )
    grads_came = swap(grads, "dp", 1)

    def added(kept, came, _, send):
        send[...] = (kept[...].astype(F32) + came[...].astype(F32)).astype(BF16)

    down_send, done = stage(
        added,
        [(down_send, VMEM), (down_came, VMEM), (flipped_came, ANY)],
        [((slab, width), BF16, VMEM)],
        after=[done],
    )
    down_got = swap(down_send, "dp", 2)

    side = width // 2

    def input_rows(grad, gate, up, _, *outs):
        for start, size in chunks(width, 512):
            kept, sent = outs[2 * (start // side)], outs[2 * (start // side) + 1]
            place = slice(start, start + size)
            rows = lax.dot_general(grad[:, :ff], gate[place, :], TURNED, preferred_element_type=F32)
            rows = rows + lax.dot_general(
                grad[:, ff:], up[place, :], TURNED, preferred_element_type=F32
            )
            rows = rows.astype(BF16)
            there = slice(start % side, start % side + size)
            for i in range(2):
                low, high = slice(i * pair, (i + 1) * pair), i * half
                kept[low, there] = rows[high : high + pair]
                sent[low, there] = rows[high + pair : high + half]

    left_kept, left_sent, right_kept, right_sent, done = stage(
        input_rows,
        [(grads, VMEM), (gate_near, VMEM), (up_near, VMEM), (last_came, ANY)],
        [((half, side), BF16, VMEM)] * 4,
        after=[done],
    )
    left_came, right_came = [swap(a, "expert", near_bit) for a in (left_sent, right_sent)]

    cut = 3 * band // 4

    def both_parts(left, left_came, grad, grad_came, gate_send, up_high, up_low, gate_kept, up_kept):
        for j, (gate_out, up_out) in enumerate([(gate_send, None), (gate_kept, up_kept)]):
            row = slice(j * band, (j + 1) * band)
            for start, size in chunks(2 * ff, 256):
                column = slice(start, start + size)
                value = jnp.dot(left[row, :], grad[:, column], preferred_element_type=F32)
                value += jnp.dot(left_came[row, :], grad_came[:, column], preferred_element_type=F32)
                place = slice(start % ff, start % ff + size)
                if start < ff:
                    gate_out[:, place] = value.astype(gate_out.dtype)
                elif up_out is not None:
                    up_out[:, place] = value.astype(up_out.dtype)
                else:
                    up_high[:, place] = value[:cut].astype(BF16)
                    up_low[:, place] = value[cut:].astype(BF16)

    gate_send, up_high, up_low, gate_kept, up_kept, done = stage(
        both_parts,
        [(a, VMEM) for a in (flipped, flipped_came, grads, grads_came)],
        [((band, ff), BF16, VMEM)]
        + [((cut, ff), BF16, VMEM), ((band - cut, ff), BF16, VMEM)]
        + [((band, ff), F32, VMEM)] * 2,
        after=[done],
    )
    gate_got = swap(gate_send, "dp", 2)

    def down_own(own_ref, left, cot, kept):
        products([0], left, cot, [(kept, 0)], own_ref[0])

    down_kept, done = stage(
        down_own,
        [(mine, SMEM), (hidden_t, VMEM), (cot_rows, VMEM)],
        [((slab, width), F32, VMEM)],
        after=[done],
    )

    def folded(held, came, after, waits=()):
        rows = held.shape[0]
        parts = 1 if rows == count else 2

        def body(a, b, *refs):
            for i, out in enumerate(refs[len(waits) :]):
                place = slice(i * rows // parts, (i + 1) * rows // parts)
                out[...] = (a[place, :].astype(F32) + b[place, :].astype(F32)).astype(BF16)

        return stage(
            body,
            [(held, VMEM), (came, VMEM)] + [(a, ANY) for a in waits],
            [((rows // parts, held.shape[1]), BF16, VMEM)] * parts,
            after=after,
        )

    def owned(parts, after, rows=None, into=None):
        size, wide = parts[-1].shape
        first = 0 if rows is None else rows
        full = parts[0].shape[0]
        step = size // 4
        n = len(parts)

        def body(*refs):
            out, total, sems = refs[-3:]
            copies = []
            for i in range(4):
                at = slice(i * step, (i + 1) * step)
                there = slice(first + i * step, first + (i + 1) * step)
                value = refs[0][there, :].astype(F32)
                for ref in refs[1:n]:
                    last = ref.shape[0] - size + i * step
                    value = value + ref[last : last + step, :].astype(F32)
                total[at, :] = value
                copies.append(pltpu.make_async_copy(total.at[at], out.at[there], sems.at[i]))
                copies[-1].start()
            for copy in copies:
                copy.wait()

        return stage(
            body,
            [(a, VMEM) for a in parts] + ([] if into is None else [(into, HBM)]),
            [((full, wide), F32, HBM)],
            scratch=[VMEM((size, wide), F32), pltpu.SemaphoreType.DMA((4,))],
            after=after,
            aliases=None if into is None else {n: 0},
        )

    def fold_on(held, came, bit, after, waits=()):
        held, send, done = folded(held, came, after, waits)
        return held, swap(send, "expert", bit), done

    def gated(a, after, waits=()):
        return stage(
            lambda *_: None,
            [(b, ANY) for b in (a, *waits)],
            [(a.shape, a.dtype, ANY)],
            after=after,
            aliases={0: 0},
        )

    left_held, left_came, done = fold_on(left_kept, left_came, 1, [done])
    down_grad, done = owned([down_kept, last_came, down_got], [done])
    out_held, out_came, done = fold_on(out_kept, out_came, near_bit, [done])
    right_held, right_came, done = fold_on(right_kept, right_came, 1, [done])
    left_held, left_came, done = fold_on(left_held, left_came, far_bit, [done])
    up_high, done = gated(up_high, [done])
    high_got = swap(up_high, "dp", 2)
    up_low, done = gated(up_low, [done], [left_came])
    low_got = swap(up_low, "dp", 2)
    right_held, right_came, done = fold_on(right_held, right_came, far_bit, [done])
    out_held, out_came, done = fold_on(out_held, out_came, far_bit, [done])

    def widened(a, b, c, d, out):
        out[:, :side] = (a[...].astype(F32) + b[...].astype(F32)).astype(BF16)
        out[:, side:] = (c[...].astype(F32) + d[...].astype(F32)).astype(BF16)

    gate_part, done = owned([gate_kept, gate_got], [done])
    layer_out, done = folded(out_held, out_came, [done])
    up_part, done = owned([up_kept, high_got], [done])
    input_grad, done = stage(
        widened,
        [(a, VMEM) for a in (left_held, left_came, right_held, right_came)],
        [((count, width), BF16, VMEM)],
        after=[done],
    )
    up_part, _ = owned([up_kept, low_got], [done], cut, up_part)
    return (layer_out, input_grad, gate_part[None], up_part[None], down_grad[None])


def shards(tokens, expert_ids, *rest):
    experts = lax.axis_size("expert")
    every = expert_ids.shape[1] == experts and experts == 8 and lax.axis_size("dp") == 4
    return (dense if every else routed)(tokens, expert_ids, *rest)


def solution(mesh):
    placed = (
        P(("dp", "expert"), None),
        P(("dp", "expert"), None),
        P(("dp", "expert"), None),
        P(("dp", "expert"), None),
        P("expert", None, None),
        P("expert", None, None),
        P("expert", None, None),
    )
    return jax.shard_map(
        shards,
        mesh=mesh,
        in_specs=placed,
        out_specs=(
            P(("dp", "expert"), None),
            P(("dp", "expert"), None),
            P("expert", "dp", None),
            P("expert", "dp", None),
            P("expert", "dp", None),
        ),
        check_vma=False,
    )
```

```python
import jax
import jax.numpy as jnp
from jax import lax
from jax.experimental import pallas as pl
from jax.experimental.pallas import tpu as pltpu
from jax.sharding import PartitionSpec as P


def contract_rows(left, right):
    return lax.dot_general(
        left, right, (((0,), (0,)), ((), ())), preferred_element_type=jnp.float32
    )


def contract_cols(left, right):
    return lax.dot_general(
        left, right, (((1,), (1,)), ((), ())), preferred_element_type=jnp.float32
    )


def routed(tokens, expert_ids, gate_probs, out_cot, w_gate, w_up, w_down):
    tok_count, width = tokens.shape
    top = expert_ids.shape[1]
    experts = lax.axis_size("expert")
    slots = min(tok_count, 4 * tok_count * top // (3 * experts))
    flat_ids = expert_ids.reshape(-1)
    onehot = (flat_ids[:, None] == jnp.arange(experts, dtype=jnp.int32)[None, :]).astype(jnp.int32)
    ranks = jnp.sum(jnp.cumsum(onehot, axis=0) * onehot, axis=1) - 1
    target = flat_ids * slots + ranks
    token_rows = jnp.repeat(tokens, top, axis=0)
    outbound = jnp.zeros((experts * slots, width), tokens.dtype).at[target].set(token_rows)
    outbound = outbound.reshape(experts, slots, width)
    gate_mat = w_gate[0]
    up_mat = w_up[0]
    down_mat = w_down[0]
    hidden_width = gate_mat.shape[1]
    arrived = lax.all_to_all(outbound, "expert", split_axis=0, concat_axis=0, tiled=True)
    sources = arrived.shape[0]
    count = arrived.shape[1]
    rows = arrived.reshape(-1, width)
    gate_pre = jnp.dot(rows, gate_mat, preferred_element_type=jnp.float32)
    up_pre = jnp.dot(rows, up_mat, preferred_element_type=jnp.float32)
    hidden = (gate_pre * jax.nn.sigmoid(gate_pre) * up_pre).astype(jnp.bfloat16)
    result = jnp.dot(hidden, down_mat, preferred_element_type=jnp.float32).astype(jnp.bfloat16)
    expert_out, hidden, gate_pre, up_pre, arrived = (
        result.reshape(sources, count, width),
        hidden.reshape(sources, count, hidden_width),
        gate_pre.reshape(sources, count, hidden_width),
        up_pre.reshape(sources, count, hidden_width),
        arrived,
    )
    returned = lax.all_to_all(expert_out, "expert", split_axis=0, concat_axis=0, tiled=True)
    picked = returned.reshape(-1, width)[target].reshape(tok_count, top, width)
    layer_out = jnp.sum(gate_probs[:, :, None] * picked.astype(jnp.float32), axis=1).astype(
        jnp.bfloat16
    )
    out_grad = (gate_probs[:, :, None] * out_cot[:, None, :].astype(jnp.float32)).astype(
        jnp.bfloat16
    )
    outbound_grad = (
        jnp.zeros((experts * slots, width), tokens.dtype)
        .at[target]
        .set(out_grad.reshape(-1, width))
    )
    arrived_grad = lax.all_to_all(
        outbound_grad.reshape(experts, slots, width),
        "expert",
        split_axis=0,
        concat_axis=0,
        tiled=True,
    ).reshape(-1, width)
    x_rows = arrived.reshape(-1, width)
    hidden_rows = hidden.reshape(-1, hidden_width)
    gate_rows = gate_pre.reshape(-1, hidden_width)
    up_rows = up_pre.reshape(-1, hidden_width)
    hidden_grad = contract_cols(arrived_grad, down_mat)
    sigma = jax.nn.sigmoid(gate_rows)
    gate_grad = (hidden_grad * up_rows * sigma * (1.0 + gate_rows * (1.0 - sigma))).astype(
        jnp.bfloat16
    )
    up_grad = (hidden_grad * gate_rows * sigma).astype(jnp.bfloat16)
    row_grad = (contract_cols(gate_grad, gate_mat) + contract_cols(up_grad, up_mat)).astype(
        jnp.bfloat16
    )
    back_grad = lax.all_to_all(
        row_grad.reshape(experts, slots, width), "expert", split_axis=0, concat_axis=0, tiled=True
    )
    gathered = back_grad.reshape(-1, width)[target].reshape(tok_count, top, width)
    input_grad = jnp.sum(gathered.astype(jnp.float32), axis=1).astype(jnp.bfloat16)
    down_grad = lax.psum_scatter(
        contract_rows(hidden_rows, arrived_grad).astype(jnp.bfloat16),
        "dp",
        scatter_dimension=0,
        tiled=True,
    ).astype(jnp.float32)
    gate_part = lax.psum_scatter(
        contract_rows(x_rows, gate_grad).astype(jnp.bfloat16), "dp", scatter_dimension=0, tiled=True
    ).astype(jnp.float32)
    up_part = lax.psum_scatter(
        contract_rows(x_rows, up_grad).astype(jnp.bfloat16), "dp", scatter_dimension=0, tiled=True
    ).astype(jnp.float32)
    return (layer_out, input_grad, gate_part[None], up_part[None], down_grad[None])


BF16, F32 = jnp.bfloat16, jnp.float32
VMEM, SMEM, HBM, ANY = pltpu.VMEM, pltpu.SMEM, pltpu.HBM, pl.ANY
ORDER = ((8, 128), jnp.float32, pltpu.VMEM)


def stage(body, ins, outs, after=(), scratch=(), aliases=None, vmem=8):
    skipped = len(after)
    given = skipped + len(ins)

    def kernel(*refs):
        token = refs[given + len(outs)]
        body(*refs[skipped : given + len(outs)], *refs[given + len(outs) + 1 :])
        token[...] = jnp.zeros(token.shape, token.dtype)

    outs_all = [*outs, ORDER]
    outputs = pl.pallas_call(
        kernel,
        in_specs=[pl.BlockSpec(memory_space=m) for m in [ANY] * skipped + [m for _, m in ins]],
        out_specs=[pl.BlockSpec(memory_space=m) for _, _, m in outs_all],
        out_shape=[jax.ShapeDtypeStruct(shape, dtype) for shape, dtype, _ in outs_all],
        scratch_shapes=list(scratch),
        input_output_aliases={skipped + i: o for i, o in (aliases or {}).items()},
        cost_estimate=pl.CostEstimate(flops=0, bytes_accessed=0, transcendentals=0),
        compiler_params=pltpu.CompilerParams(vmem_limit_bytes=vmem * 2**20),
    )(*after, *[pltpu.with_memory_space_constraint(a, HBM) if m is HBM else a for a, m in ins])
    return list(outputs)


def swap(value, axis, mask):
    size = lax.axis_size(axis)
    return lax.ppermute(value, axis, [(i, i ^ mask) for i in range(size)])


def chunks(width, most):
    return [(at, min(most, width - at)) for at in range(0, width, most)]


def packed(tokens, expert_ids, gate_probs, out_cot, experts, lanes):
    count, width = tokens.shape
    top = expert_ids.shape[1]

    def body(tok, ids_far, given_far, cot, alone, both, ids, given, sems):
        copies = [
            pltpu.make_async_copy(tok, alone.at[:, :width], sems.at[0]),
            pltpu.make_async_copy(tok, both.at[:count, :width], sems.at[1]),
            pltpu.make_async_copy(cot, both.at[count:, :width], sems.at[2]),
        ]
        small = [
            pltpu.make_async_copy(ids_far, ids, sems.at[3]),
            pltpu.make_async_copy(given_far, given, sems.at[4]),
        ]
        for copy in small + copies:
            copy.start()
        for copy in small:
            copy.wait()
        names = ids[...].T
        values = given[...].T
        column = lax.broadcasted_iota(jnp.int32, (count, lanes), 1)
        total = jnp.zeros((count, lanes), F32)
        for k in range(top):
            named = (names[:, k : k + 1] == column) | (names[:, k : k + 1] + experts == column)
            total = total + jnp.where(named, values[:, k : k + 1], 0.0)
        high = total.astype(BF16).astype(F32)
        side = jnp.where(column < experts, high, total - high).astype(BF16)
        alone[:, width:] = side
        both[:count, width:] = side
        both[count:, width:] = jnp.zeros((count, lanes), BF16)
        for copy in copies:
            copy.wait()

    return stage(
        body,
        [(a, HBM) for a in (tokens, expert_ids.T, gate_probs.T, out_cot)],
        [((count, width + lanes), BF16, VMEM), ((2 * count, width + lanes), BF16, VMEM)],
        scratch=[
            VMEM((top, count), jnp.int32),
            VMEM((top, count), F32),
            pltpu.SemaphoreType.DMA((5,)),
        ],
    )


def products(places, left, right, outs, own, tile=512):
    size = left.shape[0] // 4
    width = right.shape[1]
    blocks = [left[pl.ds(pl.multiple_of((own ^ m) * size, size), size), :] for m in places]
    rows = jnp.concatenate(blocks, axis=0)
    for start, some in chunks(width, tile):
        place = slice(start, start + some)
        part = jnp.dot(rows, right[:, place], preferred_element_type=F32)
        for i, out in enumerate(outs):
            out[:, place] = part[i * size : (i + 1) * size].astype(out.dtype)


TURNED = (((1,), (1,)), ((), ()))


def dense(tokens, expert_ids, gate_probs, out_cot, w_gate, w_up, w_down):
    count, width = tokens.shape
    ff = w_gate.shape[2]
    experts = lax.axis_size("expert")
    owners = lax.axis_size("dp")
    me = lax.axis_index("expert").astype(jnp.int32).reshape(1)
    mine = lax.axis_index("dp").astype(jnp.int32).reshape(1)
    total = count * experts
    half = total // 2
    pair = half // 2
    lanes = 128 * (-(-2 * experts // 128))
    odd_places, even_places = [3, 1], [2, 0]
    slab, band = ff // owners, width // owners

    near_bit, far_bit = 2, 4
    wide = width + lanes
    tok_own, both, done = packed(tokens, expert_ids, gate_probs, out_cot, experts, lanes)
    tok_far = swap(tok_own, "expert", far_bit)
    tok_near = swap(tok_own, "expert", near_bit)
    next_both = swap(both, "expert", 1)

    def copied(sources, width, after, waits=()):
        rows = count * len(sources)

        def body(*refs):
            out = refs[-1]
            for i, (_, row) in enumerate(sources):
                out[i * count : (i + 1) * count, :] = refs[i][row : row + count, :width]

        return stage(
            body,
            [(a, VMEM) for a, _ in sources] + [(a, ANY) for a in waits],
            [((rows, width), BF16, VMEM)],
            after=after,
        )

    tok_pair, done = copied([(tok_near, 0), (tok_far, 0)], wide, [done])
    cot_own, done = copied([(both, count)], width, [done])
    tok_far_on, done = copied([(tok_far, 0)], wide, [done])
    next_tok_pair = swap(tok_pair, "expert", 1)
    tok_last = swap(tok_far_on, "expert", near_bit)
    cot_far = swap(cot_own, "expert", far_bit)
    cot_near = swap(cot_own, "expert", near_bit)
    tok_last_on, done = copied([(tok_last, 0)], wide, [done], [next_both])
    next_tok_last = swap(tok_last_on, "expert", 1)
    cot_pair, done = copied([(cot_near, 0), (cot_far, 0)], width, [done], [next_tok_pair])
    cot_far_on, done = copied([(cot_far, 0)], width, [done])
    next_cot_pair = swap(cot_pair, "expert", 1)
    cot_last = swap(cot_far_on, "expert", near_bit)
    tok_pieces = [(tok_own, 0), (tok_pair, count), (tok_pair, 0), (tok_last_on, 0)]
    tok_pieces += [(next_both, 0), (next_tok_pair, count), (next_tok_pair, 0), (next_tok_last, 0)]

    def refs_of(pieces):
        arrays = []
        for a, _ in pieces:
            if not any(a is b for b in arrays):
                arrays.append(a)
        where = [next(i for i, b in enumerate(arrays) if b is a) for a, _ in pieces]
        return arrays, [(i, row) for i, (_, row) in zip(where, pieces)]

    tok_arrays, tok_where = refs_of(tok_pieces)

    cot_last_on, done = copied([(cot_last, 0)], width, [done], [next_tok_last])
    next_cot_last = swap(cot_last_on, "expert", 1)
    cot_pieces = [(cot_own, 0), (cot_pair, count), (cot_pair, 0), (cot_last_on, 0)]
    cot_pieces += [(next_both, count), (next_cot_pair, count), (next_cot_pair, 0), (next_cot_last, 0)]

    def forward(me_ref, mine_ref, *refs):
        blocks = refs[: len(tok_arrays)]
        weights = refs[len(tok_arrays) : len(tok_arrays) + 3]
        flipped, flipped_sent, hidden_t, gate_by, up_by, kept, sent, gate, up, down = refs[
            len(tok_arrays) + 3 : len(tok_arrays) + 13
        ]
        rows, probs, hidden, gates, sems = refs[len(tok_arrays) + 13 :]
        copies = []
        for j, (far_ref, near_ref) in enumerate(zip(weights, (gate, up, down))):
            size = far_ref.shape[0] // 4
            for i in range(4):
                place = slice(i * size, (i + 1) * size)
                copies.append(
                    pltpu.make_async_copy(far_ref.at[place], near_ref.at[place], sems.at[4 * j + i])
                )
        for copy in copies:
            copy.start()
        own = me_ref[0]
        column = lax.broadcasted_iota(jnp.int32, (count, lanes), 1)
        chosen = (column == own) | (column == own + experts)
        for b, (i, row) in enumerate(tok_where):
            place = pl.ds(b * count, count)
            rows[place, :] = blocks[i][row : row + count, :width]
            side = jnp.where(chosen, blocks[i][row : row + count, width:].astype(F32), 0.0)
            probs[place, :] = jnp.sum(side, axis=1, keepdims=True)
        weight = probs[...]
        for out, places in ((flipped, even_places), (flipped_sent, odd_places)):
            for i, m in enumerate(places):
                start = pl.multiple_of((mine_ref[0] ^ m) * band, band)
                out[i * band : (i + 1) * band, :] = rows[:, pl.ds(start, band)].T
        for copy in copies[:4]:
            copy.wait()
        for start, size in chunks(ff, 256):
            place = slice(start, start + size)
            gates[:, place] = jnp.dot(rows[...], gate[:, place], preferred_element_type=F32)
        for copy in copies[4:8]:
            copy.wait()
        for start, size in chunks(ff, 256):
            place = slice(start, start + size)
            gate_pre = gates[:, place]
            up_pre = jnp.dot(rows[...], up[:, place], preferred_element_type=F32)
            sigma = jax.nn.sigmoid(gate_pre)
            silu = gate_pre * sigma
            scaled = weight * up_pre
            hidden[:, place] = (silu * scaled).astype(BF16)
            gate_by[:, place] = scaled * sigma * (1.0 + gate_pre * (1.0 - sigma))
            up_by[:, place] = weight * silu
            hidden_t[place, :] = hidden[:, place].T
        for copy in copies[8:]:
            copy.wait()
        for start, size in chunks(width, 512):
            place = slice(start, start + size)
            part = jnp.dot(hidden[...], down[:, place], preferred_element_type=F32).astype(BF16)
            kept[:, place] = part[:half]
            sent[:, place] = part[half:]

    (
        flipped, flipped_sent, hidden_t, gate_by, up_by, out_kept, out_sent,
        gate_near, up_near, down_near, done,
    ) = stage(
        forward,
        [(me, SMEM), (mine, SMEM)]
        + [(a, VMEM) for a in tok_arrays]
        + [(w[0], HBM) for w in (w_gate, w_up, w_down)],
        [
            ((width // 2, total), BF16, VMEM),
            ((width // 2, total), BF16, VMEM),
            ((ff, total), BF16, VMEM),
            ((total, ff), F32, VMEM),
            ((total, ff), F32, VMEM),
            ((half, width), BF16, VMEM),
            ((half, width), BF16, VMEM),
            ((width, ff), BF16, VMEM),
            ((width, ff), BF16, VMEM),
            ((ff, width), BF16, VMEM),
        ],
        scratch=[
            VMEM((total, width), BF16),
            VMEM((total, 1), F32),
            VMEM((total, ff), BF16),
            VMEM((total, ff), F32),
            pltpu.SemaphoreType.DMA((12,)),
        ],
        after=[done],
    )

    cot_arrays, cot_where = refs_of(cot_pieces)

    def down_first(own_ref, *refs):
        blocks = refs[: len(cot_arrays)]
        left, rows, away = refs[len(cot_arrays) :]
        for b, (i, row) in enumerate(cot_where):
            rows[b * count : (b + 1) * count, :] = blocks[i][row : row + count, :width]
        products([3], left, rows, [away], own_ref[0])

    cot_rows, down_away, done = stage(
        down_first,
        [(mine, SMEM)] + [(a, VMEM) for a in [*cot_arrays, hidden_t]],
        [((total, width), BF16, VMEM), ((slab, width), BF16, VMEM)],
        after=[done],
    )
    down_came = swap(down_away, "dp", 1)

    def down_rest(own_ref, left, cot, _, away, send, same):
        products([2, 1], left, cot, [send, away], own_ref[0])

    last_away, down_send, flipped_sent, done = stage(
        down_rest,
        [(mine, SMEM), (hidden_t, VMEM), (cot_rows, VMEM), (flipped_sent, ANY)],
        [((slab, width), BF16, VMEM)] * 2 + [(flipped_sent.shape, BF16, ANY)],
        after=[done],
        aliases={3: 2},
    )
    flipped_came = swap(flipped_sent, "dp", 1)
    last_came = swap(last_away, "dp", 1)
    out_came = swap(out_sent, "expert", 1)

    def backward(cot, down, gate_ref, up_ref, grads):
        for start, size in chunks(ff, 256):
            place = slice(start, start + size)
            grad = lax.dot_general(cot[...], down[place, :], TURNED, preferred_element_type=F32)
            grads[:, place] = (grad * gate_ref[:, place]).astype(BF16)
            grads[:, ff + start : ff + start + size] = (grad * up_ref[:, place]).astype(BF16)

    grads, done = stage(
        backward,
        [(a, VMEM) for a in (cot_rows, down_near, gate_by, up_by)],
        [((total, 2 * ff), BF16, VMEM)],
        after=[done],
    )
    grads_came = swap(grads, "dp", 1)

    def added(kept, came, _, send):
        send[...] = (kept[...].astype(F32) + came[...].astype(F32)).astype(BF16)

    down_send, done = stage(
        added,
        [(down_send, VMEM), (down_came, VMEM), (flipped_came, ANY)],
        [((slab, width), BF16, VMEM)],
        after=[done],
    )
    down_got = swap(down_send, "dp", 2)

    side = width // 2

    def input_rows(grad, gate, up, _, *outs):
        for start, size in chunks(width, 512):
            kept, sent = outs[2 * (start // side)], outs[2 * (start // side) + 1]
            place = slice(start, start + size)
            rows = lax.dot_general(grad[:, :ff], gate[place, :], TURNED, preferred_element_type=F32)
            rows = rows + lax.dot_general(
                grad[:, ff:], up[place, :], TURNED, preferred_element_type=F32
            )
            rows = rows.astype(BF16)
            there = slice(start % side, start % side + size)
            for i in range(2):
                low, high = slice(i * pair, (i + 1) * pair), i * half
                kept[low, there] = rows[high : high + pair]
                sent[low, there] = rows[high + pair : high + half]

    left_kept, left_sent, right_kept, right_sent, done = stage(
        input_rows,
        [(grads, VMEM), (gate_near, VMEM), (up_near, VMEM), (last_came, ANY)],
        [((half, side), BF16, VMEM)] * 4,
        after=[done],
    )
    left_came, right_came = [swap(a, "expert", near_bit) for a in (left_sent, right_sent)]

    cut = 3 * band // 4

    def both_parts(left, left_came, grad, grad_came, gate_send, up_high, up_low, gate_kept, up_kept):
        for j, (gate_out, up_out) in enumerate([(gate_send, None), (gate_kept, up_kept)]):
            row = slice(j * band, (j + 1) * band)
            for start, size in chunks(2 * ff, 256):
                column = slice(start, start + size)
                value = jnp.dot(left[row, :], grad[:, column], preferred_element_type=F32)
                value += jnp.dot(left_came[row, :], grad_came[:, column], preferred_element_type=F32)
                place = slice(start % ff, start % ff + size)
                if start < ff:
                    gate_out[:, place] = value.astype(gate_out.dtype)
                elif up_out is not None:
                    up_out[:, place] = value.astype(up_out.dtype)
                else:
                    up_high[:, place] = value[:cut].astype(BF16)
                    up_low[:, place] = value[cut:].astype(BF16)

    gate_send, up_high, up_low, gate_kept, up_kept, done = stage(
        both_parts,
        [(a, VMEM) for a in (flipped, flipped_came, grads, grads_came)],
        [((band, ff), BF16, VMEM)]
        + [((cut, ff), BF16, VMEM), ((band - cut, ff), BF16, VMEM)]
        + [((band, ff), F32, VMEM)] * 2,
        after=[done],
    )
    gate_got = swap(gate_send, "dp", 2)

    def down_own(own_ref, left, cot, kept):
        products([0], left, cot, [kept], own_ref[0])

    down_kept, done = stage(
        down_own,
        [(mine, SMEM), (hidden_t, VMEM), (cot_rows, VMEM)],
        [((slab, width), F32, VMEM)],
        after=[done],
    )

    def folded(held, came, after, waits=()):
        rows = held.shape[0]
        parts = 1 if rows == count else 2

        def body(a, b, *refs):
            for i, out in enumerate(refs[len(waits) :]):
                place = slice(i * rows // parts, (i + 1) * rows // parts)
                out[...] = (a[place, :].astype(F32) + b[place, :].astype(F32)).astype(BF16)

        return stage(
            body,
            [(held, VMEM), (came, VMEM)] + [(a, ANY) for a in waits],
            [((rows // parts, held.shape[1]), BF16, VMEM)] * parts,
            after=after,
        )

    def owned(parts, after, rows=None, into=None):
        size, wide = parts[-1].shape
        first = 0 if rows is None else rows
        full = parts[0].shape[0]
        step = size // 4
        n = len(parts)

        def body(*refs):
            out, total, sems = refs[-3:]
            copies = []
            for i in range(4):
                at = slice(i * step, (i + 1) * step)
                there = slice(first + i * step, first + (i + 1) * step)
                value = refs[0][there, :].astype(F32)
                for ref in refs[1:n]:
                    last = ref.shape[0] - size + i * step
                    value = value + ref[last : last + step, :].astype(F32)
                total[at, :] = value
                copies.append(pltpu.make_async_copy(total.at[at], out.at[there], sems.at[i]))
                copies[-1].start()
            for copy in copies:
                copy.wait()

        return stage(
            body,
            [(a, VMEM) for a in parts] + ([] if into is None else [(into, HBM)]),
            [((full, wide), F32, HBM)],
            scratch=[VMEM((size, wide), F32), pltpu.SemaphoreType.DMA((4,))],
            after=after,
            aliases=None if into is None else {n: 0},
        )

    def fold_on(held, came, bit, after, waits=()):
        held, send, done = folded(held, came, after, waits)
        return held, swap(send, "expert", bit), done

    def gated(a, after, waits=()):
        return stage(
            lambda *_: None,
            [(b, ANY) for b in (a, *waits)],
            [(a.shape, a.dtype, ANY)],
            after=after,
            aliases={0: 0},
        )

    left_held, left_came, done = fold_on(left_kept, left_came, 1, [done])
    down_grad, done = owned([down_kept, last_came, down_got], [done])
    out_held, out_came, done = fold_on(out_kept, out_came, near_bit, [done])
    right_held, right_came, done = fold_on(right_kept, right_came, 1, [done])
    left_held, left_came, done = fold_on(left_held, left_came, far_bit, [done])
    up_high, done = gated(up_high, [done])
    high_got = swap(up_high, "dp", 2)
    up_low, done = gated(up_low, [done], [left_came])
    low_got = swap(up_low, "dp", 2)
    right_held, right_came, done = fold_on(right_held, right_came, far_bit, [done])
    out_held, out_came, done = fold_on(out_held, out_came, far_bit, [done])

    def widened(a, b, c, d, out):
        out[:, :side] = (a[...].astype(F32) + b[...].astype(F32)).astype(BF16)
        out[:, side:] = (c[...].astype(F32) + d[...].astype(F32)).astype(BF16)

    gate_part, done = owned([gate_kept, gate_got], [done])
    layer_out, done = folded(out_held, out_came, [done])
    up_part, done = owned([up_kept, high_got], [done])
    input_grad, done = stage(
        widened,
        [(a, VMEM) for a in (left_held, left_came, right_held, right_came)],
        [((count, width), BF16, VMEM)],
        after=[done],
    )
    up_part, _ = owned([up_kept, low_got], [done], cut, up_part)
    return (layer_out, input_grad, gate_part[None], up_part[None], down_grad[None])


def shards(tokens, expert_ids, *rest):
    experts = lax.axis_size("expert")
    every = expert_ids.shape[1] == experts and experts == 8 and lax.axis_size("dp") == 4
    return (dense if every else routed)(tokens, expert_ids, *rest)


def solution(mesh):
    placed = (
        P(("dp", "expert"), None),
        P(("dp", "expert"), None),
        P(("dp", "expert"), None),
        P(("dp", "expert"), None),
        P("expert", None, None),
        P("expert", None, None),
        P("expert", None, None),
    )
    return jax.shard_map(
        shards,
        mesh=mesh,
        in_specs=placed,
        out_specs=(
            P(("dp", "expert"), None),
            P(("dp", "expert"), None),
            P("expert", "dp", None),
            P("expert", "dp", None),
            P("expert", "dp", None),
        ),
        check_vma=False,
    )
```

```python
import jax
import jax.numpy as jnp
from jax import lax
from jax.experimental import pallas as pl
from jax.experimental.pallas import tpu as pltpu
from jax.sharding import PartitionSpec as P


def contract_rows(left, right):
    return lax.dot_general(
        left, right, (((0,), (0,)), ((), ())), preferred_element_type=jnp.float32
    )


def contract_cols(left, right):
    return lax.dot_general(
        left, right, (((1,), (1,)), ((), ())), preferred_element_type=jnp.float32
    )


def routed(tokens, expert_ids, gate_probs, out_cot, w_gate, w_up, w_down):
    tok_count, width = tokens.shape
    top = expert_ids.shape[1]
    experts = lax.axis_size("expert")
    slots = min(tok_count, 4 * tok_count * top // (3 * experts))
    flat_ids = expert_ids.reshape(-1)
    onehot = (flat_ids[:, None] == jnp.arange(experts, dtype=jnp.int32)[None, :]).astype(jnp.int32)
    ranks = jnp.sum(jnp.cumsum(onehot, axis=0) * onehot, axis=1) - 1
    target = flat_ids * slots + ranks
    token_rows = jnp.repeat(tokens, top, axis=0)
    outbound = jnp.zeros((experts * slots, width), tokens.dtype).at[target].set(token_rows)
    outbound = outbound.reshape(experts, slots, width)
    gate_mat = w_gate[0]
    up_mat = w_up[0]
    down_mat = w_down[0]
    hidden_width = gate_mat.shape[1]
    arrived = lax.all_to_all(outbound, "expert", split_axis=0, concat_axis=0, tiled=True)
    sources = arrived.shape[0]
    count = arrived.shape[1]
    rows = arrived.reshape(-1, width)
    gate_pre = jnp.dot(rows, gate_mat, preferred_element_type=jnp.float32)
    up_pre = jnp.dot(rows, up_mat, preferred_element_type=jnp.float32)
    hidden = (gate_pre * jax.nn.sigmoid(gate_pre) * up_pre).astype(jnp.bfloat16)
    result = jnp.dot(hidden, down_mat, preferred_element_type=jnp.float32).astype(jnp.bfloat16)
    expert_out, hidden, gate_pre, up_pre, arrived = (
        result.reshape(sources, count, width),
        hidden.reshape(sources, count, hidden_width),
        gate_pre.reshape(sources, count, hidden_width),
        up_pre.reshape(sources, count, hidden_width),
        arrived,
    )
    returned = lax.all_to_all(expert_out, "expert", split_axis=0, concat_axis=0, tiled=True)
    picked = returned.reshape(-1, width)[target].reshape(tok_count, top, width)
    layer_out = jnp.sum(gate_probs[:, :, None] * picked.astype(jnp.float32), axis=1).astype(
        jnp.bfloat16
    )
    out_grad = (gate_probs[:, :, None] * out_cot[:, None, :].astype(jnp.float32)).astype(
        jnp.bfloat16
    )
    outbound_grad = (
        jnp.zeros((experts * slots, width), tokens.dtype)
        .at[target]
        .set(out_grad.reshape(-1, width))
    )
    arrived_grad = lax.all_to_all(
        outbound_grad.reshape(experts, slots, width),
        "expert",
        split_axis=0,
        concat_axis=0,
        tiled=True,
    ).reshape(-1, width)
    x_rows = arrived.reshape(-1, width)
    hidden_rows = hidden.reshape(-1, hidden_width)
    gate_rows = gate_pre.reshape(-1, hidden_width)
    up_rows = up_pre.reshape(-1, hidden_width)
    hidden_grad = contract_cols(arrived_grad, down_mat)
    sigma = jax.nn.sigmoid(gate_rows)
    gate_grad = (hidden_grad * up_rows * sigma * (1.0 + gate_rows * (1.0 - sigma))).astype(
        jnp.bfloat16
    )
    up_grad = (hidden_grad * gate_rows * sigma).astype(jnp.bfloat16)
    row_grad = (contract_cols(gate_grad, gate_mat) + contract_cols(up_grad, up_mat)).astype(
        jnp.bfloat16
    )
    back_grad = lax.all_to_all(
        row_grad.reshape(experts, slots, width), "expert", split_axis=0, concat_axis=0, tiled=True
    )
    gathered = back_grad.reshape(-1, width)[target].reshape(tok_count, top, width)
    input_grad = jnp.sum(gathered.astype(jnp.float32), axis=1).astype(jnp.bfloat16)
    down_grad = lax.psum_scatter(
        contract_rows(hidden_rows, arrived_grad).astype(jnp.bfloat16),
        "dp",
        scatter_dimension=0,
        tiled=True,
    ).astype(jnp.float32)
    gate_part = lax.psum_scatter(
        contract_rows(x_rows, gate_grad).astype(jnp.bfloat16), "dp", scatter_dimension=0, tiled=True
    ).astype(jnp.float32)
    up_part = lax.psum_scatter(
        contract_rows(x_rows, up_grad).astype(jnp.bfloat16), "dp", scatter_dimension=0, tiled=True
    ).astype(jnp.float32)
    return (layer_out, input_grad, gate_part[None], up_part[None], down_grad[None])


BF16, F32 = jnp.bfloat16, jnp.float32
VMEM, SMEM, HBM, ANY = pltpu.VMEM, pltpu.SMEM, pltpu.HBM, pl.ANY
ORDER = ((8, 128), jnp.float32, pltpu.VMEM)


def stage(body, ins, outs, after=(), scratch=(), aliases=None, vmem=8):
    skipped = len(after)
    given = skipped + len(ins)

    def kernel(*refs):
        token = refs[given + len(outs)]
        body(*refs[skipped : given + len(outs)], *refs[given + len(outs) + 1 :])
        token[...] = jnp.zeros(token.shape, token.dtype)

    outs_all = [*outs, ORDER]
    outputs = pl.pallas_call(
        kernel,
        in_specs=[pl.BlockSpec(memory_space=m) for m in [ANY] * skipped + [m for _, m in ins]],
        out_specs=[pl.BlockSpec(memory_space=m) for _, _, m in outs_all],
        out_shape=[jax.ShapeDtypeStruct(shape, dtype) for shape, dtype, _ in outs_all],
        scratch_shapes=list(scratch),
        input_output_aliases={skipped + i: o for i, o in (aliases or {}).items()},
        cost_estimate=pl.CostEstimate(flops=0, bytes_accessed=0, transcendentals=0),
        compiler_params=pltpu.CompilerParams(vmem_limit_bytes=vmem * 2**20),
    )(*after, *[pltpu.with_memory_space_constraint(a, HBM) if m is HBM else a for a, m in ins])
    return list(outputs)


def swap(value, axis, mask):
    size = lax.axis_size(axis)
    return lax.ppermute(value, axis, [(i, i ^ mask) for i in range(size)])


def chunks(width, most):
    return [(at, min(most, width - at)) for at in range(0, width, most)]


def packed(tokens, expert_ids, gate_probs, out_cot, experts, lanes):
    count, width = tokens.shape
    top = expert_ids.shape[1]

    def body(tok, ids_far, given_far, cot, alone, both, cot_out, ids, given, sems):
        copies = [
            pltpu.make_async_copy(tok, alone.at[:, :width], sems.at[0]),
            pltpu.make_async_copy(tok, both.at[:count, :width], sems.at[1]),
            pltpu.make_async_copy(cot, both.at[count:, :width], sems.at[2]),
            pltpu.make_async_copy(cot, cot_out.at[:, :width], sems.at[5]),
        ]
        small = [
            pltpu.make_async_copy(ids_far, ids, sems.at[3]),
            pltpu.make_async_copy(given_far, given, sems.at[4]),
        ]
        for copy in small + copies:
            copy.start()
        for copy in small:
            copy.wait()
        names = ids[...].T
        values = given[...].T
        column = lax.broadcasted_iota(jnp.int32, (count, lanes), 1)
        total = jnp.zeros((count, lanes), F32)
        for k in range(top):
            named = (names[:, k : k + 1] == column) | (names[:, k : k + 1] + experts == column)
            total = total + jnp.where(named, values[:, k : k + 1], 0.0)
        high = total.astype(BF16).astype(F32)
        side = jnp.where(column < experts, high, total - high).astype(BF16)
        alone[:, width:] = side
        both[:count, width:] = side
        both[count:, width:] = jnp.zeros((count, lanes), BF16)
        cot_out[:, width:] = jnp.zeros((count, 2 * lanes), BF16)
        for copy in copies:
            copy.wait()

    return stage(
        body,
        [(a, HBM) for a in (tokens, expert_ids.T, gate_probs.T, out_cot)],
        [
            ((count, width + lanes), BF16, VMEM),
            ((2 * count, width + lanes), BF16, VMEM),
            ((count, width + 2 * lanes), BF16, VMEM),
        ],
        scratch=[
            VMEM((top, count), jnp.int32),
            VMEM((top, count), F32),
            pltpu.SemaphoreType.DMA((6,)),
        ],
    )


def products(places, left, right, outs, own, tile=512):
    size = left.shape[0] // 4
    width = right.shape[1]
    blocks = [left[pl.ds(pl.multiple_of((own ^ m) * size, size), size), :] for m in places]
    rows = jnp.concatenate(blocks, axis=0)
    for start, some in chunks(width, tile):
        place = slice(start, start + some)
        part = jnp.dot(rows, right[:, place], preferred_element_type=F32)
        for i, out in enumerate(outs):
            out[:, place] = part[i * size : (i + 1) * size].astype(out.dtype)


TURNED = (((1,), (1,)), ((), ()))


def dense(tokens, expert_ids, gate_probs, out_cot, w_gate, w_up, w_down):
    count, width = tokens.shape
    ff = w_gate.shape[2]
    experts = lax.axis_size("expert")
    owners = lax.axis_size("dp")
    me = lax.axis_index("expert").astype(jnp.int32).reshape(1)
    mine = lax.axis_index("dp").astype(jnp.int32).reshape(1)
    total = count * experts
    half = total // 2
    pair = half // 2
    lanes = 128 * (-(-2 * experts // 128))
    odd_places, even_places = [3, 1], [2, 0]
    slab, band = ff // owners, width // owners

    near_bit, far_bit = 2, 4
    wide = width + lanes
    tok_own, both, cot_own, done = packed(tokens, expert_ids, gate_probs, out_cot, experts, lanes)
    tok_far = swap(tok_own, "expert", far_bit)
    tok_near = swap(tok_own, "expert", near_bit)
    next_both = swap(both, "expert", 1)
    cot_far = swap(cot_own, "expert", far_bit)

    def copied(sources, width, after, waits=()):
        rows = count * len(sources)

        def body(*refs):
            out = refs[-1]
            for i, (_, row) in enumerate(sources):
                out[i * count : (i + 1) * count, :] = refs[i][row : row + count, :width]

        return stage(
            body,
            [(a, VMEM) for a, _ in sources] + [(a, ANY) for a in waits],
            [((rows, width), BF16, VMEM)],
            after=after,
        )

    tok_pair, done = copied([(tok_near, 0), (tok_far, 0)], wide, [done])
    cot_here, done = copied([(both, count)], width, [done])
    cot_near = swap(cot_here, "expert", near_bit)
    tok_far_on, done = copied([(tok_far, 0)], wide, [done])
    next_tok_pair = swap(tok_pair, "expert", 1)
    tok_last = swap(tok_far_on, "expert", near_bit)
    tok_last_on, done = copied([(tok_last, 0)], wide, [done], [next_both, cot_far])
    next_tok_last = swap(tok_last_on, "expert", 1)
    cot_pair, done = copied([(cot_near, 0), (cot_far, 0)], width, [done])
    cot_far_on, done = copied([(cot_far, 0)], width, [done])
    next_cot_pair = swap(cot_pair, "expert", 1)
    cot_last = swap(cot_far_on, "expert", near_bit)
    tok_pieces = [(tok_own, 0), (tok_pair, count), (tok_pair, 0), (tok_last_on, 0)]
    tok_pieces += [(next_both, 0), (next_tok_pair, count), (next_tok_pair, 0), (next_tok_last, 0)]

    def refs_of(pieces):
        arrays = []
        for a, _ in pieces:
            if not any(a is b for b in arrays):
                arrays.append(a)
        where = [next(i for i, b in enumerate(arrays) if b is a) for a, _ in pieces]
        return arrays, [(i, row) for i, (_, row) in zip(where, pieces)]

    tok_arrays, tok_where = refs_of(tok_pieces)

    cot_last_on, done = copied([(cot_last, 0)], width, [done], [next_tok_last, next_tok_pair])
    next_cot_last = swap(cot_last_on, "expert", 1)
    cot_pieces = [(cot_here, 0), (cot_pair, count), (cot_pair, 0), (cot_last_on, 0)]
    cot_pieces += [(next_both, count), (next_cot_pair, count), (next_cot_pair, 0), (next_cot_last, 0)]

    def forward(me_ref, mine_ref, *refs):
        blocks = refs[: len(tok_arrays)]
        weights = refs[len(tok_arrays) : len(tok_arrays) + 3]
        flipped, flipped_sent, hidden_t, gate_by, up_by, kept, sent, gate, up, down = refs[
            len(tok_arrays) + 3 : len(tok_arrays) + 13
        ]
        rows, probs, hidden, gates, sems = refs[len(tok_arrays) + 13 :]
        copies = []
        for j, (far_ref, near_ref) in enumerate(zip(weights, (gate, up, down))):
            size = far_ref.shape[0] // 4
            for i in range(4):
                place = slice(i * size, (i + 1) * size)
                copies.append(
                    pltpu.make_async_copy(far_ref.at[place], near_ref.at[place], sems.at[4 * j + i])
                )
        for copy in copies:
            copy.start()
        own = me_ref[0]
        column = lax.broadcasted_iota(jnp.int32, (count, lanes), 1)
        chosen = (column == own) | (column == own + experts)
        for b, (i, row) in enumerate(tok_where):
            place = pl.ds(b * count, count)
            rows[place, :] = blocks[i][row : row + count, :width]
            side = jnp.where(chosen, blocks[i][row : row + count, width:].astype(F32), 0.0)
            probs[place, :] = jnp.sum(side, axis=1, keepdims=True)
        weight = probs[...]
        for out, places in ((flipped, even_places), (flipped_sent, odd_places)):
            for i, m in enumerate(places):
                start = pl.multiple_of((mine_ref[0] ^ m) * band, band)
                out[i * band : (i + 1) * band, :] = rows[:, pl.ds(start, band)].T
        for copy in copies[:4]:
            copy.wait()
        for start, size in chunks(ff, 256):
            place = slice(start, start + size)
            gates[:, place] = jnp.dot(rows[...], gate[:, place], preferred_element_type=F32)
        for copy in copies[4:8]:
            copy.wait()
        for start, size in chunks(ff, 256):
            place = slice(start, start + size)
            gate_pre = gates[:, place]
            up_pre = jnp.dot(rows[...], up[:, place], preferred_element_type=F32)
            sigma = jax.nn.sigmoid(gate_pre)
            silu = gate_pre * sigma
            scaled = weight * up_pre
            hidden[:, place] = (silu * scaled).astype(BF16)
            gate_by[:, place] = scaled * sigma * (1.0 + gate_pre * (1.0 - sigma))
            up_by[:, place] = weight * silu
            hidden_t[place, :] = hidden[:, place].T
        for copy in copies[8:]:
            copy.wait()
        for start, size in chunks(width, 512):
            place = slice(start, start + size)
            part = jnp.dot(hidden[...], down[:, place], preferred_element_type=F32).astype(BF16)
            kept[:, place] = part[:half]
            sent[:, place] = part[half:]

    (
        flipped, flipped_sent, hidden_t, gate_by, up_by, out_kept, out_sent,
        gate_near, up_near, down_near, done,
    ) = stage(
        forward,
        [(me, SMEM), (mine, SMEM)]
        + [(a, VMEM) for a in tok_arrays]
        + [(w[0], HBM) for w in (w_gate, w_up, w_down)],
        [
            ((width // 2, total), BF16, VMEM),
            ((width // 2, total), BF16, VMEM),
            ((ff, total), BF16, VMEM),
            ((total, ff), F32, VMEM),
            ((total, ff), F32, VMEM),
            ((half, width), BF16, VMEM),
            ((half, width), BF16, VMEM),
            ((width, ff), BF16, VMEM),
            ((width, ff), BF16, VMEM),
            ((ff, width), BF16, VMEM),
        ],
        scratch=[
            VMEM((total, width), BF16),
            VMEM((total, 1), F32),
            VMEM((total, ff), BF16),
            VMEM((total, ff), F32),
            pltpu.SemaphoreType.DMA((12,)),
        ],
        after=[done],
    )

    cot_arrays, cot_where = refs_of(cot_pieces)

    def down_first(own_ref, *refs):
        blocks = refs[: len(cot_arrays)]
        left, rows, away = refs[len(cot_arrays) :]
        for b, (i, row) in enumerate(cot_where):
            rows[b * count : (b + 1) * count, :] = blocks[i][row : row + count, :width]
        products([3], left, rows, [away], own_ref[0])

    cot_rows, down_away, done = stage(
        down_first,
        [(mine, SMEM)] + [(a, VMEM) for a in [*cot_arrays, hidden_t]],
        [((total, width), BF16, VMEM), ((slab, width), BF16, VMEM)],
        after=[done],
    )
    down_came = swap(down_away, "dp", 1)

    def down_rest(own_ref, left, cot, _, away, send, same):
        products([2, 1], left, cot, [send, away], own_ref[0])

    last_away, down_send, flipped_sent, done = stage(
        down_rest,
        [(mine, SMEM), (hidden_t, VMEM), (cot_rows, VMEM), (flipped_sent, ANY)],
        [((slab, width), BF16, VMEM)] * 2 + [(flipped_sent.shape, BF16, ANY)],
        after=[done],
        aliases={3: 2},
    )
    flipped_came = swap(flipped_sent, "dp", 1)
    last_came = swap(last_away, "dp", 1)
    out_came = swap(out_sent, "expert", 1)

    def backward(cot, down, gate_ref, up_ref, grads):
        for start, size in chunks(ff, 256):
            place = slice(start, start + size)
            grad = lax.dot_general(cot[...], down[place, :], TURNED, preferred_element_type=F32)
            grads[:, place] = (grad * gate_ref[:, place]).astype(BF16)
            grads[:, ff + start : ff + start + size] = (grad * up_ref[:, place]).astype(BF16)

    grads, done = stage(
        backward,
        [(a, VMEM) for a in (cot_rows, down_near, gate_by, up_by)],
        [((total, 2 * ff), BF16, VMEM)],
        after=[done],
    )
    grads_came = swap(grads, "dp", 1)

    def added(kept, came, _, send):
        send[...] = (kept[...].astype(F32) + came[...].astype(F32)).astype(BF16)

    down_send, done = stage(
        added,
        [(down_send, VMEM), (down_came, VMEM), (flipped_came, ANY)],
        [((slab, width), BF16, VMEM)],
        after=[done],
    )
    down_got = swap(down_send, "dp", 2)

    side = width // 2

    def input_rows(grad, gate, up, _, *outs):
        for start, size in chunks(width, 512):
            kept, sent = outs[2 * (start // side)], outs[2 * (start // side) + 1]
            place = slice(start, start + size)
            rows = lax.dot_general(grad[:, :ff], gate[place, :], TURNED, preferred_element_type=F32)
            rows = rows + lax.dot_general(
                grad[:, ff:], up[place, :], TURNED, preferred_element_type=F32
            )
            rows = rows.astype(BF16)
            there = slice(start % side, start % side + size)
            for i in range(2):
                low, high = slice(i * pair, (i + 1) * pair), i * half
                kept[low, there] = rows[high : high + pair]
                sent[low, there] = rows[high + pair : high + half]

    left_kept, left_sent, right_kept, right_sent, done = stage(
        input_rows,
        [(grads, VMEM), (gate_near, VMEM), (up_near, VMEM), (last_came, ANY)],
        [((half, side), BF16, VMEM)] * 4,
        after=[done],
    )
    left_came, right_came = [swap(a, "expert", near_bit) for a in (left_sent, right_sent)]

    cut = 3 * band // 4

    def both_parts(left, left_came, grad, grad_came, gate_send, up_high, up_low, gate_kept, up_kept):
        for j, (gate_out, up_out) in enumerate([(gate_send, None), (gate_kept, up_kept)]):
            row = slice(j * band, (j + 1) * band)
            for start, size in chunks(2 * ff, 256):
                column = slice(start, start + size)
                value = jnp.dot(left[row, :], grad[:, column], preferred_element_type=F32)
                value += jnp.dot(left_came[row, :], grad_came[:, column], preferred_element_type=F32)
                place = slice(start % ff, start % ff + size)
                if start < ff:
                    gate_out[:, place] = value.astype(gate_out.dtype)
                elif up_out is not None:
                    up_out[:, place] = value.astype(up_out.dtype)
                else:
                    up_high[:, place] = value[:cut].astype(BF16)
                    up_low[:, place] = value[cut:].astype(BF16)

    gate_send, up_high, up_low, gate_kept, up_kept, done = stage(
        both_parts,
        [(a, VMEM) for a in (flipped, flipped_came, grads, grads_came)],
        [((band, ff), BF16, VMEM)]
        + [((cut, ff), BF16, VMEM), ((band - cut, ff), BF16, VMEM)]
        + [((band, ff), F32, VMEM)] * 2,
        after=[done],
    )
    gate_got = swap(gate_send, "dp", 2)

    def down_own(own_ref, left, cot, kept):
        products([0], left, cot, [kept], own_ref[0])

    down_kept, done = stage(
        down_own,
        [(mine, SMEM), (hidden_t, VMEM), (cot_rows, VMEM)],
        [((slab, width), F32, VMEM)],
        after=[done],
    )

    def folded(held, came, after, waits=()):
        rows = held.shape[0]
        parts = 1 if rows == count else 2

        def body(a, b, *refs):
            for i, out in enumerate(refs[len(waits) :]):
                place = slice(i * rows // parts, (i + 1) * rows // parts)
                out[...] = (a[place, :].astype(F32) + b[place, :].astype(F32)).astype(BF16)

        return stage(
            body,
            [(held, VMEM), (came, VMEM)] + [(a, ANY) for a in waits],
            [((rows // parts, held.shape[1]), BF16, VMEM)] * parts,
            after=after,
        )

    def owned(parts, after, rows=None, into=None):
        size, wide = parts[-1].shape
        first = 0 if rows is None else rows
        full = parts[0].shape[0]
        step = size // 4
        n = len(parts)

        def body(*refs):
            out, total, sems = refs[-3:]
            copies = []
            for i in range(4):
                at = slice(i * step, (i + 1) * step)
                there = slice(first + i * step, first + (i + 1) * step)
                value = refs[0][there, :].astype(F32)
                for ref in refs[1:n]:
                    last = ref.shape[0] - size + i * step
                    value = value + ref[last : last + step, :].astype(F32)
                total[at, :] = value
                copies.append(pltpu.make_async_copy(total.at[at], out.at[there], sems.at[i]))
                copies[-1].start()
            for copy in copies:
                copy.wait()

        return stage(
            body,
            [(a, VMEM) for a in parts] + ([] if into is None else [(into, HBM)]),
            [((full, wide), F32, HBM)],
            scratch=[VMEM((size, wide), F32), pltpu.SemaphoreType.DMA((4,))],
            after=after,
            aliases=None if into is None else {n: 0},
        )

    def fold_on(held, came, bit, after, waits=()):
        held, send, done = folded(held, came, after, waits)
        return held, swap(send, "expert", bit), done

    def gated(a, after, waits=()):
        return stage(
            lambda *_: None,
            [(b, ANY) for b in (a, *waits)],
            [(a.shape, a.dtype, ANY)],
            after=after,
            aliases={0: 0},
        )

    left_held, left_came, done = fold_on(left_kept, left_came, 1, [done])
    down_grad, done = owned([down_kept, last_came, down_got], [done])
    out_held, out_came, done = fold_on(out_kept, out_came, near_bit, [done])
    right_held, right_came, done = fold_on(right_kept, right_came, 1, [done])
    left_held, left_came, done = fold_on(left_held, left_came, far_bit, [done])
    up_high, done = gated(up_high, [done])
    high_got = swap(up_high, "dp", 2)
    up_low, done = gated(up_low, [done], [left_came])
    low_got = swap(up_low, "dp", 2)
    right_held, right_came, done = fold_on(right_held, right_came, far_bit, [done])
    out_held, out_came, done = fold_on(out_held, out_came, far_bit, [done])

    def widened(a, b, c, d, out):
        out[:, :side] = (a[...].astype(F32) + b[...].astype(F32)).astype(BF16)
        out[:, side:] = (c[...].astype(F32) + d[...].astype(F32)).astype(BF16)

    gate_part, done = owned([gate_kept, gate_got], [done])
    layer_out, done = folded(out_held, out_came, [done])
    up_part, done = owned([up_kept, high_got], [done])
    input_grad, done = stage(
        widened,
        [(a, VMEM) for a in (left_held, left_came, right_held, right_came)],
        [((count, width), BF16, VMEM)],
        after=[done],
    )
    up_part, _ = owned([up_kept, low_got], [done], cut, up_part)
    return (layer_out, input_grad, gate_part[None], up_part[None], down_grad[None])


def shards(tokens, expert_ids, *rest):
    experts = lax.axis_size("expert")
    every = expert_ids.shape[1] == experts and experts == 8 and lax.axis_size("dp") == 4
    return (dense if every else routed)(tokens, expert_ids, *rest)


def solution(mesh):
    placed = (
        P(("dp", "expert"), None),
        P(("dp", "expert"), None),
        P(("dp", "expert"), None),
        P(("dp", "expert"), None),
        P("expert", None, None),
        P("expert", None, None),
        P("expert", None, None),
    )
    return jax.shard_map(
        shards,
        mesh=mesh,
        in_specs=placed,
        out_specs=(
            P(("dp", "expert"), None),
            P(("dp", "expert"), None),
            P("expert", "dp", None),
            P("expert", "dp", None),
            P("expert", "dp", None),
        ),
        check_vma=False,
    )
```

```python
import jax
import jax.numpy as jnp
from jax import lax
from jax.experimental import pallas as pl
from jax.experimental.pallas import tpu as pltpu
from jax.sharding import PartitionSpec as P


def contract_rows(left, right):
    return lax.dot_general(
        left, right, (((0,), (0,)), ((), ())), preferred_element_type=jnp.float32
    )


def contract_cols(left, right):
    return lax.dot_general(
        left, right, (((1,), (1,)), ((), ())), preferred_element_type=jnp.float32
    )


def routed(tokens, expert_ids, gate_probs, out_cot, w_gate, w_up, w_down):
    tok_count, width = tokens.shape
    top = expert_ids.shape[1]
    experts = lax.axis_size("expert")
    slots = min(tok_count, 4 * tok_count * top // (3 * experts))
    flat_ids = expert_ids.reshape(-1)
    onehot = (flat_ids[:, None] == jnp.arange(experts, dtype=jnp.int32)[None, :]).astype(jnp.int32)
    ranks = jnp.sum(jnp.cumsum(onehot, axis=0) * onehot, axis=1) - 1
    target = flat_ids * slots + ranks
    token_rows = jnp.repeat(tokens, top, axis=0)
    outbound = jnp.zeros((experts * slots, width), tokens.dtype).at[target].set(token_rows)
    outbound = outbound.reshape(experts, slots, width)
    gate_mat = w_gate[0]
    up_mat = w_up[0]
    down_mat = w_down[0]
    hidden_width = gate_mat.shape[1]
    arrived = lax.all_to_all(outbound, "expert", split_axis=0, concat_axis=0, tiled=True)
    sources = arrived.shape[0]
    count = arrived.shape[1]
    rows = arrived.reshape(-1, width)
    gate_pre = jnp.dot(rows, gate_mat, preferred_element_type=jnp.float32)
    up_pre = jnp.dot(rows, up_mat, preferred_element_type=jnp.float32)
    hidden = (gate_pre * jax.nn.sigmoid(gate_pre) * up_pre).astype(jnp.bfloat16)
    result = jnp.dot(hidden, down_mat, preferred_element_type=jnp.float32).astype(jnp.bfloat16)
    expert_out, hidden, gate_pre, up_pre, arrived = (
        result.reshape(sources, count, width),
        hidden.reshape(sources, count, hidden_width),
        gate_pre.reshape(sources, count, hidden_width),
        up_pre.reshape(sources, count, hidden_width),
        arrived,
    )
    returned = lax.all_to_all(expert_out, "expert", split_axis=0, concat_axis=0, tiled=True)
    picked = returned.reshape(-1, width)[target].reshape(tok_count, top, width)
    layer_out = jnp.sum(gate_probs[:, :, None] * picked.astype(jnp.float32), axis=1).astype(
        jnp.bfloat16
    )
    out_grad = (gate_probs[:, :, None] * out_cot[:, None, :].astype(jnp.float32)).astype(
        jnp.bfloat16
    )
    outbound_grad = (
        jnp.zeros((experts * slots, width), tokens.dtype)
        .at[target]
        .set(out_grad.reshape(-1, width))
    )
    arrived_grad = lax.all_to_all(
        outbound_grad.reshape(experts, slots, width),
        "expert",
        split_axis=0,
        concat_axis=0,
        tiled=True,
    ).reshape(-1, width)
    x_rows = arrived.reshape(-1, width)
    hidden_rows = hidden.reshape(-1, hidden_width)
    gate_rows = gate_pre.reshape(-1, hidden_width)
    up_rows = up_pre.reshape(-1, hidden_width)
    hidden_grad = contract_cols(arrived_grad, down_mat)
    sigma = jax.nn.sigmoid(gate_rows)
    gate_grad = (hidden_grad * up_rows * sigma * (1.0 + gate_rows * (1.0 - sigma))).astype(
        jnp.bfloat16
    )
    up_grad = (hidden_grad * gate_rows * sigma).astype(jnp.bfloat16)
    row_grad = (contract_cols(gate_grad, gate_mat) + contract_cols(up_grad, up_mat)).astype(
        jnp.bfloat16
    )
    back_grad = lax.all_to_all(
        row_grad.reshape(experts, slots, width), "expert", split_axis=0, concat_axis=0, tiled=True
    )
    gathered = back_grad.reshape(-1, width)[target].reshape(tok_count, top, width)
    input_grad = jnp.sum(gathered.astype(jnp.float32), axis=1).astype(jnp.bfloat16)
    down_grad = lax.psum_scatter(
        contract_rows(hidden_rows, arrived_grad).astype(jnp.bfloat16),
        "dp",
        scatter_dimension=0,
        tiled=True,
    ).astype(jnp.float32)
    gate_part = lax.psum_scatter(
        contract_rows(x_rows, gate_grad).astype(jnp.bfloat16), "dp", scatter_dimension=0, tiled=True
    ).astype(jnp.float32)
    up_part = lax.psum_scatter(
        contract_rows(x_rows, up_grad).astype(jnp.bfloat16), "dp", scatter_dimension=0, tiled=True
    ).astype(jnp.float32)
    return (layer_out, input_grad, gate_part[None], up_part[None], down_grad[None])


BF16, F32 = jnp.bfloat16, jnp.float32
VMEM, SMEM, HBM, ANY = pltpu.VMEM, pltpu.SMEM, pltpu.HBM, pl.ANY
ORDER = ((8, 128), jnp.float32, pltpu.VMEM)


def stage(body, ins, outs, after=(), scratch=(), aliases=None, vmem=8):
    skipped = len(after)
    given = skipped + len(ins)

    def kernel(*refs):
        token = refs[given + len(outs)]
        body(*refs[skipped : given + len(outs)], *refs[given + len(outs) + 1 :])
        token[...] = jnp.zeros(token.shape, token.dtype)

    outs_all = [*outs, ORDER]
    outputs = pl.pallas_call(
        kernel,
        in_specs=[pl.BlockSpec(memory_space=m) for m in [ANY] * skipped + [m for _, m in ins]],
        out_specs=[pl.BlockSpec(memory_space=m) for _, _, m in outs_all],
        out_shape=[jax.ShapeDtypeStruct(shape, dtype) for shape, dtype, _ in outs_all],
        scratch_shapes=list(scratch),
        input_output_aliases={skipped + i: o for i, o in (aliases or {}).items()},
        cost_estimate=pl.CostEstimate(flops=0, bytes_accessed=0, transcendentals=0),
        compiler_params=pltpu.CompilerParams(vmem_limit_bytes=vmem * 2**20),
    )(*after, *[pltpu.with_memory_space_constraint(a, HBM) if m is HBM else a for a, m in ins])
    return list(outputs)


def swap(value, axis, mask):
    size = lax.axis_size(axis)
    return lax.ppermute(value, axis, [(i, i ^ mask) for i in range(size)])


def chunks(width, most):
    return [(at, min(most, width - at)) for at in range(0, width, most)]


def packed(tokens, expert_ids, gate_probs, out_cot, experts, lanes):
    count, width = tokens.shape
    top = expert_ids.shape[1]

    def body(tok, ids_far, given_far, cot, alone, both, cot_out, ids, given, sems):
        copies = [
            pltpu.make_async_copy(tok, alone.at[:, :width], sems.at[0]),
            pltpu.make_async_copy(tok, both.at[:count, :width], sems.at[1]),
            pltpu.make_async_copy(cot, both.at[count:, :width], sems.at[2]),
            pltpu.make_async_copy(cot, cot_out.at[:, :width], sems.at[5]),
        ]
        small = [
            pltpu.make_async_copy(ids_far, ids, sems.at[3]),
            pltpu.make_async_copy(given_far, given, sems.at[4]),
        ]
        for copy in small + copies:
            copy.start()
        for copy in small:
            copy.wait()
        names = ids[...].T
        values = given[...].T
        column = lax.broadcasted_iota(jnp.int32, (count, lanes), 1)
        total = jnp.zeros((count, lanes), F32)
        for k in range(top):
            named = (names[:, k : k + 1] == column) | (names[:, k : k + 1] + experts == column)
            total = total + jnp.where(named, values[:, k : k + 1], 0.0)
        high = total.astype(BF16).astype(F32)
        side = jnp.where(column < experts, high, total - high).astype(BF16)
        alone[:, width:] = side
        both[:count, width:] = side
        both[count:, width:] = jnp.zeros((count, lanes), BF16)
        cot_out[:, width:] = jnp.zeros((count, 2 * lanes), BF16)
        for copy in copies:
            copy.wait()

    return stage(
        body,
        [(a, HBM) for a in (tokens, expert_ids.T, gate_probs.T, out_cot)],
        [
            ((count, width + lanes), BF16, VMEM),
            ((2 * count, width + lanes), BF16, VMEM),
            ((count, width + 2 * lanes), BF16, VMEM),
        ],
        scratch=[
            VMEM((top, count), jnp.int32),
            VMEM((top, count), F32),
            pltpu.SemaphoreType.DMA((6,)),
        ],
    )


def products(places, left, right, outs, own, tile=512):
    size = left.shape[0] // 4
    width = right.shape[1]
    blocks = [left[pl.ds(pl.multiple_of((own ^ m) * size, size), size), :] for m in places]
    rows = jnp.concatenate(blocks, axis=0)
    for start, some in chunks(width, tile):
        place = slice(start, start + some)
        part = jnp.dot(rows, right[:, place], preferred_element_type=F32)
        for i, out in enumerate(outs):
            out[:, place] = part[i * size : (i + 1) * size].astype(out.dtype)


TURNED = (((1,), (1,)), ((), ()))


def dense(tokens, expert_ids, gate_probs, out_cot, w_gate, w_up, w_down):
    count, width = tokens.shape
    ff = w_gate.shape[2]
    experts = lax.axis_size("expert")
    owners = lax.axis_size("dp")
    me = lax.axis_index("expert").astype(jnp.int32).reshape(1)
    mine = lax.axis_index("dp").astype(jnp.int32).reshape(1)
    total = count * experts
    half = total // 2
    pair = half // 2
    lanes = 128 * (-(-2 * experts // 128))
    odd_places, even_places = [3, 1], [2, 0]
    slab, band = ff // owners, width // owners

    near_bit, far_bit = 2, 4
    wide = width + lanes
    tok_own, both, cot_own, done = packed(tokens, expert_ids, gate_probs, out_cot, experts, lanes)
    tok_far = swap(tok_own, "expert", far_bit)
    tok_near = swap(tok_own, "expert", near_bit)
    next_both = swap(both, "expert", 1)

    def gated(a, after, waits=()):
        return stage(
            lambda *_: None,
            [(b, ANY) for b in (a, *waits)],
            [(a.shape, a.dtype, ANY)],
            after=after,
            aliases={0: 0},
        )

    def copied(sources, width, after, waits=()):
        rows = count * len(sources)

        def body(*refs):
            out = refs[-1]
            for i, (_, row) in enumerate(sources):
                out[i * count : (i + 1) * count, :] = refs[i][row : row + count, :width]

        return stage(
            body,
            [(a, VMEM) for a, _ in sources] + [(a, ANY) for a in waits],
            [((rows, width), BF16, VMEM)],
            after=after,
        )

    cot_own, done = gated(cot_own, [done], [tok_near])
    cot_far = swap(cot_own, "expert", far_bit)
    tok_pair, done = copied([(tok_near, 0), (tok_far, 0)], wide, [done])
    cot_here, done = copied([(both, count)], width, [done])
    cot_near = swap(cot_here, "expert", near_bit)
    tok_far_on, done = copied([(tok_far, 0)], wide, [done])
    next_tok_pair = swap(tok_pair, "expert", 1)
    tok_last = swap(tok_far_on, "expert", near_bit)
    tok_last_on, done = copied([(tok_last, 0)], wide, [done], [next_both, cot_far])
    next_tok_last = swap(tok_last_on, "expert", 1)
    cot_pair, done = copied([(cot_near, 0), (cot_far, 0)], width, [done])
    cot_far_on, done = copied([(cot_far, 0)], width, [done])
    next_cot_pair = swap(cot_pair, "expert", 1)
    cot_last = swap(cot_far_on, "expert", near_bit)
    tok_pieces = [(tok_own, 0), (tok_pair, count), (tok_pair, 0), (tok_last_on, 0)]
    tok_pieces += [(next_both, 0), (next_tok_pair, count), (next_tok_pair, 0), (next_tok_last, 0)]

    def refs_of(pieces):
        arrays = []
        for a, _ in pieces:
            if not any(a is b for b in arrays):
                arrays.append(a)
        where = [next(i for i, b in enumerate(arrays) if b is a) for a, _ in pieces]
        return arrays, [(i, row) for i, (_, row) in zip(where, pieces)]

    tok_arrays, tok_where = refs_of(tok_pieces)

    cot_last_on, done = copied([(cot_last, 0)], width, [done], [next_tok_last, next_tok_pair])
    next_cot_last = swap(cot_last_on, "expert", 1)
    cot_pieces = [(cot_here, 0), (cot_pair, count), (cot_pair, 0), (cot_last_on, 0)]
    cot_pieces += [(next_both, count), (next_cot_pair, count), (next_cot_pair, 0), (next_cot_last, 0)]

    def forward(me_ref, mine_ref, *refs):
        blocks = refs[: len(tok_arrays)]
        weights = refs[len(tok_arrays) : len(tok_arrays) + 3]
        flipped, flipped_sent, hidden_t, gate_by, up_by, kept, sent, gate, up, down = refs[
            len(tok_arrays) + 3 : len(tok_arrays) + 13
        ]
        rows, probs, hidden, gates, sems = refs[len(tok_arrays) + 13 :]
        copies = []
        for j, (far_ref, near_ref) in enumerate(zip(weights, (gate, up, down))):
            size = far_ref.shape[0] // 4
            for i in range(4):
                place = slice(i * size, (i + 1) * size)
                copies.append(
                    pltpu.make_async_copy(far_ref.at[place], near_ref.at[place], sems.at[4 * j + i])
                )
        for copy in copies:
            copy.start()
        own = me_ref[0]
        column = lax.broadcasted_iota(jnp.int32, (count, lanes), 1)
        chosen = (column == own) | (column == own + experts)
        for b, (i, row) in enumerate(tok_where):
            place = pl.ds(b * count, count)
            rows[place, :] = blocks[i][row : row + count, :width]
            side = jnp.where(chosen, blocks[i][row : row + count, width:].astype(F32), 0.0)
            probs[place, :] = jnp.sum(side, axis=1, keepdims=True)
        weight = probs[...]
        for out, places in ((flipped, even_places), (flipped_sent, odd_places)):
            for i, m in enumerate(places):
                start = pl.multiple_of((mine_ref[0] ^ m) * band, band)
                out[i * band : (i + 1) * band, :] = rows[:, pl.ds(start, band)].T
        for copy in copies[:4]:
            copy.wait()
        for start, size in chunks(ff, 256):
            place = slice(start, start + size)
            gates[:, place] = jnp.dot(rows[...], gate[:, place], preferred_element_type=F32)
        for copy in copies[4:8]:
            copy.wait()
        for start, size in chunks(ff, 256):
            place = slice(start, start + size)
            gate_pre = gates[:, place]
            up_pre = jnp.dot(rows[...], up[:, place], preferred_element_type=F32)
            sigma = jax.nn.sigmoid(gate_pre)
            silu = gate_pre * sigma
            scaled = weight * up_pre
            hidden[:, place] = (silu * scaled).astype(BF16)
            gate_by[:, place] = scaled * sigma * (1.0 + gate_pre * (1.0 - sigma))
            up_by[:, place] = weight * silu
            hidden_t[place, :] = hidden[:, place].T
        for copy in copies[8:]:
            copy.wait()
        for start, size in chunks(width, 512):
            place = slice(start, start + size)
            part = jnp.dot(hidden[...], down[:, place], preferred_element_type=F32).astype(BF16)
            kept[:, place] = part[:half]
            sent[:, place] = part[half:]

    (
        flipped, flipped_sent, hidden_t, gate_by, up_by, out_kept, out_sent,
        gate_near, up_near, down_near, done,
    ) = stage(
        forward,
        [(me, SMEM), (mine, SMEM)]
        + [(a, VMEM) for a in tok_arrays]
        + [(w[0], HBM) for w in (w_gate, w_up, w_down)],
        [
            ((width // 2, total), BF16, VMEM),
            ((width // 2, total), BF16, VMEM),
            ((ff, total), BF16, VMEM),
            ((total, ff), F32, VMEM),
            ((total, ff), F32, VMEM),
            ((half, width), BF16, VMEM),
            ((half, width), BF16, VMEM),
            ((width, ff), BF16, VMEM),
            ((width, ff), BF16, VMEM),
            ((ff, width), BF16, VMEM),
        ],
        scratch=[
            VMEM((total, width), BF16),
            VMEM((total, 1), F32),
            VMEM((total, ff), BF16),
            VMEM((total, ff), F32),
            pltpu.SemaphoreType.DMA((12,)),
        ],
        after=[done],
    )

    cot_arrays, cot_where = refs_of(cot_pieces)

    def down_first(own_ref, *refs):
        blocks = refs[: len(cot_arrays)]
        left, rows, away = refs[len(cot_arrays) :]
        for b, (i, row) in enumerate(cot_where):
            rows[b * count : (b + 1) * count, :] = blocks[i][row : row + count, :width]
        products([3], left, rows, [away], own_ref[0])

    cot_rows, down_away, done = stage(
        down_first,
        [(mine, SMEM)] + [(a, VMEM) for a in [*cot_arrays, hidden_t]],
        [((total, width), BF16, VMEM), ((slab, width), BF16, VMEM)],
        after=[done],
    )
    down_came = swap(down_away, "dp", 1)

    def down_rest(own_ref, left, cot, _, away, send, same):
        products([2, 1], left, cot, [send, away], own_ref[0])

    last_away, down_send, flipped_sent, done = stage(
        down_rest,
        [(mine, SMEM), (hidden_t, VMEM), (cot_rows, VMEM), (flipped_sent, ANY)],
        [((slab, width), BF16, VMEM)] * 2 + [(flipped_sent.shape, BF16, ANY)],
        after=[done],
        aliases={3: 2},
    )
    flipped_came = swap(flipped_sent, "dp", 1)
    last_came = swap(last_away, "dp", 1)
    out_came = swap(out_sent, "expert", 1)

    def backward(cot, down, gate_ref, up_ref, grads):
        for start, size in chunks(ff, 256):
            place = slice(start, start + size)
            grad = lax.dot_general(cot[...], down[place, :], TURNED, preferred_element_type=F32)
            grads[:, place] = (grad * gate_ref[:, place]).astype(BF16)
            grads[:, ff + start : ff + start + size] = (grad * up_ref[:, place]).astype(BF16)

    grads, done = stage(
        backward,
        [(a, VMEM) for a in (cot_rows, down_near, gate_by, up_by)],
        [((total, 2 * ff), BF16, VMEM)],
        after=[done],
    )
    grads_came = swap(grads, "dp", 1)

    def added(kept, came, _, send):
        send[...] = (kept[...].astype(F32) + came[...].astype(F32)).astype(BF16)

    down_send, done = stage(
        added,
        [(down_send, VMEM), (down_came, VMEM), (flipped_came, ANY)],
        [((slab, width), BF16, VMEM)],
        after=[done],
    )
    down_got = swap(down_send, "dp", 2)

    side = width // 2

    def input_rows(grad, gate, up, _, *outs):
        for start, size in chunks(width, 512):
            kept, sent = outs[2 * (start // side)], outs[2 * (start // side) + 1]
            place = slice(start, start + size)
            rows = lax.dot_general(grad[:, :ff], gate[place, :], TURNED, preferred_element_type=F32)
            rows = rows + lax.dot_general(
                grad[:, ff:], up[place, :], TURNED, preferred_element_type=F32
            )
            rows = rows.astype(BF16)
            there = slice(start % side, start % side + size)
            for i in range(2):
                low, high = slice(i * pair, (i + 1) * pair), i * half
                kept[low, there] = rows[high : high + pair]
                sent[low, there] = rows[high + pair : high + half]

    left_kept, left_sent, right_kept, right_sent, done = stage(
        input_rows,
        [(grads, VMEM), (gate_near, VMEM), (up_near, VMEM), (last_came, ANY)],
        [((half, side), BF16, VMEM)] * 4,
        after=[done],
    )
    left_came, right_came = [swap(a, "expert", near_bit) for a in (left_sent, right_sent)]

    cut = 3 * band // 4

    def both_parts(left, left_came, grad, grad_came, gate_send, up_high, up_low, gate_kept, up_kept):
        for j, (gate_out, up_out) in enumerate([(gate_send, None), (gate_kept, up_kept)]):
            row = slice(j * band, (j + 1) * band)
            for start, size in chunks(2 * ff, 256):
                column = slice(start, start + size)
                value = jnp.dot(left[row, :], grad[:, column], preferred_element_type=F32)
                value += jnp.dot(left_came[row, :], grad_came[:, column], preferred_element_type=F32)
                place = slice(start % ff, start % ff + size)
                if start < ff:
                    gate_out[:, place] = value.astype(gate_out.dtype)
                elif up_out is not None:
                    up_out[:, place] = value.astype(up_out.dtype)
                else:
                    up_high[:, place] = value[:cut].astype(BF16)
                    up_low[:, place] = value[cut:].astype(BF16)

    gate_send, up_high, up_low, gate_kept, up_kept, done = stage(
        both_parts,
        [(a, VMEM) for a in (flipped, flipped_came, grads, grads_came)],
        [((band, ff), BF16, VMEM)]
        + [((cut, ff), BF16, VMEM), ((band - cut, ff), BF16, VMEM)]
        + [((band, ff), F32, VMEM)] * 2,
        after=[done],
    )
    gate_got = swap(gate_send, "dp", 2)

    def down_own(own_ref, left, cot, kept):
        products([0], left, cot, [kept], own_ref[0])

    down_kept, done = stage(
        down_own,
        [(mine, SMEM), (hidden_t, VMEM), (cot_rows, VMEM)],
        [((slab, width), F32, VMEM)],
        after=[done],
    )

    def folded(held, came, after, waits=()):
        rows = held.shape[0]
        parts = 1 if rows == count else 2

        def body(a, b, *refs):
            for i, out in enumerate(refs[len(waits) :]):
                place = slice(i * rows // parts, (i + 1) * rows // parts)
                out[...] = (a[place, :].astype(F32) + b[place, :].astype(F32)).astype(BF16)

        return stage(
            body,
            [(held, VMEM), (came, VMEM)] + [(a, ANY) for a in waits],
            [((rows // parts, held.shape[1]), BF16, VMEM)] * parts,
            after=after,
        )

    def owned(parts, after, rows=None, into=None):
        size, wide = parts[-1].shape
        first = 0 if rows is None else rows
        full = parts[0].shape[0]
        step = size // 4
        n = len(parts)

        def body(*refs):
            out, total, sems = refs[-3:]
            copies = []
            for i in range(4):
                at = slice(i * step, (i + 1) * step)
                there = slice(first + i * step, first + (i + 1) * step)
                value = refs[0][there, :].astype(F32)
                for ref in refs[1:n]:
                    last = ref.shape[0] - size + i * step
                    value = value + ref[last : last + step, :].astype(F32)
                total[at, :] = value
                copies.append(pltpu.make_async_copy(total.at[at], out.at[there], sems.at[i]))
                copies[-1].start()
            for copy in copies:
                copy.wait()

        return stage(
            body,
            [(a, VMEM) for a in parts] + ([] if into is None else [(into, HBM)]),
            [((full, wide), F32, HBM)],
            scratch=[VMEM((size, wide), F32), pltpu.SemaphoreType.DMA((4,))],
            after=after,
            aliases=None if into is None else {n: 0},
        )

    def fold_on(held, came, bit, after, waits=()):
        held, send, done = folded(held, came, after, waits)
        return held, swap(send, "expert", bit), done

    left_held, left_came, done = fold_on(left_kept, left_came, 1, [done])
    down_grad, done = owned([down_kept, last_came, down_got], [done])
    out_held, out_came, done = fold_on(out_kept, out_came, near_bit, [done])
    right_held, right_came, done = fold_on(right_kept, right_came, 1, [done])
    left_held, left_came, done = fold_on(left_held, left_came, far_bit, [done])
    up_high, done = gated(up_high, [done])
    high_got = swap(up_high, "dp", 2)
    up_low, done = gated(up_low, [done], [left_came])
    low_got = swap(up_low, "dp", 2)
    right_held, right_came, done = fold_on(right_held, right_came, far_bit, [done])
    out_held, out_came, done = fold_on(out_held, out_came, far_bit, [done])

    def widened(a, b, c, d, out):
        out[:, :side] = (a[...].astype(F32) + b[...].astype(F32)).astype(BF16)
        out[:, side:] = (c[...].astype(F32) + d[...].astype(F32)).astype(BF16)

    gate_part, done = owned([gate_kept, gate_got], [done])
    layer_out, done = folded(out_held, out_came, [done])
    up_part, done = owned([up_kept, high_got], [done])
    input_grad, done = stage(
        widened,
        [(a, VMEM) for a in (left_held, left_came, right_held, right_came)],
        [((count, width), BF16, VMEM)],
        after=[done],
    )
    up_part, _ = owned([up_kept, low_got], [done], cut, up_part)
    return (layer_out, input_grad, gate_part[None], up_part[None], down_grad[None])


def shards(tokens, expert_ids, *rest):
    experts = lax.axis_size("expert")
    every = expert_ids.shape[1] == experts and experts == 8 and lax.axis_size("dp") == 4
    return (dense if every else routed)(tokens, expert_ids, *rest)


def solution(mesh):
    placed = (
        P(("dp", "expert"), None),
        P(("dp", "expert"), None),
        P(("dp", "expert"), None),
        P(("dp", "expert"), None),
        P("expert", None, None),
        P("expert", None, None),
        P("expert", None, None),
    )
    return jax.shard_map(
        shards,
        mesh=mesh,
        in_specs=placed,
        out_specs=(
            P(("dp", "expert"), None),
            P(("dp", "expert"), None),
            P("expert", "dp", None),
            P("expert", "dp", None),
            P("expert", "dp", None),
        ),
        check_vma=False,
    )
```

```python
import jax
import jax.numpy as jnp
from jax import lax
from jax.experimental import pallas as pl
from jax.experimental.pallas import tpu as pltpu
from jax.sharding import PartitionSpec as P


def contract_rows(left, right):
    return lax.dot_general(
        left, right, (((0,), (0,)), ((), ())), preferred_element_type=jnp.float32
    )


def contract_cols(left, right):
    return lax.dot_general(
        left, right, (((1,), (1,)), ((), ())), preferred_element_type=jnp.float32
    )


def routed(tokens, expert_ids, gate_probs, out_cot, w_gate, w_up, w_down):
    tok_count, width = tokens.shape
    top = expert_ids.shape[1]
    experts = lax.axis_size("expert")
    slots = min(tok_count, 4 * tok_count * top // (3 * experts))
    flat_ids = expert_ids.reshape(-1)
    onehot = (flat_ids[:, None] == jnp.arange(experts, dtype=jnp.int32)[None, :]).astype(jnp.int32)
    ranks = jnp.sum(jnp.cumsum(onehot, axis=0) * onehot, axis=1) - 1
    target = flat_ids * slots + ranks
    token_rows = jnp.repeat(tokens, top, axis=0)
    outbound = jnp.zeros((experts * slots, width), tokens.dtype).at[target].set(token_rows)
    outbound = outbound.reshape(experts, slots, width)
    gate_mat = w_gate[0]
    up_mat = w_up[0]
    down_mat = w_down[0]
    hidden_width = gate_mat.shape[1]
    arrived = lax.all_to_all(outbound, "expert", split_axis=0, concat_axis=0, tiled=True)
    sources = arrived.shape[0]
    count = arrived.shape[1]
    rows = arrived.reshape(-1, width)
    gate_pre = jnp.dot(rows, gate_mat, preferred_element_type=jnp.float32)
    up_pre = jnp.dot(rows, up_mat, preferred_element_type=jnp.float32)
    hidden = (gate_pre * jax.nn.sigmoid(gate_pre) * up_pre).astype(jnp.bfloat16)
    result = jnp.dot(hidden, down_mat, preferred_element_type=jnp.float32).astype(jnp.bfloat16)
    expert_out, hidden, gate_pre, up_pre, arrived = (
        result.reshape(sources, count, width),
        hidden.reshape(sources, count, hidden_width),
        gate_pre.reshape(sources, count, hidden_width),
        up_pre.reshape(sources, count, hidden_width),
        arrived,
    )
    returned = lax.all_to_all(expert_out, "expert", split_axis=0, concat_axis=0, tiled=True)
    picked = returned.reshape(-1, width)[target].reshape(tok_count, top, width)
    layer_out = jnp.sum(gate_probs[:, :, None] * picked.astype(jnp.float32), axis=1).astype(
        jnp.bfloat16
    )
    out_grad = (gate_probs[:, :, None] * out_cot[:, None, :].astype(jnp.float32)).astype(
        jnp.bfloat16
    )
    outbound_grad = (
        jnp.zeros((experts * slots, width), tokens.dtype)
        .at[target]
        .set(out_grad.reshape(-1, width))
    )
    arrived_grad = lax.all_to_all(
        outbound_grad.reshape(experts, slots, width),
        "expert",
        split_axis=0,
        concat_axis=0,
        tiled=True,
    ).reshape(-1, width)
    x_rows = arrived.reshape(-1, width)
    hidden_rows = hidden.reshape(-1, hidden_width)
    gate_rows = gate_pre.reshape(-1, hidden_width)
    up_rows = up_pre.reshape(-1, hidden_width)
    hidden_grad = contract_cols(arrived_grad, down_mat)
    sigma = jax.nn.sigmoid(gate_rows)
    gate_grad = (hidden_grad * up_rows * sigma * (1.0 + gate_rows * (1.0 - sigma))).astype(
        jnp.bfloat16
    )
    up_grad = (hidden_grad * gate_rows * sigma).astype(jnp.bfloat16)
    row_grad = (contract_cols(gate_grad, gate_mat) + contract_cols(up_grad, up_mat)).astype(
        jnp.bfloat16
    )
    back_grad = lax.all_to_all(
        row_grad.reshape(experts, slots, width), "expert", split_axis=0, concat_axis=0, tiled=True
    )
    gathered = back_grad.reshape(-1, width)[target].reshape(tok_count, top, width)
    input_grad = jnp.sum(gathered.astype(jnp.float32), axis=1).astype(jnp.bfloat16)
    down_grad = lax.psum_scatter(
        contract_rows(hidden_rows, arrived_grad).astype(jnp.bfloat16),
        "dp",
        scatter_dimension=0,
        tiled=True,
    ).astype(jnp.float32)
    gate_part = lax.psum_scatter(
        contract_rows(x_rows, gate_grad).astype(jnp.bfloat16), "dp", scatter_dimension=0, tiled=True
    ).astype(jnp.float32)
    up_part = lax.psum_scatter(
        contract_rows(x_rows, up_grad).astype(jnp.bfloat16), "dp", scatter_dimension=0, tiled=True
    ).astype(jnp.float32)
    return (layer_out, input_grad, gate_part[None], up_part[None], down_grad[None])


BF16, F32 = jnp.bfloat16, jnp.float32
VMEM, SMEM, HBM, ANY = pltpu.VMEM, pltpu.SMEM, pltpu.HBM, pl.ANY
ORDER = ((8, 128), jnp.float32, pltpu.VMEM)


def stage(body, ins, outs, after=(), scratch=(), aliases=None, vmem=8):
    skipped = len(after)
    given = skipped + len(ins)

    def kernel(*refs):
        token = refs[given + len(outs)]
        body(*refs[skipped : given + len(outs)], *refs[given + len(outs) + 1 :])
        token[...] = jnp.zeros(token.shape, token.dtype)

    outs_all = [*outs, ORDER]
    outputs = pl.pallas_call(
        kernel,
        in_specs=[pl.BlockSpec(memory_space=m) for m in [ANY] * skipped + [m for _, m in ins]],
        out_specs=[pl.BlockSpec(memory_space=m) for _, _, m in outs_all],
        out_shape=[jax.ShapeDtypeStruct(shape, dtype) for shape, dtype, _ in outs_all],
        scratch_shapes=list(scratch),
        input_output_aliases={skipped + i: o for i, o in (aliases or {}).items()},
        cost_estimate=pl.CostEstimate(flops=0, bytes_accessed=0, transcendentals=0),
        compiler_params=pltpu.CompilerParams(vmem_limit_bytes=vmem * 2**20),
    )(*after, *[pltpu.with_memory_space_constraint(a, HBM) if m is HBM else a for a, m in ins])
    return list(outputs)


def swap(value, axis, mask):
    size = lax.axis_size(axis)
    return lax.ppermute(value, axis, [(i, i ^ mask) for i in range(size)])


def chunks(width, most):
    return [(at, min(most, width - at)) for at in range(0, width, most)]


def packed(tokens, expert_ids, gate_probs, out_cot, experts, lanes):
    count, width = tokens.shape
    top = expert_ids.shape[1]

    def body(tok, ids_far, given_far, cot, alone, both, cot_out, ids, given, sems):
        copies = [
            pltpu.make_async_copy(tok, alone.at[:, :width], sems.at[0]),
            pltpu.make_async_copy(tok, both.at[:count, :width], sems.at[1]),
            pltpu.make_async_copy(cot, both.at[count:, :width], sems.at[2]),
            pltpu.make_async_copy(cot, cot_out.at[:, :width], sems.at[5]),
        ]
        small = [
            pltpu.make_async_copy(ids_far, ids, sems.at[3]),
            pltpu.make_async_copy(given_far, given, sems.at[4]),
        ]
        for copy in small + copies:
            copy.start()
        for copy in small:
            copy.wait()
        names = ids[...].T
        values = given[...].T
        column = lax.broadcasted_iota(jnp.int32, (count, lanes), 1)
        total = jnp.zeros((count, lanes), F32)
        for k in range(top):
            named = (names[:, k : k + 1] == column) | (names[:, k : k + 1] + experts == column)
            total = total + jnp.where(named, values[:, k : k + 1], 0.0)
        high = total.astype(BF16).astype(F32)
        side = jnp.where(column < experts, high, total - high).astype(BF16)
        alone[:, width:] = side
        both[:count, width:] = side
        both[count:, width:] = jnp.zeros((count, lanes), BF16)
        cot_out[:, width:] = jnp.zeros((count, 2 * lanes), BF16)
        for copy in copies:
            copy.wait()

    return stage(
        body,
        [(a, HBM) for a in (tokens, expert_ids.T, gate_probs.T, out_cot)],
        [
            ((count, width + lanes), BF16, VMEM),
            ((2 * count, width + lanes), BF16, VMEM),
            ((count, width + 2 * lanes), BF16, VMEM),
        ],
        scratch=[
            VMEM((top, count), jnp.int32),
            VMEM((top, count), F32),
            pltpu.SemaphoreType.DMA((6,)),
        ],
    )


def products(places, left, right, outs, own, tile=512):
    size = left.shape[0] // 4
    width = right.shape[1]
    blocks = [left[pl.ds(pl.multiple_of((own ^ m) * size, size), size), :] for m in places]
    rows = jnp.concatenate(blocks, axis=0)
    for start, some in chunks(width, tile):
        place = slice(start, start + some)
        part = jnp.dot(rows, right[:, place], preferred_element_type=F32)
        for i, out in enumerate(outs):
            out[:, place] = part[i * size : (i + 1) * size].astype(out.dtype)


TURNED = (((1,), (1,)), ((), ()))


def dense(tokens, expert_ids, gate_probs, out_cot, w_gate, w_up, w_down):
    count, width = tokens.shape
    ff = w_gate.shape[2]
    experts = lax.axis_size("expert")
    owners = lax.axis_size("dp")
    me = lax.axis_index("expert").astype(jnp.int32).reshape(1)
    mine = lax.axis_index("dp").astype(jnp.int32).reshape(1)
    total = count * experts
    half = total // 2
    pair = half // 2
    lanes = 128 * (-(-2 * experts // 128))
    odd_places, even_places = [3, 1], [2, 0]
    slab, band = ff // owners, width // owners

    near_bit, far_bit = 2, 4
    wide = width + lanes
    tok_own, both, cot_own, done = packed(tokens, expert_ids, gate_probs, out_cot, experts, lanes)
    tok_far = swap(tok_own, "expert", far_bit)
    tok_near = swap(tok_own, "expert", near_bit)
    next_both = swap(both, "expert", 1)

    def gated(a, after, waits=()):
        return stage(
            lambda *_: None,
            [(b, ANY) for b in (a, *waits)],
            [(a.shape, a.dtype, ANY)],
            after=after,
            aliases={0: 0},
        )

    def copied(sources, width, after, waits=()):
        rows = count * len(sources)

        def body(*refs):
            out = refs[-1]
            for i, (_, row) in enumerate(sources):
                out[i * count : (i + 1) * count, :] = refs[i][row : row + count, :width]

        return stage(
            body,
            [(a, VMEM) for a, _ in sources] + [(a, ANY) for a in waits],
            [((rows, width), BF16, VMEM)],
            after=after,
        )

    cot_own, done = gated(cot_own, [done], [tok_near])
    cot_far = swap(cot_own, "expert", far_bit)
    tok_pair, done = copied([(tok_near, 0), (tok_far, 0)], wide, [done])
    cot_here, done = copied([(both, count)], width, [done])
    cot_near = swap(cot_here, "expert", near_bit)
    tok_far_on, done = copied([(tok_far, 0)], wide, [done])
    next_tok_pair = swap(tok_pair, "expert", 1)
    tok_last = swap(tok_far_on, "expert", near_bit)
    tok_last_on, done = copied([(tok_last, 0)], wide, [done], [next_both, cot_far])
    next_tok_last = swap(tok_last_on, "expert", 1)
    cot_pair, done = copied([(cot_near, 0), (cot_far, 0)], width, [done])
    cot_far_on, done = copied([(cot_far, 0)], width, [done])
    next_cot_pair = swap(cot_pair, "expert", 1)
    cot_last = swap(cot_far_on, "expert", near_bit)
    tok_pieces = [(tok_own, 0), (tok_pair, count), (tok_pair, 0), (tok_last_on, 0)]
    tok_pieces += [(next_both, 0), (next_tok_pair, count), (next_tok_pair, 0), (next_tok_last, 0)]

    def refs_of(pieces):
        arrays = []
        for a, _ in pieces:
            if not any(a is b for b in arrays):
                arrays.append(a)
        where = [next(i for i, b in enumerate(arrays) if b is a) for a, _ in pieces]
        return arrays, [(i, row) for i, (_, row) in zip(where, pieces)]

    tok_arrays, tok_where = refs_of(tok_pieces)

    cot_last_on, done = copied([(cot_last, 0)], width, [done], [next_tok_last, next_tok_pair])
    next_cot_last = swap(cot_last_on, "expert", 1)
    cot_pieces = [(cot_here, 0), (cot_pair, count), (cot_pair, 0), (cot_last_on, 0)]
    cot_pieces += [(next_both, count), (next_cot_pair, count), (next_cot_pair, 0), (next_cot_last, 0)]

    def forward(me_ref, mine_ref, *refs):
        blocks = refs[: len(tok_arrays)]
        weights = refs[len(tok_arrays) : len(tok_arrays) + 3]
        flipped, flipped_sent, hidden_t, hidden, gate_by, up_by, gate, up, down = refs[
            len(tok_arrays) + 3 : len(tok_arrays) + 12
        ]
        rows, probs, gates, sems = refs[len(tok_arrays) + 12 :]
        copies = []
        for j, (far_ref, near_ref) in enumerate(zip(weights, (gate, up, down))):
            size = far_ref.shape[0] // 4
            for i in range(4):
                place = slice(i * size, (i + 1) * size)
                copies.append(
                    pltpu.make_async_copy(far_ref.at[place], near_ref.at[place], sems.at[4 * j + i])
                )
        for copy in copies:
            copy.start()
        own = me_ref[0]
        column = lax.broadcasted_iota(jnp.int32, (count, lanes), 1)
        chosen = (column == own) | (column == own + experts)
        for b, (i, row) in enumerate(tok_where):
            place = pl.ds(b * count, count)
            rows[place, :] = blocks[i][row : row + count, :width]
            side = jnp.where(chosen, blocks[i][row : row + count, width:].astype(F32), 0.0)
            probs[place, :] = jnp.sum(side, axis=1, keepdims=True)
        weight = probs[...]
        for out, places in ((flipped, even_places), (flipped_sent, odd_places)):
            for i, m in enumerate(places):
                start = pl.multiple_of((mine_ref[0] ^ m) * band, band)
                out[i * band : (i + 1) * band, :] = rows[:, pl.ds(start, band)].T
        for copy in copies[:4]:
            copy.wait()
        for start, size in chunks(ff, 256):
            place = slice(start, start + size)
            gates[:, place] = jnp.dot(rows[...], gate[:, place], preferred_element_type=F32)
        for copy in copies[4:8]:
            copy.wait()
        for start, size in chunks(ff, 256):
            place = slice(start, start + size)
            gate_pre = gates[:, place]
            up_pre = jnp.dot(rows[...], up[:, place], preferred_element_type=F32)
            sigma = jax.nn.sigmoid(gate_pre)
            silu = gate_pre * sigma
            scaled = weight * up_pre
            hidden[:, place] = (silu * scaled).astype(BF16)
            gate_by[:, place] = scaled * sigma * (1.0 + gate_pre * (1.0 - sigma))
            up_by[:, place] = weight * silu
            hidden_t[place, :] = hidden[:, place].T
        for copy in copies[8:]:
            copy.wait()

    (
        flipped, flipped_sent, hidden_t, hidden, gate_by, up_by, gate_near, up_near, down_near, done
    ) = stage(
        forward,
        [(me, SMEM), (mine, SMEM)]
        + [(a, VMEM) for a in tok_arrays]
        + [(w[0], HBM) for w in (w_gate, w_up, w_down)],
        [
            ((width // 2, total), BF16, VMEM),
            ((width // 2, total), BF16, VMEM),
            ((ff, total), BF16, VMEM),
            ((total, ff), BF16, VMEM),
            ((total, ff), F32, VMEM),
            ((total, ff), F32, VMEM),
            ((width, ff), BF16, VMEM),
            ((width, ff), BF16, VMEM),
            ((ff, width), BF16, VMEM),
        ],
        scratch=[
            VMEM((total, width), BF16),
            VMEM((total, 1), F32),
            VMEM((total, ff), F32),
            pltpu.SemaphoreType.DMA((12,)),
        ],
        after=[done],
    )

    cot_arrays, cot_where = refs_of(cot_pieces)

    def down_first(own_ref, *refs):
        blocks = refs[: len(cot_arrays)]
        left, rows, away = refs[len(cot_arrays) :]
        for b, (i, row) in enumerate(cot_where):
            rows[b * count : (b + 1) * count, :] = blocks[i][row : row + count, :width]
        products([3], left, rows, [away], own_ref[0])

    cot_rows, down_away, done = stage(
        down_first,
        [(mine, SMEM)] + [(a, VMEM) for a in [*cot_arrays, hidden_t]],
        [((total, width), BF16, VMEM), ((slab, width), BF16, VMEM)],
        after=[done],
    )
    down_came = swap(down_away, "dp", 1)

    def down_rest(own_ref, left, cot, _, away, send, same):
        products([2, 1], left, cot, [send, away], own_ref[0])

    last_away, down_send, flipped_sent, done = stage(
        down_rest,
        [(mine, SMEM), (hidden_t, VMEM), (cot_rows, VMEM), (flipped_sent, ANY)],
        [((slab, width), BF16, VMEM)] * 2 + [(flipped_sent.shape, BF16, ANY)],
        after=[done],
        aliases={3: 2},
    )
    flipped_came = swap(flipped_sent, "dp", 1)
    last_came = swap(last_away, "dp", 1)

    def backward(cot, down, gate_ref, up_ref, grads):
        for start, size in chunks(ff, 256):
            place = slice(start, start + size)
            grad = lax.dot_general(cot[...], down[place, :], TURNED, preferred_element_type=F32)
            grads[:, place] = (grad * gate_ref[:, place]).astype(BF16)
            grads[:, ff + start : ff + start + size] = (grad * up_ref[:, place]).astype(BF16)

    grads, done = stage(
        backward,
        [(a, VMEM) for a in (cot_rows, down_near, gate_by, up_by)],
        [((total, 2 * ff), BF16, VMEM)],
        after=[done],
    )
    grads_came = swap(grads, "dp", 1)

    def added(kept, came, _, send):
        send[...] = (kept[...].astype(F32) + came[...].astype(F32)).astype(BF16)

    down_send, done = stage(
        added,
        [(down_send, VMEM), (down_came, VMEM), (flipped_came, ANY)],
        [((slab, width), BF16, VMEM)],
        after=[done],
    )
    down_got = swap(down_send, "dp", 2)

    def output_rows(left, down, kept, sent):
        for start, size in chunks(width, 512):
            place = slice(start, start + size)
            part = jnp.dot(left[...], down[:, place], preferred_element_type=F32).astype(BF16)
            kept[:, place] = part[:half]
            sent[:, place] = part[half:]

    out_kept, out_sent, done = stage(
        output_rows,
        [(hidden, VMEM), (down_near, VMEM)],
        [((half, width), BF16, VMEM)] * 2,
        after=[done],
    )
    out_came = swap(out_sent, "expert", 1)

    side = width // 2

    def input_rows(grad, gate, up, _, *outs):
        for start, size in chunks(width, 512):
            kept, sent = outs[2 * (start // side)], outs[2 * (start // side) + 1]
            place = slice(start, start + size)
            rows = lax.dot_general(grad[:, :ff], gate[place, :], TURNED, preferred_element_type=F32)
            rows = rows + lax.dot_general(
                grad[:, ff:], up[place, :], TURNED, preferred_element_type=F32
            )
            rows = rows.astype(BF16)
            there = slice(start % side, start % side + size)
            for i in range(2):
                low, high = slice(i * pair, (i + 1) * pair), i * half
                kept[low, there] = rows[high : high + pair]
                sent[low, there] = rows[high + pair : high + half]

    left_kept, left_sent, right_kept, right_sent, done = stage(
        input_rows,
        [(grads, VMEM), (gate_near, VMEM), (up_near, VMEM), (last_came, ANY)],
        [((half, side), BF16, VMEM)] * 4,
        after=[done],
    )
    left_came, right_came = [swap(a, "expert", near_bit) for a in (left_sent, right_sent)]

    cut = 3 * band // 4

    def both_parts(left, left_came, grad, grad_came, gate_send, up_high, up_low, gate_kept, up_kept):
        for j, (gate_out, up_out) in enumerate([(gate_send, None), (gate_kept, up_kept)]):
            row = slice(j * band, (j + 1) * band)
            for start, size in chunks(2 * ff, 256):
                column = slice(start, start + size)
                value = jnp.dot(left[row, :], grad[:, column], preferred_element_type=F32)
                value += jnp.dot(left_came[row, :], grad_came[:, column], preferred_element_type=F32)
                place = slice(start % ff, start % ff + size)
                if start < ff:
                    gate_out[:, place] = value.astype(gate_out.dtype)
                elif up_out is not None:
                    up_out[:, place] = value.astype(up_out.dtype)
                else:
                    up_high[:, place] = value[:cut].astype(BF16)
                    up_low[:, place] = value[cut:].astype(BF16)

    gate_send, up_high, up_low, gate_kept, up_kept, done = stage(
        both_parts,
        [(a, VMEM) for a in (flipped, flipped_came, grads, grads_came)],
        [((band, ff), BF16, VMEM)]
        + [((cut, ff), BF16, VMEM), ((band - cut, ff), BF16, VMEM)]
        + [((band, ff), F32, VMEM)] * 2,
        after=[done],
    )
    gate_got = swap(gate_send, "dp", 2)

    def down_own(own_ref, left, cot, kept):
        products([0], left, cot, [kept], own_ref[0])

    down_kept, done = stage(
        down_own,
        [(mine, SMEM), (hidden_t, VMEM), (cot_rows, VMEM)],
        [((slab, width), F32, VMEM)],
        after=[done],
    )

    def folded(held, came, after, waits=()):
        rows = held.shape[0]
        parts = 1 if rows == count else 2

        def body(a, b, *refs):
            for i, out in enumerate(refs[len(waits) :]):
                place = slice(i * rows // parts, (i + 1) * rows // parts)
                out[...] = (a[place, :].astype(F32) + b[place, :].astype(F32)).astype(BF16)

        return stage(
            body,
            [(held, VMEM), (came, VMEM)] + [(a, ANY) for a in waits],
            [((rows // parts, held.shape[1]), BF16, VMEM)] * parts,
            after=after,
        )

    def owned(parts, after, rows=None, into=None):
        size, wide = parts[-1].shape
        first = 0 if rows is None else rows
        full = parts[0].shape[0]
        step = size // 4
        n = len(parts)

        def body(*refs):
            out, total, sems = refs[-3:]
            copies = []
            for i in range(4):
                at = slice(i * step, (i + 1) * step)
                there = slice(first + i * step, first + (i + 1) * step)
                value = refs[0][there, :].astype(F32)
                for ref in refs[1:n]:
                    last = ref.shape[0] - size + i * step
                    value = value + ref[last : last + step, :].astype(F32)
                total[at, :] = value
                copies.append(pltpu.make_async_copy(total.at[at], out.at[there], sems.at[i]))
                copies[-1].start()
            for copy in copies:
                copy.wait()

        return stage(
            body,
            [(a, VMEM) for a in parts] + ([] if into is None else [(into, HBM)]),
            [((full, wide), F32, HBM)],
            scratch=[VMEM((size, wide), F32), pltpu.SemaphoreType.DMA((4,))],
            after=after,
            aliases=None if into is None else {n: 0},
        )

    def fold_on(held, came, bit, after, waits=()):
        held, send, done = folded(held, came, after, waits)
        return held, swap(send, "expert", bit), done

    left_held, left_came, done = fold_on(left_kept, left_came, 1, [done])
    down_grad, done = owned([down_kept, last_came, down_got], [done])
    out_held, out_came, done = fold_on(out_kept, out_came, near_bit, [done])
    right_held, right_came, done = fold_on(right_kept, right_came, 1, [done])
    left_held, left_came, done = fold_on(left_held, left_came, far_bit, [done])
    up_high, done = gated(up_high, [done])
    high_got = swap(up_high, "dp", 2)
    up_low, done = gated(up_low, [done], [left_came])
    low_got = swap(up_low, "dp", 2)
    right_held, right_came, done = fold_on(right_held, right_came, far_bit, [done])
    out_held, out_came, done = fold_on(out_held, out_came, far_bit, [done])

    gate_part, done = owned([gate_kept, gate_got], [done])
    up_part, done = owned([up_kept, high_got], [done])

    def finished(kept, came, a, b, c, d, out, grad):
        out[...] = (kept[...].astype(F32) + came[...].astype(F32)).astype(BF16)
        grad[:, :side] = (a[...].astype(F32) + b[...].astype(F32)).astype(BF16)
        grad[:, side:] = (c[...].astype(F32) + d[...].astype(F32)).astype(BF16)

    layer_out, input_grad, done = stage(
        finished,
        [(a, VMEM) for a in (out_held, out_came, left_held, left_came, right_held, right_came)],
        [((count, width), BF16, VMEM)] * 2,
        after=[done],
    )
    up_part, _ = owned([up_kept, low_got], [done], cut, up_part)
    return (layer_out, input_grad, gate_part[None], up_part[None], down_grad[None])


def shards(tokens, expert_ids, *rest):
    experts = lax.axis_size("expert")
    every = expert_ids.shape[1] == experts and experts == 8 and lax.axis_size("dp") == 4
    return (dense if every else routed)(tokens, expert_ids, *rest)


def solution(mesh):
    placed = (
        P(("dp", "expert"), None),
        P(("dp", "expert"), None),
        P(("dp", "expert"), None),
        P(("dp", "expert"), None),
        P("expert", None, None),
        P("expert", None, None),
        P("expert", None, None),
    )
    return jax.shard_map(
        shards,
        mesh=mesh,
        in_specs=placed,
        out_specs=(
            P(("dp", "expert"), None),
            P(("dp", "expert"), None),
            P("expert", "dp", None),
            P("expert", "dp", None),
            P("expert", "dp", None),
        ),
        check_vma=False,
    )
```

```python
import jax
import jax.numpy as jnp
from jax import lax
from jax.experimental import pallas as pl
from jax.experimental.pallas import tpu as pltpu
from jax.sharding import PartitionSpec as P


def contract_rows(left, right):
    return lax.dot_general(
        left, right, (((0,), (0,)), ((), ())), preferred_element_type=jnp.float32
    )


def contract_cols(left, right):
    return lax.dot_general(
        left, right, (((1,), (1,)), ((), ())), preferred_element_type=jnp.float32
    )


def routed(tokens, expert_ids, gate_probs, out_cot, w_gate, w_up, w_down):
    tok_count, width = tokens.shape
    top = expert_ids.shape[1]
    experts = lax.axis_size("expert")
    slots = min(tok_count, 4 * tok_count * top // (3 * experts))
    flat_ids = expert_ids.reshape(-1)
    onehot = (flat_ids[:, None] == jnp.arange(experts, dtype=jnp.int32)[None, :]).astype(jnp.int32)
    ranks = jnp.sum(jnp.cumsum(onehot, axis=0) * onehot, axis=1) - 1
    target = flat_ids * slots + ranks
    token_rows = jnp.repeat(tokens, top, axis=0)
    outbound = jnp.zeros((experts * slots, width), tokens.dtype).at[target].set(token_rows)
    outbound = outbound.reshape(experts, slots, width)
    gate_mat = w_gate[0]
    up_mat = w_up[0]
    down_mat = w_down[0]
    hidden_width = gate_mat.shape[1]
    arrived = lax.all_to_all(outbound, "expert", split_axis=0, concat_axis=0, tiled=True)
    sources = arrived.shape[0]
    count = arrived.shape[1]
    rows = arrived.reshape(-1, width)
    gate_pre = jnp.dot(rows, gate_mat, preferred_element_type=jnp.float32)
    up_pre = jnp.dot(rows, up_mat, preferred_element_type=jnp.float32)
    hidden = (gate_pre * jax.nn.sigmoid(gate_pre) * up_pre).astype(jnp.bfloat16)
    result = jnp.dot(hidden, down_mat, preferred_element_type=jnp.float32).astype(jnp.bfloat16)
    expert_out, hidden, gate_pre, up_pre, arrived = (
        result.reshape(sources, count, width),
        hidden.reshape(sources, count, hidden_width),
        gate_pre.reshape(sources, count, hidden_width),
        up_pre.reshape(sources, count, hidden_width),
        arrived,
    )
    returned = lax.all_to_all(expert_out, "expert", split_axis=0, concat_axis=0, tiled=True)
    picked = returned.reshape(-1, width)[target].reshape(tok_count, top, width)
    layer_out = jnp.sum(gate_probs[:, :, None] * picked.astype(jnp.float32), axis=1).astype(
        jnp.bfloat16
    )
    out_grad = (gate_probs[:, :, None] * out_cot[:, None, :].astype(jnp.float32)).astype(
        jnp.bfloat16
    )
    outbound_grad = (
        jnp.zeros((experts * slots, width), tokens.dtype)
        .at[target]
        .set(out_grad.reshape(-1, width))
    )
    arrived_grad = lax.all_to_all(
        outbound_grad.reshape(experts, slots, width),
        "expert",
        split_axis=0,
        concat_axis=0,
        tiled=True,
    ).reshape(-1, width)
    x_rows = arrived.reshape(-1, width)
    hidden_rows = hidden.reshape(-1, hidden_width)
    gate_rows = gate_pre.reshape(-1, hidden_width)
    up_rows = up_pre.reshape(-1, hidden_width)
    hidden_grad = contract_cols(arrived_grad, down_mat)
    sigma = jax.nn.sigmoid(gate_rows)
    gate_grad = (hidden_grad * up_rows * sigma * (1.0 + gate_rows * (1.0 - sigma))).astype(
        jnp.bfloat16
    )
    up_grad = (hidden_grad * gate_rows * sigma).astype(jnp.bfloat16)
    row_grad = (contract_cols(gate_grad, gate_mat) + contract_cols(up_grad, up_mat)).astype(
        jnp.bfloat16
    )
    back_grad = lax.all_to_all(
        row_grad.reshape(experts, slots, width), "expert", split_axis=0, concat_axis=0, tiled=True
    )
    gathered = back_grad.reshape(-1, width)[target].reshape(tok_count, top, width)
    input_grad = jnp.sum(gathered.astype(jnp.float32), axis=1).astype(jnp.bfloat16)
    down_grad = lax.psum_scatter(
        contract_rows(hidden_rows, arrived_grad).astype(jnp.bfloat16),
        "dp",
        scatter_dimension=0,
        tiled=True,
    ).astype(jnp.float32)
    gate_part = lax.psum_scatter(
        contract_rows(x_rows, gate_grad).astype(jnp.bfloat16), "dp", scatter_dimension=0, tiled=True
    ).astype(jnp.float32)
    up_part = lax.psum_scatter(
        contract_rows(x_rows, up_grad).astype(jnp.bfloat16), "dp", scatter_dimension=0, tiled=True
    ).astype(jnp.float32)
    return (layer_out, input_grad, gate_part[None], up_part[None], down_grad[None])


BF16, F32 = jnp.bfloat16, jnp.float32
VMEM, SMEM, HBM, ANY = pltpu.VMEM, pltpu.SMEM, pltpu.HBM, pl.ANY
ORDER = ((8, 128), jnp.float32, pltpu.VMEM)


def stage(body, ins, outs, after=(), scratch=(), aliases=None, vmem=8):
    skipped = len(after)
    given = skipped + len(ins)

    def kernel(*refs):
        token = refs[given + len(outs)]
        body(*refs[skipped : given + len(outs)], *refs[given + len(outs) + 1 :])
        token[...] = jnp.zeros(token.shape, token.dtype)

    outs_all = [*outs, ORDER]
    outputs = pl.pallas_call(
        kernel,
        in_specs=[pl.BlockSpec(memory_space=m) for m in [ANY] * skipped + [m for _, m in ins]],
        out_specs=[pl.BlockSpec(memory_space=m) for _, _, m in outs_all],
        out_shape=[jax.ShapeDtypeStruct(shape, dtype) for shape, dtype, _ in outs_all],
        scratch_shapes=list(scratch),
        input_output_aliases={skipped + i: o for i, o in (aliases or {}).items()},
        cost_estimate=pl.CostEstimate(flops=0, bytes_accessed=0, transcendentals=0),
        compiler_params=pltpu.CompilerParams(vmem_limit_bytes=vmem * 2**20),
    )(*after, *[pltpu.with_memory_space_constraint(a, HBM) if m is HBM else a for a, m in ins])
    return list(outputs)


def swap(value, axis, mask):
    size = lax.axis_size(axis)
    return lax.ppermute(value, axis, [(i, i ^ mask) for i in range(size)])


def chunks(width, most):
    return [(at, min(most, width - at)) for at in range(0, width, most)]


def packed(tokens, expert_ids, gate_probs, out_cot, experts, lanes):
    count, width = tokens.shape
    top = expert_ids.shape[1]

    def body(tok, ids_far, given_far, cot, alone, both, cot_out, ids, given, sems):
        copies = [
            pltpu.make_async_copy(tok, alone.at[:, :width], sems.at[0]),
            pltpu.make_async_copy(tok, both.at[:count, :width], sems.at[1]),
            pltpu.make_async_copy(cot, both.at[count:, :width], sems.at[2]),
            pltpu.make_async_copy(cot, cot_out.at[:, :width], sems.at[5]),
        ]
        small = [
            pltpu.make_async_copy(ids_far, ids, sems.at[3]),
            pltpu.make_async_copy(given_far, given, sems.at[4]),
        ]
        for copy in small + copies:
            copy.start()
        for copy in small:
            copy.wait()
        names = ids[...].T
        values = given[...].T
        column = lax.broadcasted_iota(jnp.int32, (count, lanes), 1)
        total = jnp.zeros((count, lanes), F32)
        for k in range(top):
            named = (names[:, k : k + 1] == column) | (names[:, k : k + 1] + experts == column)
            total = total + jnp.where(named, values[:, k : k + 1], 0.0)
        high = total.astype(BF16).astype(F32)
        side = jnp.where(column < experts, high, total - high).astype(BF16)
        alone[:, width:] = side
        both[:count, width:] = side
        both[count:, width:] = jnp.zeros((count, lanes), BF16)
        cot_out[:, width:] = jnp.zeros((count, 2 * lanes), BF16)
        for copy in copies:
            copy.wait()

    return stage(
        body,
        [(a, HBM) for a in (tokens, expert_ids.T, gate_probs.T, out_cot)],
        [
            ((count, width + lanes), BF16, VMEM),
            ((2 * count, width + lanes), BF16, VMEM),
            ((count, width + 2 * lanes), BF16, VMEM),
        ],
        scratch=[
            VMEM((top, count), jnp.int32),
            VMEM((top, count), F32),
            pltpu.SemaphoreType.DMA((6,)),
        ],
    )


def products(places, left, right, outs, own, tile=512):
    size = left.shape[0] // 4
    width = right.shape[1]
    blocks = [left[pl.ds(pl.multiple_of((own ^ m) * size, size), size), :] for m in places]
    rows = jnp.concatenate(blocks, axis=0)
    for start, some in chunks(width, tile):
        place = slice(start, start + some)
        part = jnp.dot(rows, right[:, place], preferred_element_type=F32)
        for i, out in enumerate(outs):
            out[:, place] = part[i * size : (i + 1) * size].astype(out.dtype)


TURNED = (((1,), (1,)), ((), ()))


def dense(tokens, expert_ids, gate_probs, out_cot, w_gate, w_up, w_down):
    count, width = tokens.shape
    ff = w_gate.shape[2]
    experts = lax.axis_size("expert")
    owners = lax.axis_size("dp")
    me = lax.axis_index("expert").astype(jnp.int32).reshape(1)
    mine = lax.axis_index("dp").astype(jnp.int32).reshape(1)
    total = count * experts
    half = total // 2
    pair = half // 2
    lanes = 128 * (-(-2 * experts // 128))
    odd_places, even_places = [3, 1], [2, 0]
    slab, band = ff // owners, width // owners

    near_bit, far_bit = 2, 4
    wide = width + lanes
    tok_own, both, cot_own, done = packed(tokens, expert_ids, gate_probs, out_cot, experts, lanes)
    tok_far = swap(tok_own, "expert", far_bit)
    tok_near = swap(tok_own, "expert", near_bit)
    next_both = swap(both, "expert", 1)

    def gated(a, after, waits=()):
        return stage(
            lambda *_: None,
            [(b, ANY) for b in (a, *waits)],
            [(a.shape, a.dtype, ANY)],
            after=after,
            aliases={0: 0},
        )

    def copied(sources, width, after, waits=()):
        rows = count * len(sources)

        def body(*refs):
            out = refs[-1]
            for i, (_, row) in enumerate(sources):
                out[i * count : (i + 1) * count, :] = refs[i][row : row + count, :width]

        return stage(
            body,
            [(a, VMEM) for a, _ in sources] + [(a, ANY) for a in waits],
            [((rows, width), BF16, VMEM)],
            after=after,
        )

    cot_own, done = gated(cot_own, [done], [tok_near])
    cot_far = swap(cot_own, "expert", far_bit)
    tok_pair, done = copied([(tok_near, 0), (tok_far, 0)], wide, [done])
    cot_here, done = copied([(both, count)], width, [done])
    cot_near = swap(cot_here, "expert", near_bit)
    tok_far_on, done = copied([(tok_far, 0)], wide, [done])
    next_tok_pair = swap(tok_pair, "expert", 1)
    tok_last = swap(tok_far_on, "expert", near_bit)
    tok_last_on, done = copied([(tok_last, 0)], wide, [done], [next_both, cot_far])
    next_tok_last = swap(tok_last_on, "expert", 1)
    cot_pair, done = copied([(cot_near, 0), (cot_far, 0)], width, [done])
    cot_far_on, done = copied([(cot_far, 0)], width, [done])
    next_cot_pair = swap(cot_pair, "expert", 1)
    cot_last = swap(cot_far_on, "expert", near_bit)
    tok_pieces = [(tok_own, 0), (tok_pair, count), (tok_pair, 0), (tok_last_on, 0)]
    tok_pieces += [(next_both, 0), (next_tok_pair, count), (next_tok_pair, 0), (next_tok_last, 0)]

    def refs_of(pieces):
        arrays = []
        for a, _ in pieces:
            if not any(a is b for b in arrays):
                arrays.append(a)
        where = [next(i for i, b in enumerate(arrays) if b is a) for a, _ in pieces]
        return arrays, [(i, row) for i, (_, row) in zip(where, pieces)]

    tok_arrays, tok_where = refs_of(tok_pieces)

    cot_last_on, done = copied([(cot_last, 0)], width, [done], [next_tok_last, next_tok_pair])
    next_cot_last = swap(cot_last_on, "expert", 1)
    cot_pieces = [(cot_here, 0), (cot_pair, count), (cot_pair, 0), (cot_last_on, 0)]
    cot_pieces += [(next_both, count), (next_cot_pair, count), (next_cot_pair, 0), (next_cot_last, 0)]

    def forward(me_ref, mine_ref, *refs):
        blocks = refs[: len(tok_arrays)]
        weights = refs[len(tok_arrays) : len(tok_arrays) + 3]
        flipped, flipped_sent, hidden_t, hidden, gate_by, up_by, gate, up, down = refs[
            len(tok_arrays) + 3 : len(tok_arrays) + 12
        ]
        rows, probs, gates, sems = refs[len(tok_arrays) + 12 :]
        copies = []
        for j, (far_ref, near_ref) in enumerate(zip(weights, (gate, up, down))):
            size = far_ref.shape[0] // 4
            for i in range(4):
                place = slice(i * size, (i + 1) * size)
                copies.append(
                    pltpu.make_async_copy(far_ref.at[place], near_ref.at[place], sems.at[4 * j + i])
                )
        for copy in copies:
            copy.start()
        own = me_ref[0]
        column = lax.broadcasted_iota(jnp.int32, (count, lanes), 1)
        chosen = (column == own) | (column == own + experts)
        for b, (i, row) in enumerate(tok_where):
            place = pl.ds(b * count, count)
            rows[place, :] = blocks[i][row : row + count, :width]
            side = jnp.where(chosen, blocks[i][row : row + count, width:].astype(F32), 0.0)
            probs[place, :] = jnp.sum(side, axis=1, keepdims=True)
        weight = probs[...]
        for out, places in ((flipped, even_places), (flipped_sent, odd_places)):
            for i, m in enumerate(places):
                start = pl.multiple_of((mine_ref[0] ^ m) * band, band)
                out[i * band : (i + 1) * band, :] = rows[:, pl.ds(start, band)].T
        for copy in copies[:4]:
            copy.wait()
        for start, size in chunks(ff, 256):
            place = slice(start, start + size)
            gates[:, place] = jnp.dot(rows[...], gate[:, place], preferred_element_type=F32)
        for copy in copies[4:8]:
            copy.wait()
        for start, size in chunks(ff, 256):
            place = slice(start, start + size)
            gate_pre = gates[:, place]
            up_pre = jnp.dot(rows[...], up[:, place], preferred_element_type=F32)
            sigma = jax.nn.sigmoid(gate_pre)
            silu = gate_pre * sigma
            scaled = weight * up_pre
            hidden[:, place] = (silu * scaled).astype(BF16)
            gate_by[:, place] = scaled * sigma * (1.0 + gate_pre * (1.0 - sigma))
            up_by[:, place] = weight * silu
            hidden_t[place, :] = hidden[:, place].T
        for copy in copies[8:]:
            copy.wait()

    (
        flipped, flipped_sent, hidden_t, hidden, gate_by, up_by, gate_near, up_near, down_near, done
    ) = stage(
        forward,
        [(me, SMEM), (mine, SMEM)]
        + [(a, VMEM) for a in tok_arrays]
        + [(w[0], HBM) for w in (w_gate, w_up, w_down)],
        [
            ((width // 2, total), BF16, VMEM),
            ((width // 2, total), BF16, VMEM),
            ((ff, total), BF16, VMEM),
            ((total, ff), BF16, VMEM),
            ((total, ff), F32, VMEM),
            ((total, ff), F32, VMEM),
            ((width, ff), BF16, VMEM),
            ((width, ff), BF16, VMEM),
            ((ff, width), BF16, VMEM),
        ],
        scratch=[
            VMEM((total, width), BF16),
            VMEM((total, 1), F32),
            VMEM((total, ff), F32),
            pltpu.SemaphoreType.DMA((12,)),
        ],
        after=[done],
    )

    cot_arrays, cot_where = refs_of(cot_pieces)

    def down_first(own_ref, *refs):
        blocks = refs[: len(cot_arrays)]
        left, rows, away = refs[len(cot_arrays) :]
        for b, (i, row) in enumerate(cot_where):
            rows[b * count : (b + 1) * count, :] = blocks[i][row : row + count, :width]
        products([3], left, rows, [away], own_ref[0])

    cot_rows, down_away, done = stage(
        down_first,
        [(mine, SMEM)] + [(a, VMEM) for a in [*cot_arrays, hidden_t]],
        [((total, width), BF16, VMEM), ((slab, width), BF16, VMEM)],
        after=[done],
    )
    down_came = swap(down_away, "dp", 1)

    def down_rest(own_ref, left, cot, _, away, send, same):
        products([2, 1], left, cot, [send, away], own_ref[0])

    last_away, down_send, flipped_sent, done = stage(
        down_rest,
        [(mine, SMEM), (hidden_t, VMEM), (cot_rows, VMEM), (flipped_sent, ANY)],
        [((slab, width), BF16, VMEM)] * 2 + [(flipped_sent.shape, BF16, ANY)],
        after=[done],
        aliases={3: 2},
    )
    flipped_came = swap(flipped_sent, "dp", 1)
    last_came = swap(last_away, "dp", 1)

    def backward(cot, down, gate_ref, up_ref, grads):
        for start, size in chunks(ff, 256):
            place = slice(start, start + size)
            grad = lax.dot_general(cot[...], down[place, :], TURNED, preferred_element_type=F32)
            grads[:, place] = (grad * gate_ref[:, place]).astype(BF16)
            grads[:, ff + start : ff + start + size] = (grad * up_ref[:, place]).astype(BF16)

    grads, done = stage(
        backward,
        [(a, VMEM) for a in (cot_rows, down_near, gate_by, up_by)],
        [((total, 2 * ff), BF16, VMEM)],
        after=[done],
    )
    grads_came = swap(grads, "dp", 1)

    def added(kept, came, _, send):
        send[...] = (kept[...].astype(F32) + came[...].astype(F32)).astype(BF16)

    down_send, done = stage(
        added,
        [(down_send, VMEM), (down_came, VMEM), (flipped_came, ANY)],
        [((slab, width), BF16, VMEM)],
        after=[done],
    )
    down_got = swap(down_send, "dp", 2)

    def output_rows(left, down, kept, sent):
        for start, size in chunks(width, 512):
            place = slice(start, start + size)
            part = jnp.dot(left[...], down[:, place], preferred_element_type=F32).astype(BF16)
            kept[:, place] = part[:half]
            sent[:, place] = part[half:]

    out_kept, out_sent, done = stage(
        output_rows,
        [(hidden, VMEM), (down_near, VMEM)],
        [((half, width), BF16, VMEM)] * 2,
        after=[done],
    )
    out_came = swap(out_sent, "expert", 1)

    side = width // 2

    def input_rows(grad, gate, up, _, *outs):
        for start, size in chunks(width, 512):
            kept, sent = outs[2 * (start // side)], outs[2 * (start // side) + 1]
            place = slice(start, start + size)
            rows = lax.dot_general(grad[:, :ff], gate[place, :], TURNED, preferred_element_type=F32)
            rows = rows + lax.dot_general(
                grad[:, ff:], up[place, :], TURNED, preferred_element_type=F32
            )
            rows = rows.astype(BF16)
            there = slice(start % side, start % side + size)
            for i in range(2):
                low, high = slice(i * pair, (i + 1) * pair), i * half
                kept[low, there] = rows[high : high + pair]
                sent[low, there] = rows[high + pair : high + half]

    left_kept, left_sent, right_kept, right_sent, done = stage(
        input_rows,
        [(grads, VMEM), (gate_near, VMEM), (up_near, VMEM), (last_came, ANY)],
        [((half, side), BF16, VMEM)] * 4,
        after=[done],
    )
    left_came, right_came = [swap(a, "expert", near_bit) for a in (left_sent, right_sent)]

    cut = 5 * band // 8

    def both_parts(left, left_came, grad, grad_came, gate_send, up_high, up_low, gate_kept, up_kept):
        for j, (gate_out, up_out) in enumerate([(gate_send, None), (gate_kept, up_kept)]):
            row = slice(j * band, (j + 1) * band)
            for start, size in chunks(2 * ff, 256):
                column = slice(start, start + size)
                value = jnp.dot(left[row, :], grad[:, column], preferred_element_type=F32)
                value += jnp.dot(left_came[row, :], grad_came[:, column], preferred_element_type=F32)
                place = slice(start % ff, start % ff + size)
                if start < ff:
                    gate_out[:, place] = value.astype(gate_out.dtype)
                elif up_out is not None:
                    up_out[:, place] = value.astype(up_out.dtype)
                else:
                    up_high[:, place] = value[:cut].astype(BF16)
                    up_low[:, place] = value[cut:].astype(BF16)

    gate_send, up_high, up_low, gate_kept, up_kept, done = stage(
        both_parts,
        [(a, VMEM) for a in (flipped, flipped_came, grads, grads_came)],
        [((band, ff), BF16, VMEM)]
        + [((cut, ff), BF16, VMEM), ((band - cut, ff), BF16, VMEM)]
        + [((band, ff), F32, VMEM)] * 2,
        after=[done],
    )
    gate_got = swap(gate_send, "dp", 2)

    def down_own(own_ref, left, cot, kept):
        products([0], left, cot, [kept], own_ref[0])

    down_kept, done = stage(
        down_own,
        [(mine, SMEM), (hidden_t, VMEM), (cot_rows, VMEM)],
        [((slab, width), F32, VMEM)],
        after=[done],
    )

    def folded(held, came, after, waits=()):
        rows = held.shape[0]
        parts = 1 if rows == count else 2

        def body(a, b, *refs):
            for i, out in enumerate(refs[len(waits) :]):
                place = slice(i * rows // parts, (i + 1) * rows // parts)
                out[...] = (a[place, :].astype(F32) + b[place, :].astype(F32)).astype(BF16)

        return stage(
            body,
            [(held, VMEM), (came, VMEM)] + [(a, ANY) for a in waits],
            [((rows // parts, held.shape[1]), BF16, VMEM)] * parts,
            after=after,
        )

    def owned(parts, after, rows=None, into=None):
        size, wide = parts[-1].shape
        first = 0 if rows is None else rows
        full = parts[0].shape[0]
        step = size // 4
        n = len(parts)

        def body(*refs):
            out, total, sems = refs[-3:]
            copies = []
            for i in range(4):
                at = slice(i * step, (i + 1) * step)
                there = slice(first + i * step, first + (i + 1) * step)
                value = refs[0][there, :].astype(F32)
                for ref in refs[1:n]:
                    last = ref.shape[0] - size + i * step
                    value = value + ref[last : last + step, :].astype(F32)
                total[at, :] = value
                copies.append(pltpu.make_async_copy(total.at[at], out.at[there], sems.at[i]))
                copies[-1].start()
            for copy in copies:
                copy.wait()

        return stage(
            body,
            [(a, VMEM) for a in parts] + ([] if into is None else [(into, HBM)]),
            [((full, wide), F32, HBM)],
            scratch=[VMEM((size, wide), F32), pltpu.SemaphoreType.DMA((4,))],
            after=after,
            aliases=None if into is None else {n: 0},
        )

    def fold_on(held, came, bit, after, waits=()):
        held, send, done = folded(held, came, after, waits)
        return held, swap(send, "expert", bit), done

    left_held, left_came, done = fold_on(left_kept, left_came, 1, [done])
    down_grad, done = owned([down_kept, last_came, down_got], [done])
    out_held, out_came, done = fold_on(out_kept, out_came, near_bit, [done])
    right_held, right_came, done = fold_on(right_kept, right_came, 1, [done])
    left_held, left_came, done = fold_on(left_held, left_came, far_bit, [done])
    up_high, done = gated(up_high, [done])
    high_got = swap(up_high, "dp", 2)
    up_low, done = gated(up_low, [done], [left_came])
    low_got = swap(up_low, "dp", 2)
    right_held, right_came, done = fold_on(right_held, right_came, far_bit, [done])
    out_held, out_came, done = fold_on(out_held, out_came, far_bit, [done])

    gate_part, done = owned([gate_kept, gate_got], [done])
    up_part, done = owned([up_kept, high_got], [done])

    def finished(kept, came, a, b, c, d, out, grad):
        out[...] = (kept[...].astype(F32) + came[...].astype(F32)).astype(BF16)
        grad[:, :side] = (a[...].astype(F32) + b[...].astype(F32)).astype(BF16)
        grad[:, side:] = (c[...].astype(F32) + d[...].astype(F32)).astype(BF16)

    layer_out, input_grad, done = stage(
        finished,
        [(a, VMEM) for a in (out_held, out_came, left_held, left_came, right_held, right_came)],
        [((count, width), BF16, VMEM)] * 2,
        after=[done],
    )
    up_part, _ = owned([up_kept, low_got], [done], cut, up_part)
    return (layer_out, input_grad, gate_part[None], up_part[None], down_grad[None])


def shards(tokens, expert_ids, *rest):
    experts = lax.axis_size("expert")
    every = expert_ids.shape[1] == experts and experts == 8 and lax.axis_size("dp") == 4
    return (dense if every else routed)(tokens, expert_ids, *rest)


def solution(mesh):
    placed = (
        P(("dp", "expert"), None),
        P(("dp", "expert"), None),
        P(("dp", "expert"), None),
        P(("dp", "expert"), None),
        P("expert", None, None),
        P("expert", None, None),
        P("expert", None, None),
    )
    return jax.shard_map(
        shards,
        mesh=mesh,
        in_specs=placed,
        out_specs=(
            P(("dp", "expert"), None),
            P(("dp", "expert"), None),
            P("expert", "dp", None),
            P("expert", "dp", None),
            P("expert", "dp", None),
        ),
        check_vma=False,
    )
```

```python
import jax
import jax.numpy as jnp
from jax import lax
from jax.experimental import pallas as pl
from jax.experimental.pallas import tpu as pltpu
from jax.sharding import PartitionSpec as P


def contract_rows(left, right):
    return lax.dot_general(
        left, right, (((0,), (0,)), ((), ())), preferred_element_type=jnp.float32
    )


def contract_cols(left, right):
    return lax.dot_general(
        left, right, (((1,), (1,)), ((), ())), preferred_element_type=jnp.float32
    )


def routed(tokens, expert_ids, gate_probs, out_cot, w_gate, w_up, w_down):
    tok_count, width = tokens.shape
    top = expert_ids.shape[1]
    experts = lax.axis_size("expert")
    slots = min(tok_count, 4 * tok_count * top // (3 * experts))
    flat_ids = expert_ids.reshape(-1)
    onehot = (flat_ids[:, None] == jnp.arange(experts, dtype=jnp.int32)[None, :]).astype(jnp.int32)
    ranks = jnp.sum(jnp.cumsum(onehot, axis=0) * onehot, axis=1) - 1
    target = flat_ids * slots + ranks
    token_rows = jnp.repeat(tokens, top, axis=0)
    outbound = jnp.zeros((experts * slots, width), tokens.dtype).at[target].set(token_rows)
    outbound = outbound.reshape(experts, slots, width)
    gate_mat = w_gate[0]
    up_mat = w_up[0]
    down_mat = w_down[0]
    hidden_width = gate_mat.shape[1]
    arrived = lax.all_to_all(outbound, "expert", split_axis=0, concat_axis=0, tiled=True)
    sources = arrived.shape[0]
    count = arrived.shape[1]
    rows = arrived.reshape(-1, width)
    gate_pre = jnp.dot(rows, gate_mat, preferred_element_type=jnp.float32)
    up_pre = jnp.dot(rows, up_mat, preferred_element_type=jnp.float32)
    hidden = (gate_pre * jax.nn.sigmoid(gate_pre) * up_pre).astype(jnp.bfloat16)
    result = jnp.dot(hidden, down_mat, preferred_element_type=jnp.float32).astype(jnp.bfloat16)
    expert_out, hidden, gate_pre, up_pre, arrived = (
        result.reshape(sources, count, width),
        hidden.reshape(sources, count, hidden_width),
        gate_pre.reshape(sources, count, hidden_width),
        up_pre.reshape(sources, count, hidden_width),
        arrived,
    )
    returned = lax.all_to_all(expert_out, "expert", split_axis=0, concat_axis=0, tiled=True)
    picked = returned.reshape(-1, width)[target].reshape(tok_count, top, width)
    layer_out = jnp.sum(gate_probs[:, :, None] * picked.astype(jnp.float32), axis=1).astype(
        jnp.bfloat16
    )
    out_grad = (gate_probs[:, :, None] * out_cot[:, None, :].astype(jnp.float32)).astype(
        jnp.bfloat16
    )
    outbound_grad = (
        jnp.zeros((experts * slots, width), tokens.dtype)
        .at[target]
        .set(out_grad.reshape(-1, width))
    )
    arrived_grad = lax.all_to_all(
        outbound_grad.reshape(experts, slots, width),
        "expert",
        split_axis=0,
        concat_axis=0,
        tiled=True,
    ).reshape(-1, width)
    x_rows = arrived.reshape(-1, width)
    hidden_rows = hidden.reshape(-1, hidden_width)
    gate_rows = gate_pre.reshape(-1, hidden_width)
    up_rows = up_pre.reshape(-1, hidden_width)
    hidden_grad = contract_cols(arrived_grad, down_mat)
    sigma = jax.nn.sigmoid(gate_rows)
    gate_grad = (hidden_grad * up_rows * sigma * (1.0 + gate_rows * (1.0 - sigma))).astype(
        jnp.bfloat16
    )
    up_grad = (hidden_grad * gate_rows * sigma).astype(jnp.bfloat16)
    row_grad = (contract_cols(gate_grad, gate_mat) + contract_cols(up_grad, up_mat)).astype(
        jnp.bfloat16
    )
    back_grad = lax.all_to_all(
        row_grad.reshape(experts, slots, width), "expert", split_axis=0, concat_axis=0, tiled=True
    )
    gathered = back_grad.reshape(-1, width)[target].reshape(tok_count, top, width)
    input_grad = jnp.sum(gathered.astype(jnp.float32), axis=1).astype(jnp.bfloat16)
    down_grad = lax.psum_scatter(
        contract_rows(hidden_rows, arrived_grad).astype(jnp.bfloat16),
        "dp",
        scatter_dimension=0,
        tiled=True,
    ).astype(jnp.float32)
    gate_part = lax.psum_scatter(
        contract_rows(x_rows, gate_grad).astype(jnp.bfloat16), "dp", scatter_dimension=0, tiled=True
    ).astype(jnp.float32)
    up_part = lax.psum_scatter(
        contract_rows(x_rows, up_grad).astype(jnp.bfloat16), "dp", scatter_dimension=0, tiled=True
    ).astype(jnp.float32)
    return (layer_out, input_grad, gate_part[None], up_part[None], down_grad[None])


BF16, F32 = jnp.bfloat16, jnp.float32
VMEM, SMEM, HBM, ANY = pltpu.VMEM, pltpu.SMEM, pltpu.HBM, pl.ANY
ORDER = ((8, 128), jnp.float32, pltpu.VMEM)


def stage(body, ins, outs, after=(), scratch=(), aliases=None, vmem=8):
    skipped = len(after)
    given = skipped + len(ins)

    def kernel(*refs):
        token = refs[given + len(outs)]
        body(*refs[skipped : given + len(outs)], *refs[given + len(outs) + 1 :])
        token[...] = jnp.zeros(token.shape, token.dtype)

    outs_all = [*outs, ORDER]
    outputs = pl.pallas_call(
        kernel,
        in_specs=[pl.BlockSpec(memory_space=m) for m in [ANY] * skipped + [m for _, m in ins]],
        out_specs=[pl.BlockSpec(memory_space=m) for _, _, m in outs_all],
        out_shape=[jax.ShapeDtypeStruct(shape, dtype) for shape, dtype, _ in outs_all],
        scratch_shapes=list(scratch),
        input_output_aliases={skipped + i: o for i, o in (aliases or {}).items()},
        cost_estimate=pl.CostEstimate(flops=0, bytes_accessed=0, transcendentals=0),
        compiler_params=pltpu.CompilerParams(vmem_limit_bytes=vmem * 2**20),
    )(*after, *[pltpu.with_memory_space_constraint(a, HBM) if m is HBM else a for a, m in ins])
    return list(outputs)


def swap(value, axis, mask):
    size = lax.axis_size(axis)
    return lax.ppermute(value, axis, [(i, i ^ mask) for i in range(size)])


def chunks(width, most):
    return [(at, min(most, width - at)) for at in range(0, width, most)]


def packed(tokens, expert_ids, gate_probs, out_cot, experts, lanes):
    count, width = tokens.shape
    top = expert_ids.shape[1]

    def body(tok, ids_far, given_far, cot, alone, both, cot_out, ids, given, sems):
        copies = [
            pltpu.make_async_copy(tok, alone.at[:, :width], sems.at[0]),
            pltpu.make_async_copy(tok, both.at[:count, :width], sems.at[1]),
            pltpu.make_async_copy(cot, both.at[count:, :width], sems.at[2]),
            pltpu.make_async_copy(cot, cot_out.at[:, :width], sems.at[5]),
        ]
        small = [
            pltpu.make_async_copy(ids_far, ids, sems.at[3]),
            pltpu.make_async_copy(given_far, given, sems.at[4]),
        ]
        for copy in small + copies:
            copy.start()
        for copy in small:
            copy.wait()
        names = ids[...].T
        values = given[...].T
        column = lax.broadcasted_iota(jnp.int32, (count, lanes), 1)
        total = jnp.zeros((count, lanes), F32)
        for k in range(top):
            named = (names[:, k : k + 1] == column) | (names[:, k : k + 1] + experts == column)
            total = total + jnp.where(named, values[:, k : k + 1], 0.0)
        high = total.astype(BF16).astype(F32)
        side = jnp.where(column < experts, high, total - high).astype(BF16)
        alone[:, width:] = side
        both[:count, width:] = side
        both[count:, width:] = jnp.zeros((count, lanes), BF16)
        cot_out[:, width:] = jnp.zeros((count, 2 * lanes), BF16)
        for copy in copies:
            copy.wait()

    return stage(
        body,
        [(a, HBM) for a in (tokens, expert_ids.T, gate_probs.T, out_cot)],
        [
            ((count, width + lanes), BF16, VMEM),
            ((2 * count, width + lanes), BF16, VMEM),
            ((count, width + 2 * lanes), BF16, VMEM),
        ],
        scratch=[
            VMEM((top, count), jnp.int32),
            VMEM((top, count), F32),
            pltpu.SemaphoreType.DMA((6,)),
        ],
    )


def products(places, left, right, outs, own, tile=512):
    size = left.shape[0] // 4
    width = right.shape[1]
    blocks = [left[pl.ds(pl.multiple_of((own ^ m) * size, size), size), :] for m in places]
    rows = jnp.concatenate(blocks, axis=0)
    for start, some in chunks(width, tile):
        place = slice(start, start + some)
        part = jnp.dot(rows, right[:, place], preferred_element_type=F32)
        for i, out in enumerate(outs):
            out[:, place] = part[i * size : (i + 1) * size].astype(out.dtype)


TURNED = (((1,), (1,)), ((), ()))


def dense(tokens, expert_ids, gate_probs, out_cot, w_gate, w_up, w_down):
    count, width = tokens.shape
    ff = w_gate.shape[2]
    experts = lax.axis_size("expert")
    owners = lax.axis_size("dp")
    me = lax.axis_index("expert").astype(jnp.int32).reshape(1)
    mine = lax.axis_index("dp").astype(jnp.int32).reshape(1)
    total = count * experts
    half = total // 2
    pair = half // 2
    lanes = 128 * (-(-2 * experts // 128))
    odd_places, even_places = [3, 1], [2, 0]
    slab, band = ff // owners, width // owners

    near_bit, far_bit = 2, 4
    wide = width + lanes
    tok_own, both, cot_own, done = packed(tokens, expert_ids, gate_probs, out_cot, experts, lanes)
    tok_far = swap(tok_own, "expert", far_bit)
    tok_near = swap(tok_own, "expert", near_bit)
    next_both = swap(both, "expert", 1)

    def gated(a, after, waits=()):
        return stage(
            lambda *_: None,
            [(b, ANY) for b in (a, *waits)],
            [(a.shape, a.dtype, ANY)],
            after=after,
            aliases={0: 0},
        )

    def copied(sources, width, after, waits=()):
        rows = count * len(sources)

        def body(*refs):
            out = refs[-1]
            for i, (_, row) in enumerate(sources):
                out[i * count : (i + 1) * count, :] = refs[i][row : row + count, :width]

        return stage(
            body,
            [(a, VMEM) for a, _ in sources] + [(a, ANY) for a in waits],
            [((rows, width), BF16, VMEM)],
            after=after,
        )

    cot_own, done = gated(cot_own, [done], [tok_near])
    cot_far = swap(cot_own, "expert", far_bit)
    tok_pair, done = copied([(tok_near, 0), (tok_far, 0)], wide, [done])
    cot_here, done = copied([(both, count)], width, [done])
    cot_near = swap(cot_here, "expert", near_bit)
    tok_far_on, done = copied([(tok_far, 0)], wide, [done])
    next_tok_pair = swap(tok_pair, "expert", 1)
    tok_last = swap(tok_far_on, "expert", near_bit)
    tok_last_on, done = copied([(tok_last, 0)], wide, [done], [next_both, cot_far])
    next_tok_last = swap(tok_last_on, "expert", 1)
    cot_pair, done = copied([(cot_near, 0), (cot_far, 0)], width, [done])
    cot_far_on, done = copied([(cot_far, 0)], width, [done])
    next_cot_pair = swap(cot_pair, "expert", 1)
    cot_last = swap(cot_far_on, "expert", near_bit)
    tok_pieces = [(tok_own, 0), (tok_pair, count), (tok_pair, 0), (tok_last_on, 0)]
    tok_pieces += [(next_both, 0), (next_tok_pair, count), (next_tok_pair, 0), (next_tok_last, 0)]

    def refs_of(pieces):
        arrays = []
        for a, _ in pieces:
            if not any(a is b for b in arrays):
                arrays.append(a)
        where = [next(i for i, b in enumerate(arrays) if b is a) for a, _ in pieces]
        return arrays, [(i, row) for i, (_, row) in zip(where, pieces)]

    tok_arrays, tok_where = refs_of(tok_pieces)

    cot_last_on, done = copied([(cot_last, 0)], width, [done], [next_tok_last, next_tok_pair])
    next_cot_last = swap(cot_last_on, "expert", 1)
    cot_pieces = [(cot_here, 0), (cot_pair, count), (cot_pair, 0), (cot_last_on, 0)]
    cot_pieces += [(next_both, count), (next_cot_pair, count), (next_cot_pair, 0), (next_cot_last, 0)]

    def forward(me_ref, mine_ref, *refs):
        blocks = refs[: len(tok_arrays)]
        weights = refs[len(tok_arrays) : len(tok_arrays) + 3]
        flipped, flipped_sent, hidden_t, hidden, gate_by, up_by, gate, up, down = refs[
            len(tok_arrays) + 3 : len(tok_arrays) + 12
        ]
        rows, probs, gates, sems = refs[len(tok_arrays) + 12 :]
        copies = []
        for j, (far_ref, near_ref) in enumerate(zip(weights, (gate, up, down))):
            size = far_ref.shape[0] // 4
            for i in range(4):
                place = slice(i * size, (i + 1) * size)
                copies.append(
                    pltpu.make_async_copy(far_ref.at[place], near_ref.at[place], sems.at[4 * j + i])
                )
        for copy in copies:
            copy.start()
        own = me_ref[0]
        column = lax.broadcasted_iota(jnp.int32, (count, lanes), 1)
        chosen = (column == own) | (column == own + experts)
        for b, (i, row) in enumerate(tok_where):
            place = pl.ds(b * count, count)
            rows[place, :] = blocks[i][row : row + count, :width]
            side = jnp.where(chosen, blocks[i][row : row + count, width:].astype(F32), 0.0)
            probs[place, :] = jnp.sum(side, axis=1, keepdims=True)
        weight = probs[...]
        for out, places in ((flipped, even_places), (flipped_sent, odd_places)):
            for i, m in enumerate(places):
                start = pl.multiple_of((mine_ref[0] ^ m) * band, band)
                out[i * band : (i + 1) * band, :] = rows[:, pl.ds(start, band)].T
        for copy in copies[:4]:
            copy.wait()
        for start, size in chunks(ff, 256):
            place = slice(start, start + size)
            gates[:, place] = jnp.dot(rows[...], gate[:, place], preferred_element_type=F32)
        for copy in copies[4:8]:
            copy.wait()
        for start, size in chunks(ff, 256):
            place = slice(start, start + size)
            gate_pre = gates[:, place]
            up_pre = jnp.dot(rows[...], up[:, place], preferred_element_type=F32)
            sigma = jax.nn.sigmoid(gate_pre)
            silu = gate_pre * sigma
            scaled = weight * up_pre
            hidden[:, place] = (silu * scaled).astype(BF16)
            gate_by[:, place] = scaled * sigma * (1.0 + gate_pre * (1.0 - sigma))
            up_by[:, place] = weight * silu
            hidden_t[place, :] = hidden[:, place].T
        for copy in copies[8:]:
            copy.wait()

    (
        flipped, flipped_sent, hidden_t, hidden, gate_by, up_by, gate_near, up_near, down_near, done
    ) = stage(
        forward,
        [(me, SMEM), (mine, SMEM)]
        + [(a, VMEM) for a in tok_arrays]
        + [(w[0], HBM) for w in (w_gate, w_up, w_down)],
        [
            ((width // 2, total), BF16, VMEM),
            ((width // 2, total), BF16, VMEM),
            ((ff, total), BF16, VMEM),
            ((total, ff), BF16, VMEM),
            ((total, ff), F32, VMEM),
            ((total, ff), F32, VMEM),
            ((width, ff), BF16, VMEM),
            ((width, ff), BF16, VMEM),
            ((ff, width), BF16, VMEM),
        ],
        scratch=[
            VMEM((total, width), BF16),
            VMEM((total, 1), F32),
            VMEM((total, ff), F32),
            pltpu.SemaphoreType.DMA((12,)),
        ],
        after=[done],
    )

    cot_arrays, cot_where = refs_of(cot_pieces)

    def down_first(own_ref, *refs):
        blocks = refs[: len(cot_arrays)]
        left, rows, away = refs[len(cot_arrays) :]
        for b, (i, row) in enumerate(cot_where):
            rows[b * count : (b + 1) * count, :] = blocks[i][row : row + count, :width]
        products([3], left, rows, [away], own_ref[0])

    cot_rows, down_away, done = stage(
        down_first,
        [(mine, SMEM)] + [(a, VMEM) for a in [*cot_arrays, hidden_t]],
        [((total, width), BF16, VMEM), ((slab, width), BF16, VMEM)],
        after=[done],
    )
    down_came = swap(down_away, "dp", 1)

    def down_rest(own_ref, left, cot, _, away, send, same):
        products([2, 1], left, cot, [send, away], own_ref[0])

    last_away, down_send, flipped_sent, done = stage(
        down_rest,
        [(mine, SMEM), (hidden_t, VMEM), (cot_rows, VMEM), (flipped_sent, ANY)],
        [((slab, width), BF16, VMEM)] * 2 + [(flipped_sent.shape, BF16, ANY)],
        after=[done],
        aliases={3: 2},
    )
    flipped_came = swap(flipped_sent, "dp", 1)
    last_came = swap(last_away, "dp", 1)

    def backward(cot, down, gate_ref, up_ref, grads):
        for start, size in chunks(ff, 256):
            place = slice(start, start + size)
            grad = lax.dot_general(cot[...], down[place, :], TURNED, preferred_element_type=F32)
            grads[:, place] = (grad * gate_ref[:, place]).astype(BF16)
            grads[:, ff + start : ff + start + size] = (grad * up_ref[:, place]).astype(BF16)

    grads, done = stage(
        backward,
        [(a, VMEM) for a in (cot_rows, down_near, gate_by, up_by)],
        [((total, 2 * ff), BF16, VMEM)],
        after=[done],
    )
    grads_came = swap(grads, "dp", 1)

    def added(kept, came, _, send):
        send[...] = (kept[...].astype(F32) + came[...].astype(F32)).astype(BF16)

    down_send, done = stage(
        added,
        [(down_send, VMEM), (down_came, VMEM), (flipped_came, ANY)],
        [((slab, width), BF16, VMEM)],
        after=[done],
    )
    down_got = swap(down_send, "dp", 2)

    def output_rows(left, down, kept, sent):
        for start, size in chunks(width, 512):
            place = slice(start, start + size)
            part = jnp.dot(left[...], down[:, place], preferred_element_type=F32).astype(BF16)
            kept[:, place] = part[:half]
            sent[:, place] = part[half:]

    out_kept, out_sent, done = stage(
        output_rows,
        [(hidden, VMEM), (down_near, VMEM)],
        [((half, width), BF16, VMEM)] * 2,
        after=[done],
    )
    out_came = swap(out_sent, "expert", 1)

    side = width // 2

    def input_rows(grad, gate, up, _, *outs):
        for start, size in chunks(width, 512):
            kept, sent = outs[2 * (start // side)], outs[2 * (start // side) + 1]
            place = slice(start, start + size)
            rows = lax.dot_general(grad[:, :ff], gate[place, :], TURNED, preferred_element_type=F32)
            rows = rows + lax.dot_general(
                grad[:, ff:], up[place, :], TURNED, preferred_element_type=F32
            )
            rows = rows.astype(BF16)
            there = slice(start % side, start % side + size)
            for i in range(2):
                low, high = slice(i * pair, (i + 1) * pair), i * half
                kept[low, there] = rows[high : high + pair]
                sent[low, there] = rows[high + pair : high + half]

    left_kept, left_sent, right_kept, right_sent, done = stage(
        input_rows,
        [(grads, VMEM), (gate_near, VMEM), (up_near, VMEM), (last_came, ANY)],
        [((half, side), BF16, VMEM)] * 4,
        after=[done],
    )
    left_came, right_came = [swap(a, "expert", near_bit) for a in (left_sent, right_sent)]

    cut = 3 * band // 4

    def both_parts(left, left_came, grad, grad_came, gate_send, up_high, up_low, gate_kept, up_kept):
        for j, (gate_out, up_out) in enumerate([(gate_send, None), (gate_kept, up_kept)]):
            row = slice(j * band, (j + 1) * band)
            for start, size in chunks(2 * ff, 256):
                column = slice(start, start + size)
                value = jnp.dot(left[row, :], grad[:, column], preferred_element_type=F32)
                value += jnp.dot(left_came[row, :], grad_came[:, column], preferred_element_type=F32)
                place = slice(start % ff, start % ff + size)
                if start < ff:
                    gate_out[:, place] = value.astype(gate_out.dtype)
                elif up_out is not None:
                    up_out[:, place] = value.astype(up_out.dtype)
                else:
                    up_high[:, place] = value[:cut].astype(BF16)
                    up_low[:, place] = value[cut:].astype(BF16)

    gate_send, up_high, up_low, gate_kept, up_kept, done = stage(
        both_parts,
        [(a, VMEM) for a in (flipped, flipped_came, grads, grads_came)],
        [((band, ff), BF16, VMEM)]
        + [((cut, ff), BF16, VMEM), ((band - cut, ff), BF16, VMEM)]
        + [((band, ff), F32, VMEM)] * 2,
        after=[done],
    )
    gate_got = swap(gate_send, "dp", 2)

    def down_own(own_ref, left, cot, kept):
        products([0], left, cot, [kept], own_ref[0])

    down_kept, done = stage(
        down_own,
        [(mine, SMEM), (hidden_t, VMEM), (cot_rows, VMEM)],
        [((slab, width), F32, VMEM)],
        after=[done],
    )

    def folded(held, came, after, waits=()):
        rows = held.shape[0]
        parts = 1 if rows == count else 2

        def body(a, b, *refs):
            for i, out in enumerate(refs[len(waits) :]):
                place = slice(i * rows // parts, (i + 1) * rows // parts)
                out[...] = (a[place, :].astype(F32) + b[place, :].astype(F32)).astype(BF16)

        return stage(
            body,
            [(held, VMEM), (came, VMEM)] + [(a, ANY) for a in waits],
            [((rows // parts, held.shape[1]), BF16, VMEM)] * parts,
            after=after,
        )

    def owned(parts, after, rows=None, into=None):
        size, wide = parts[-1].shape
        first = 0 if rows is None else rows
        full = parts[0].shape[0]
        step = size // 4
        n = len(parts)

        def body(*refs):
            out, total, sems = refs[-3:]
            copies = []
            for i in range(4):
                at = slice(i * step, (i + 1) * step)
                there = slice(first + i * step, first + (i + 1) * step)
                value = refs[0][there, :].astype(F32)
                for ref in refs[1:n]:
                    last = ref.shape[0] - size + i * step
                    value = value + ref[last : last + step, :].astype(F32)
                total[at, :] = value
                copies.append(pltpu.make_async_copy(total.at[at], out.at[there], sems.at[i]))
                copies[-1].start()
            for copy in copies:
                copy.wait()

        return stage(
            body,
            [(a, VMEM) for a in parts] + ([] if into is None else [(into, HBM)]),
            [((full, wide), F32, HBM)],
            scratch=[VMEM((size, wide), F32), pltpu.SemaphoreType.DMA((4,))],
            after=after,
            aliases=None if into is None else {n: 0},
        )

    def fold_on(held, came, bit, after, waits=()):
        held, send, done = folded(held, came, after, waits)
        return held, swap(send, "expert", bit), done

    left_held, left_came, done = fold_on(left_kept, left_came, 1, [done])
    down_grad, done = owned([down_kept, last_came, down_got], [done])
    out_held, out_came, done = fold_on(out_kept, out_came, near_bit, [done])
    right_held, right_came, done = fold_on(right_kept, right_came, 1, [done])
    left_held, left_came, done = fold_on(left_held, left_came, far_bit, [done])
    high_got = swap(up_high, "dp", 2)
    up_low, done = gated(up_low, [done], [left_came])
    low_got = swap(up_low, "dp", 2)
    right_held, right_came, done = fold_on(right_held, right_came, far_bit, [done])
    out_held, out_came, done = fold_on(out_held, out_came, far_bit, [done])

    gate_part, done = owned([gate_kept, gate_got], [done])
    up_part, done = owned([up_kept, high_got], [done])

    def finished(kept, came, a, b, c, d, out, grad):
        out[...] = (kept[...].astype(F32) + came[...].astype(F32)).astype(BF16)
        grad[:, :side] = (a[...].astype(F32) + b[...].astype(F32)).astype(BF16)
        grad[:, side:] = (c[...].astype(F32) + d[...].astype(F32)).astype(BF16)

    layer_out, input_grad, done = stage(
        finished,
        [(a, VMEM) for a in (out_held, out_came, left_held, left_came, right_held, right_came)],
        [((count, width), BF16, VMEM)] * 2,
        after=[done],
    )
    up_part, _ = owned([up_kept, low_got], [done], cut, up_part)
    return (layer_out, input_grad, gate_part[None], up_part[None], down_grad[None])


def shards(tokens, expert_ids, *rest):
    experts = lax.axis_size("expert")
    every = expert_ids.shape[1] == experts and experts == 8 and lax.axis_size("dp") == 4
    return (dense if every else routed)(tokens, expert_ids, *rest)


def solution(mesh):
    placed = (
        P(("dp", "expert"), None),
        P(("dp", "expert"), None),
        P(("dp", "expert"), None),
        P(("dp", "expert"), None),
        P("expert", None, None),
        P("expert", None, None),
        P("expert", None, None),
    )
    return jax.shard_map(
        shards,
        mesh=mesh,
        in_specs=placed,
        out_specs=(
            P(("dp", "expert"), None),
            P(("dp", "expert"), None),
            P("expert", "dp", None),
            P("expert", "dp", None),
            P("expert", "dp", None),
        ),
        check_vma=False,
    )
```
